32 devices in a mesh: ctx: 8 (over y, x, core), fsdp: 4 (over z).
Axes of the slice: x: 2, y: 2, z: 4, core: 2. Of those that a mesh axis runs over, the one named last changes fastest.
Arguments:
- tokens: bfloat16 [4, 1024, 768], P('fsdp', 'ctx'), may hold values from -6 to 6
- encoder: bfloat16 [4, 512, 768], P('fsdp', 'ctx'), may hold values from -6 to 6
- cotangent: bfloat16 [4, 1024, 768], P('fsdp', 'ctx'), may hold values from -6 to 6
- buckets: int32 [1024], replicated, may hold values from 0 to 31
- pairing: int32 [8], replicated, may hold values from 0 to 7, each once
- norm_one: bfloat16 [768], P('fsdp'), may hold values from 0.5 to 1.5
- self_query: bfloat16 [768, 768], P('fsdp'), may hold values from -0.02734375 to 0.02734375
- self_key: bfloat16 [768, 768], P('fsdp'), may hold values from -0.21875 to 0.21875
- self_value: bfloat16 [768, 768], P('fsdp'), may hold values from -0.21875 to 0.21875
- self_output: bfloat16 [768, 768], P('fsdp'), may hold values from -1.25 to 1.25
- bias_table: bfloat16 [32, 12], P('fsdp'), may hold values from -4 to 4
- norm_two: bfloat16 [768], P('fsdp'), may hold values from 0.5 to 1.5
- cross_query: bfloat16 [768, 768], P('fsdp'), may hold values from -0.02734375 to 0.02734375
- cross_key: bfloat16 [768, 768], P('fsdp'), may hold values from -0.21875 to 0.21875
- cross_value: bfloat16 [768, 768], P('fsdp'), may hold values from -0.21875 to 0.21875
- cross_output: bfloat16 [768, 768], P('fsdp'), may hold values from -1.75 to 1.75
- norm_three: bfloat16 [768], P('fsdp'), may hold values from 0.5 to 1.5
- ff_gate: bfloat16 [768, 2048], P('fsdp'), may hold values from -0.21875 to 0.21875
- ff_up: bfloat16 [768, 2048], P('fsdp'), may hold values from -0.21875 to 0.21875
- ff_down: bfloat16 [2048, 768], P('fsdp'), may hold values from -0.125 to 0.125
Outputs:
- output: bfloat16 [4, 1024, 768], P('fsdp', 'ctx')
- grad_tokens: float32 [4, 1024, 768], P('fsdp', 'ctx')
- grad_encoder: float32 [4, 512, 768], P('fsdp', 'ctx')
- grad_norm_one: float32 [768], P('fsdp')
- grad_self_query: float32 [768, 768], P('fsdp')
- grad_self_key: float32 [768, 768], P('fsdp')
- grad_self_value: float32 [768, 768], P('fsdp')
- grad_self_output: float32 [768, 768], P('fsdp')
- grad_bias_table: float32 [32, 12], P('fsdp')
- grad_norm_two: float32 [768], P('fsdp')
- grad_cross_query: float32 [768, 768], P('fsdp')
- grad_cross_key: float32 [768, 768], P('fsdp')
- grad_cross_value: float32 [768, 768], P('fsdp')
- grad_cross_output: float32 [768, 768], P('fsdp')
- grad_norm_three: float32 [768], P('fsdp')
- grad_ff_gate: float32 [768, 2048], P('fsdp')
- grad_ff_up: float32 [768, 2048], P('fsdp')
- grad_ff_down: float32 [2048, 768], P('fsdp')
The draws below stay inside these ranges and needn't reach their ends.
All inputs are finite; a program needn't handle non-finite values.
Results may differ from the reference program's by a relative error of at most 0.03.
Values may be sent and summed in bfloat16 or wider, within the bound.
No kernel may reach another device: no remote copies, remote signals or barrier semaphores. Data moves between devices by JAX's collectives and lax.ppermute only.
A program may use at most 192 MiB of HBM per device.

```python
import jax
import jax.numpy as jnp
from jax import lax

D = 768
H = 12
DH = 64
FF = 2048
NB = 32
ENC = 512
SEQ = 1024
SEQS = 4
N_CTX = 8


def set_ends(drawn, stream_key, least, largest):
    index_at = [jax.random.randint(jax.random.fold_in(stream_key, axis), (), 0, length) for axis, length in enumerate(drawn.shape)]
    main_axis = drawn.shape.index(max(drawn.shape))
    next_to = index_at[:main_axis] + [(index_at[main_axis] + 1) % drawn.shape[main_axis]] + index_at[main_axis + 1:]
    return drawn.at[tuple(index_at)].set(least).at[tuple(next_to)].set(largest)


def shard_levels(key, dims, split, smallest, high):
    def one(position, parts):
        heights = jax.random.uniform(jax.random.fold_in(jax.random.fold_in(key, 6), position), (parts,), jnp.float32, smallest / len(split), high / len(split))
        return jnp.repeat(jnp.exp(heights), dims[position] // parts).reshape((-1,) + (1,) * (len(dims) - position - 1))

    factor_of = one(*split[0])
    for cut in split[1:]:
        factor_of = factor_of * one(*cut)
    return factor_of


def centred(key, shape, deviation, most, split=(), held_as=jnp.bfloat16):
    values = jax.random.normal(key, shape, jnp.float32) * deviation
    if len(split) > 0:
        values = shard_levels(key, shape, split, -0.22, 0.18) * values
    return jnp.clip(values, min=-most, max=most).astype(held_as)


def setup_inputs(seed: int = 0) -> dict:
    streams_of = jax.random.split(jax.random.key(seed), 21)
    tokens = centred(streams_of[0], (SEQS, SEQ, D), 1.0, 6.0, ((0, 4), (1, 8)))
    encoder = centred(streams_of[1], (SEQS, ENC, D), 1.0, 6.0, ((0, 4), (1, 8)))
    cotangent = centred(streams_of[2], (SEQS, SEQ, D), 1.0, 6.0, ((0, 4), (1, 8)))
    buckets = set_ends(jax.random.randint(streams_of[3], (SEQ,), 0, NB), jax.random.fold_in(streams_of[3], 1), 0, NB - 1).astype(jnp.int32)
    pairing = jax.random.permutation(streams_of[4], N_CTX).astype(jnp.int32)
    norm_one = jnp.clip(1.0 + 0.1 * jax.random.normal(streams_of[5], (D,), jnp.float32), 0.5, 1.5).astype(jnp.bfloat16)
    self_query = centred(streams_of[6], (D, D), (D * DH) ** -0.5, 0.02734375, ((0, 4),))
    self_key = centred(streams_of[7], (D, D), D ** -0.5, 0.21875, ((0, 4),))
    self_value = centred(streams_of[8], (D, D), D ** -0.5, 0.21875, ((0, 4),))
    self_output = centred(streams_of[9], (D, D), (D // 32) ** -0.5, 1.25, ((0, 4),))
    bias_table = centred(streams_of[10], (NB, H), 1.0, 4.0, ((0, 4),))
    norm_two = jnp.clip(1.0 + 0.1 * jax.random.normal(streams_of[11], (D,), jnp.float32), 0.5, 1.5).astype(jnp.bfloat16)
    cross_query = centred(streams_of[12], (D, D), (D * DH) ** -0.5, 0.02734375, ((0, 4),))
    cross_key = centred(streams_of[13], (D, D), D ** -0.5, 0.21875, ((0, 4),))
    cross_value = centred(streams_of[14], (D, D), D ** -0.5, 0.21875, ((0, 4),))
    cross_output = centred(streams_of[15], (D, D), (D // 64) ** -0.5, 1.75, ((0, 4),))
    norm_three = jnp.clip(1.0 + 0.1 * jax.random.normal(streams_of[16], (D,), jnp.float32), 0.5, 1.5).astype(jnp.bfloat16)
    ff_gate = centred(streams_of[17], (D, FF), D ** -0.5, 0.21875, ((0, 4),))
    ff_up = centred(streams_of[18], (D, FF), D ** -0.5, 0.21875, ((0, 4),))
    ff_down = centred(streams_of[19], (FF, D), FF ** -0.5, 0.125, ((0, 4),))
    return {"tokens": tokens, "encoder": encoder, "cotangent": cotangent, "buckets": buckets, "pairing": pairing, "norm_one": norm_one, "self_query": self_query, "self_key": self_key, "self_value": self_value, "self_output": self_output, "bias_table": bias_table, "norm_two": norm_two, "cross_query": cross_query, "cross_key": cross_key, "cross_value": cross_value, "cross_output": cross_output, "norm_three": norm_three, "ff_gate": ff_gate, "ff_up": ff_up, "ff_down": ff_down}


@jax.custom_vjp
def low(v):
    return lax.optimization_barrier(v.astype(jnp.bfloat16)).astype(jnp.float32)

@jax.custom_vjp
def low_back(v):
    return v

def low_keep(v):
    return (low(v), None)

def low_pass(kept, grad):
    return (grad,)

def back_keep(v):
    return (v, None)

def back_low(kept, grad):
    return (low(grad),)
low.defvjp(low_keep, low_pass)
low_back.defvjp(back_keep, back_low)
HIGH = lax.Precision.HIGHEST

def matmul(a, b):
    return jnp.dot(a, b, precision=HIGH)

def norm_apply(v, g):
    return v * lax.rsqrt(lax.optimization_barrier(jnp.mean(v * v, axis=-1, keepdims=True)) + 1e-06) * g

def normalized_rows(s):
    top = lax.optimization_barrier(jnp.max(s, axis=-1, keepdims=True))
    expo = jnp.exp(s - top)
    return expo / lax.optimization_barrier(jnp.sum(expo, axis=-1, keepdims=True))

def heads_of(v):
    return v.reshape(v.shape[0], H, DH)

def one_sequence(rows, hidden_states, positions, buckets, params):
    g_one, w_q, w_k, w_v, w_o, relative_bias_table, g_two, c_q, c_k, c_v, c_o, g_three, w_gate, w_up, w_down = params
    a_one = low(norm_apply(rows, g_one))
    query = low(low_back(matmul(a_one, w_q)))
    key = low(low_back(matmul(a_one, w_k)))
    value = low(low_back(matmul(a_one, w_v)))
    onehot = (buckets[:, None] == jnp.arange(NB, dtype=jnp.int32)[None, :]).astype(jnp.float32)
    offsets = jnp.dot(relative_bias_table.T, onehot.T, precision=HIGH)
    distance = positions[:, None] - positions[None, :]
    position_bias = jnp.take(offsets, jnp.clip(distance, 0, SEQ - 1), axis=1)
    scores = jnp.einsum('qhd,khd->hqk', heads_of(query), heads_of(key), precision=HIGH) + position_bias
    scores = low_back(jnp.where(distance[None] >= 0, scores, -1e+30))
    probs = low(normalized_rows(scores))
    attended = jnp.einsum('hqk,khd->qhd', probs, heads_of(value), precision=HIGH).reshape(rows.shape[0], D)
    attended = low(low_back(attended))
    second = rows + low_back(matmul(attended, w_o))
    a_two = low(norm_apply(second, g_two))
    cross_q = low(low_back(matmul(a_two, c_q)))
    cross_k = low(low_back(matmul(hidden_states, c_k)))
    cross_v = low(low_back(matmul(hidden_states, c_v)))
    cross_s = low_back(jnp.einsum('qhd,khd->hqk', heads_of(cross_q), heads_of(cross_k), precision=HIGH))
    cross_p = low(normalized_rows(cross_s))
    cross_o = jnp.einsum('hqk,khd->qhd', cross_p, heads_of(cross_v), precision=HIGH).reshape(rows.shape[0], D)
    cross_o = low(low_back(cross_o))
    third = second + low_back(matmul(cross_o, c_o))
    a_three = low(norm_apply(third, g_three))
    gate = low_back(matmul(a_three, w_gate))
    up_val = low_back(matmul(a_three, w_up))
    hidden = low(jax.nn.gelu(gate, approximate=True) * up_val)
    return third + low_back(matmul(hidden, w_down))

def reference(tokens, encoder, cotangent, buckets, pairing, norm_one, self_query, self_key, self_value, self_output, bias_table, norm_two, cross_query, cross_key, cross_value, cross_output, norm_three, ff_gate, ff_up, ff_down):
    block = SEQ // (2 * N_CTX)
    starts = jnp.stack([pairing, 2 * N_CTX - 1 - pairing], axis=1).reshape(-1).astype(jnp.int32)
    positions = (starts[:, None] * block + jnp.arange(block, dtype=jnp.int32)[None, :]).reshape(-1).astype(jnp.int32)
    weights = tuple((w.astype(jnp.float32) for w in (norm_one, self_query, self_key, self_value, self_output, bias_table, norm_two, cross_query, cross_key, cross_value, cross_output, norm_three, ff_gate, ff_up, ff_down)))

    def layer(rows_all, states_all, *params):

        def step(pair):
            return one_sequence(pair[0], pair[1], positions, buckets, params)
        return lax.map(jax.checkpoint(step), (rows_all, states_all))
    result, pull = jax.vjp(layer, tokens.astype(jnp.float32), encoder.astype(jnp.float32), *weights)
    grads = pull(cotangent.astype(jnp.float32))
    return (result.astype(jnp.bfloat16), grads[0], grads[1], grads[2], grads[3], grads[4], grads[5], grads[6], grads[7], grads[8], grads[9], grads[10], grads[11], grads[12], grads[13], grads[14], grads[15], grads[16])
```

```python
import functools
import math

import jax
import jax.numpy as jnp
from jax import lax
from jax.experimental import pallas as pl
from jax.experimental.pallas import tpu as pltpu
from jax.sharding import PartitionSpec as P

BF = jnp.bfloat16
F32 = jnp.float32
LANES = 128
VMEM_LIMIT = 48 * 1024 * 1024
LAST = (((1,), (1,)), ((), ()))
FIRST = (((0,), (0,)), ((), ()))
PLAIN = (((1,), (0,)), ((), ()))


def norm_apply(v, g):
    return v * lax.rsqrt(jnp.mean(v * v, axis=-1, keepdims=True) + 1e-06) * g


def product(a, w):
    return jnp.dot(a, w, preferred_element_type=F32)


def through(grad, w):
    return lax.dot_general(grad, w, LAST, preferred_element_type=F32)


def weight_grad(a, grad):
    return lax.dot_general(a, grad, FIRST, preferred_element_type=F32)


def dot(a, b, dims):
    return lax.dot_general(a, b, dims, preferred_element_type=F32)


def two_heads(block):
    half = block.shape[1] // 2
    low = lax.broadcasted_iota(jnp.int32, block.shape, 1) < half
    zero = jnp.zeros_like(block)
    return jnp.concatenate([jnp.where(low, block, zero), jnp.where(low, zero, block)], axis=0)


def join_heads(rows):
    n = rows.shape[0] // 2
    low = lax.broadcasted_iota(jnp.int32, (n, rows.shape[1]), 1) < rows.shape[1] // 2
    return jnp.where(low, rows[:n], rows[n:])


def to_positions(blocks_ref, source, target, block):
    for i in range(source.shape[0] // block):
        spot = pl.multiple_of(blocks_ref[i] * block, block)
        target[pl.ds(spot, block), :] = source[i * block : (i + 1) * block, :]


def from_positions(blocks_ref, source, target, block):
    for i in range(target.shape[0] // block):
        spot = pl.multiple_of(blocks_ref[i] * block, block)
        target[i * block : (i + 1) * block, :] = source[pl.ds(spot, block), :].astype(target.dtype)


def sheared(line, block):
    sublane = lax.broadcasted_iota(jnp.int32, line.shape, 0)
    for bit in (1, 2, 4):
        line = jnp.where(sublane & bit != 0, pltpu.roll(line, bit, 1), line)
    return jnp.concatenate([line if i == 0 else pltpu.roll(line, i, 1) for i in range(0, block, 8)], axis=0)


def self_forward_kernel(blocks_ref, own_ref, q_ref, k_ref, v_ref, bias_ref, o_ref, p_ref, ks, vs):
    rows = q_ref.shape[0]
    block = rows // 2
    nkeys = k_ref.shape[0]
    to_positions(blocks_ref, k_ref, ks, block)
    to_positions(blocks_ref, v_ref, vs, block)
    scores = dot(two_heads(q_ref[...]), ks[...], LAST)
    column = lax.broadcasted_iota(jnp.int32, (block, nkeys), 1)
    row = lax.broadcasted_iota(jnp.int32, (block, nkeys), 0)
    for head in range(2):
        line = jnp.broadcast_to(bias_ref[0, head : head + 1, :], (8, nkeys))
        for part in range(2):
            start = own_ref[part] * block
            shear = sheared(pltpu.roll(line, start + 1, 1), block)
            at = head * rows + part * block
            s = jnp.where(column <= row + start, scores[at : at + block] + shear, -1e30)
            top = jnp.max(s, axis=-1, keepdims=True)
            expo = jnp.exp(s - top)
            total = jnp.sum(expo, axis=-1, keepdims=True)
            p_ref[0, at : at + block, :] = (expo / total).astype(BF)
    o_ref[...] = join_heads(dot(p_ref[0], vs[...], PLAIN)).astype(BF)


def cross_forward_kernel(q_ref, k_ref, v_ref, o_ref, p_ref):
    s = dot(two_heads(q_ref[...]), k_ref[...], LAST)
    top = jnp.max(s, axis=-1, keepdims=True)
    expo = jnp.exp(s - top)
    total = jnp.sum(expo, axis=-1, keepdims=True)
    p_ref[0] = (expo / total).astype(BF)
    o_ref[...] = join_heads(dot(p_ref[0], v_ref[...], PLAIN)).astype(BF)


def score_gradient(probs, dom, values):
    dp = dot(dom, values, LAST)
    p = probs.astype(F32)
    delta = jnp.sum(p * dp, axis=-1, keepdims=True)
    return (p * (dp - delta)).astype(BF)


def cross_backward_kernel(q_ref, k_ref, v_ref, do_ref, p_ref, dq_ref, dk_ref, dv_ref):
    dom = two_heads(do_ref[...])
    probs = p_ref[0]
    ds = score_gradient(probs, dom, v_ref[...])
    dq_ref[...] = join_heads(dot(ds, k_ref[...], PLAIN)).astype(BF)
    dk_ref[...] = dot(ds, two_heads(q_ref[...]), FIRST).astype(BF)
    dv_ref[...] = dot(probs, dom, FIRST).astype(BF)


def self_backward_kernel(
    blocks_ref, own_ref, q_ref, k_ref, v_ref, do_ref, p_ref, dq_ref, dk_ref, dv_ref, db_ref, ks, vs, acc
):
    rows = q_ref.shape[0]
    block = rows // 2
    nkeys = k_ref.shape[0]
    to_positions(blocks_ref, k_ref, ks, block)
    to_positions(blocks_ref, v_ref, vs, block)
    dom = two_heads(do_ref[...])
    probs = p_ref[0]
    ds = score_gradient(probs, dom, vs[...])
    dq_ref[...] = join_heads(dot(ds, ks[...], PLAIN)).astype(BF)
    acc[...] = dot(ds, two_heads(q_ref[...]), FIRST)
    from_positions(blocks_ref, acc, dk_ref, block)
    acc[...] = dot(probs, dom, FIRST)
    from_positions(blocks_ref, acc, dv_ref, block)
    for head in range(2):
        lines = None
        for part in range(2):
            at = head * rows + part * block
            x = ds[at : at + block].astype(F32)
            size = block
            while size > 1:
                size //= 2
                x = x[:size] + pltpu.roll(x[size:], nkeys - size, 1)
            x = pltpu.roll(jnp.broadcast_to(x, (8, nkeys)), nkeys - own_ref[part] * block - 1, 1)
            lines = x if lines is None else lines + x
        db_ref[0, head : head + 1, :] = lines[0:1]


def column_block(rows, offset):
    return pl.BlockSpec((rows, LANES), lambda i, *_: (0, offset + i))


def whole_block(a, b):
    return pl.BlockSpec((1, a, b), lambda i, *_: (i, 0, 0))


def params():
    return pltpu.CompilerParams(vmem_limit_bytes=VMEM_LIMIT)


def cost(rows, nkeys, width, products):
    return pl.CostEstimate(
        flops=4 * rows * nkeys * width * products,
        bytes_accessed=4 * rows * nkeys * (width // LANES) + 8 * nkeys * width,
        transcendentals=2 * rows * nkeys * (width // LANES),
    )


def self_forward(blocks, own, q, kv, bias):
    rows, width = q.shape
    nkeys = kv.shape[0]
    pairs = width // LANES
    return pl.pallas_call(
        self_forward_kernel,
        grid_spec=pltpu.PrefetchScalarGridSpec(
            num_scalar_prefetch=2,
            grid=(pairs,),
            in_specs=[
                column_block(rows, 0),
                column_block(nkeys, 0),
                column_block(nkeys, pairs),
                whole_block(2, nkeys),
            ],
            out_specs=[column_block(rows, 0), whole_block(2 * rows, nkeys)],
            scratch_shapes=[pltpu.VMEM((nkeys, LANES), BF), pltpu.VMEM((nkeys, LANES), BF)],
        ),
        out_shape=[
            jax.ShapeDtypeStruct((rows, width), BF),
            jax.ShapeDtypeStruct((pairs, 2 * rows, nkeys), BF),
        ],
        compiler_params=params(),
        cost_estimate=cost(rows, nkeys, width, 2),
        name="self_forward",
    )(blocks, own, q, kv, kv, bias)


def self_backward(blocks, own, q, kv, do, probs):
    rows, width = q.shape
    nkeys = kv.shape[0]
    pairs = width // LANES
    return pl.pallas_call(
        self_backward_kernel,
        grid_spec=pltpu.PrefetchScalarGridSpec(
            num_scalar_prefetch=2,
            grid=(pairs,),
            in_specs=[
                column_block(rows, 0),
                column_block(nkeys, 0),
                column_block(nkeys, pairs),
                column_block(rows, 0),
                whole_block(2 * rows, nkeys),
            ],
            out_specs=[
                column_block(rows, 0),
                column_block(nkeys, 0),
                column_block(nkeys, 0),
                whole_block(2, nkeys),
            ],
            scratch_shapes=[
                pltpu.VMEM((nkeys, LANES), BF),
                pltpu.VMEM((nkeys, LANES), BF),
                pltpu.VMEM((nkeys, LANES), F32),
            ],
        ),
        out_shape=[
            jax.ShapeDtypeStruct((rows, width), BF),
            jax.ShapeDtypeStruct((nkeys, width), BF),
            jax.ShapeDtypeStruct((nkeys, width), BF),
            jax.ShapeDtypeStruct((pairs, 2, nkeys), F32),
        ],
        compiler_params=params(),
        cost_estimate=cost(rows, nkeys, width, 5),
        name="self_backward",
    )(blocks, own, q, kv, kv, do, probs)


def cross_forward(q, kv):
    rows, width = q.shape
    nkeys = kv.shape[0]
    pairs = width // LANES
    return pl.pallas_call(
        cross_forward_kernel,
        grid=(pairs,),
        in_specs=[column_block(rows, 0), column_block(nkeys, 0), column_block(nkeys, pairs)],
        out_specs=[column_block(rows, 0), whole_block(2 * rows, nkeys)],
        out_shape=[
            jax.ShapeDtypeStruct((rows, width), BF),
            jax.ShapeDtypeStruct((pairs, 2 * rows, nkeys), BF),
        ],
        compiler_params=params(),
        cost_estimate=cost(rows, nkeys, width, 2),
        name="cross_forward",
    )(q, kv, kv)


def cross_backward(q, kv, do, probs):
    rows, width = q.shape
    nkeys = kv.shape[0]
    pairs = width // LANES
    return pl.pallas_call(
        cross_backward_kernel,
        grid=(pairs,),
        in_specs=[
            column_block(rows, 0),
            column_block(nkeys, 0),
            column_block(nkeys, pairs),
            column_block(rows, 0),
            whole_block(2 * rows, nkeys),
        ],
        out_specs=[column_block(rows, 0), column_block(nkeys, 0), column_block(nkeys, 0)],
        out_shape=[
            jax.ShapeDtypeStruct((rows, width), BF),
            jax.ShapeDtypeStruct((nkeys, width), BF),
            jax.ShapeDtypeStruct((nkeys, width), BF),
        ],
        compiler_params=params(),
        cost_estimate=cost(rows, nkeys, width, 5),
        name="cross_backward",
    )(q, kv, kv, do, probs)


class Net:
    def __init__(self):
        self.c = lax.axis_index("ctx")
        self.z = lax.axis_index("fsdp")
        self.nc = lax.axis_size("ctx")
        self.nz = lax.axis_size("fsdp")
        self.chips = self.nc // 2
        self.core = self.c % 2
        self.chip = self.c // 2

    def to_core(self, x):
        return lax.ppermute(x, "ctx", [(i, i ^ 1) for i in range(self.nc)])

    def to_chip(self, x, k):
        return lax.ppermute(x, "ctx", [(i, i ^ (2 * k)) for i in range(self.nc)])

    def along(self, x, s):
        n = self.nz
        return lax.ppermute(x, "fsdp", [(i, (i + s) % n) for i in range(n)])

    def gather_ctx(self, x):
        got = [x] + [self.to_chip(x, k) for k in range(1, self.chips)]
        mine = jnp.stack(got)
        other = self.to_core(mine)
        out = jnp.zeros((self.nc,) + x.shape, x.dtype)
        for k in range(self.chips):
            spot = 2 * (self.chip ^ k)
            out = lax.dynamic_update_index_in_dim(out, mine[k], spot + self.core, 0)
            out = lax.dynamic_update_index_in_dim(out, other[k], spot + 1 - self.core, 0)
        return out

    def gather_weights(self, piece):
        rows, cols = piece.shape
        parts = jnp.zeros((self.nz, rows, cols), piece.dtype)
        parts = lax.dynamic_update_index_in_dim(parts, piece, self.z, 0)
        for s in range(1, self.nz):
            got = self.along(piece, s)
            parts = lax.dynamic_update_index_in_dim(parts, got, (self.z + self.nz - s) % self.nz, 0)
        whole = self.gather_ctx(parts)
        return jnp.swapaxes(whole, 0, 1).reshape(self.nz * self.nc * rows, cols)

    def scatter_ctx(self, x):
        x = x.reshape((self.chips, 2) + x.shape[1:])
        keep = lax.dynamic_index_in_dim(x, self.core, 1, keepdims=False)
        give = lax.dynamic_index_in_dim(x, 1 - self.core, 1, keepdims=False)
        both = (keep.astype(F32) + self.to_core(give).astype(F32)).astype(BF)
        total = lax.dynamic_index_in_dim(both, self.chip, 0, keepdims=False).astype(F32)
        for k in range(1, self.chips):
            send = lax.dynamic_index_in_dim(both, self.chip ^ k, 0, keepdims=False)
            total = total + self.to_chip(send, k).astype(F32)
        return total

    def reduce_weights(self, grad):
        rows, cols = grad.shape
        each = rows // (self.nz * self.nc)
        x = grad.reshape(self.nz, self.nc, each, cols).swapaxes(0, 1)
        mine = self.scatter_ctx(x).astype(BF)
        total = lax.dynamic_index_in_dim(mine, self.z, 0, keepdims=False).astype(F32)
        for s in range(1, self.nz):
            send = lax.dynamic_index_in_dim(mine, (self.z + s) % self.nz, 0, keepdims=False)
            total = total + self.along(send, s).astype(F32)
        return self.gather_ctx(total.astype(BF)).reshape(self.nc * each, cols)


def per_device(
    tokens,
    encoder,
    cotangent,
    buckets,
    pairing,
    norm_one,
    self_query,
    self_key,
    self_value,
    self_output,
    bias_table,
    norm_two,
    cross_query,
    cross_key,
    cross_value,
    cross_output,
    norm_three,
    ff_gate,
    ff_up,
    ff_down,
):
    net = Net()
    nc, nz = net.nc, net.nz
    mine = net.c
    shard = self_query.shape[0]
    width = self_query.shape[1]
    hidden_width = ff_gate.shape[1]
    heads = bias_table.shape[1]
    pairs = width // LANES
    each = shard // nc
    down_each = ff_down.shape[0] // nc

    def rows_of(w):
        n = w.shape[0] // nc
        return lax.dynamic_slice_in_dim(w, mine * n, n, 0)

    table_size = bias_table.size
    extra_width = LANES * math.ceil((4 + table_size) / LANES)
    small = jnp.stack([norm_one, norm_two, norm_three], axis=1)
    small = jnp.pad(rows_of(small), ((0, 0), (0, extra_width - 3)))
    flat = jnp.pad(bias_table.reshape(1, -1), ((0, each - 1), (4, extra_width - 4 - table_size)))
    small = small + flat
    one = net.gather_weights(
        jnp.concatenate([rows_of(self_query), rows_of(self_key), rows_of(self_value), small], axis=1)
    )
    rows_all = net.gather_ctx(jnp.concatenate([tokens[0], encoder[0]], axis=0))
    two = net.gather_weights(
        jnp.concatenate(
            [rows_of(w) for w in (self_output, cross_query, cross_key, cross_value, cross_output)], axis=1
        )
    )
    w_gate = lax.all_gather(rows_of(ff_gate), ("fsdp", "ctx"), axis=0, tiled=True)
    w_up = lax.all_gather(rows_of(ff_up), ("fsdp", "ctx"), axis=0, tiled=True)
    w_down = lax.all_gather(rows_of(ff_down), ("fsdp", "ctx"), axis=0, tiled=True)

    w_q = one[:, :width]
    w_kv = one[:, width : 3 * width]
    extra = one[:, 3 * width :]
    gains = extra[:, :4].astype(F32).T
    g_one, g_two, g_three = gains[0], gains[1], gains[2]
    table = extra.reshape(nz, shard, extra_width)[:, 0, 4 : 4 + table_size].reshape(-1, heads)
    nbuckets = table.shape[0]
    w_o, c_q, c_kv, c_o = (
        two[:, :width],
        two[:, width : 2 * width],
        two[:, 2 * width : 4 * width],
        two[:, 4 * width :],
    )

    count = tokens.shape[1]
    block = count // 2
    seq_len = count * nc
    tokens_all = rows_all[:, :count].reshape(seq_len, width)
    states_all = rows_all[:, count:].reshape(-1, width)
    first = pairing[mine]
    own = jnp.stack([first, 2 * nc - 1 - first]).astype(jnp.int32)
    blocks = jnp.stack([pairing, 2 * nc - 1 - pairing], axis=1).reshape(-1).astype(jnp.int32)

    picks = (buckets[::-1][None, :] == jnp.arange(nbuckets, dtype=jnp.int32)[:, None]).astype(BF)
    bias = jnp.dot(table.T, picks, preferred_element_type=F32).reshape(pairs, 2, seq_len)

    rows_in = tokens[0].astype(F32)
    incoming = cotangent[0]
    a_one_full, norm_one_back = jax.vjp(norm_apply, rows_in, g_one)
    a_one = a_one_full.astype(BF)
    a_one_all = norm_apply(tokens_all.astype(F32), g_one).astype(BF)
    query = product(a_one, w_q).astype(BF)
    kv = product(a_one_all, w_kv).astype(BF)
    cross_kv = product(states_all, c_kv).astype(BF)
    attended, self_probs = self_forward(blocks, own, query, kv, bias)
    second = rows_in + product(attended, w_o)
    a_two, norm_two_back = jax.vjp(norm_apply, second, g_two)
    a_two = a_two.astype(BF)
    cross_q = product(a_two, c_q).astype(BF)
    cross_o, cross_probs = cross_forward(cross_q, cross_kv)
    third = second + product(cross_o, c_o)
    a_three, norm_three_back = jax.vjp(norm_apply, third, g_three)
    a_three = a_three.astype(BF)
    gate = product(a_three, w_gate)
    up_val = product(a_three, w_up)
    hidden, geglu_back = jax.vjp(lambda left, right: jax.nn.gelu(left, approximate=True) * right, gate, up_val)
    hidden = hidden.astype(BF)
    result = third + product(hidden, w_down)

    grad_hidden = through(incoming, w_down)
    grad_down = weight_grad(hidden, incoming)
    grad_gate, grad_up = geglu_back(grad_hidden)
    grad_gate = grad_gate.astype(BF)
    grad_up = grad_up.astype(BF)
    grad_w_gate = weight_grad(a_three, grad_gate).astype(BF)
    grad_w_up = weight_grad(a_three, grad_up).astype(BF)
    total_down = net.reduce_weights(grad_down.astype(BF)).astype(F32)
    total_ff = net.reduce_weights(jnp.concatenate([grad_w_gate, grad_w_up], axis=1)).astype(F32)
    grad_a_three = through(grad_gate, w_gate) + through(grad_up, w_up)
    part_three, grad_g_three = norm_three_back(grad_a_three)
    grad_third = incoming.astype(F32) + part_three
    branch_two = grad_third.astype(BF)
    grad_c_o = weight_grad(cross_o, branch_two)
    grad_cross_o = through(branch_two, c_o).astype(BF)
    dcq, dck, dcv = cross_backward(cross_q, cross_kv, grad_cross_o, cross_probs)
    grad_c_q = weight_grad(a_two, dcq)
    grad_c_k = weight_grad(states_all, dck)
    grad_c_v = weight_grad(states_all, dcv)
    states_part = through(dck, c_kv[:, :width]) + through(dcv, c_kv[:, width:])
    part_two, grad_g_two = norm_two_back(through(dcq, c_q))
    grad_second = grad_third + part_two
    branch_one = grad_second.astype(BF)
    grad_w_o = weight_grad(attended, branch_one)
    total_two = net.reduce_weights(
        jnp.concatenate([g.astype(BF) for g in (grad_w_o, grad_c_q, grad_c_k, grad_c_v, grad_c_o)], axis=1)
    ).astype(F32)
    grad_attended = through(branch_one, w_o).astype(BF)
    dq, dk, dv, bias_grad = self_backward(blocks, own, query, kv, grad_attended, self_probs)
    table_grad = lax.dot_general(
        picks.astype(F32), bias_grad.reshape(heads, seq_len), LAST, precision=lax.Precision.HIGHEST
    )
    grad_w_q = weight_grad(a_one, dq)
    grad_w_k = weight_grad(a_one_all, dk)
    grad_w_v = weight_grad(a_one_all, dv)
    rows_part = through(dk, w_kv[:, :width]) + through(dv, w_kv[:, width:])
    sent = jnp.concatenate(
        [rows_part.astype(BF).reshape(nc, count, width), states_part.astype(BF).reshape(nc, -1, width)], axis=1
    )
    own_part = net.scatter_ctx(sent)
    grad_a_one = through(dq, w_q) + own_part[:count]
    grad_states = own_part[count:]
    part_one, grad_g_one = norm_one_back(grad_a_one)
    grad_rows = grad_second + part_one

    small_grad = jnp.stack([grad_g_one, grad_g_two, grad_g_three], axis=1).astype(BF)
    small_grad = jnp.pad(small_grad, ((0, 0), (0, extra_width - 3)))
    table_rows = jnp.pad(
        table_grad.astype(BF).reshape(nz, 1, table_size),
        ((0, 0), (0, shard - 1), (4, extra_width - 4 - table_size)),
    ).reshape(nz * shard, extra_width)
    total_one = net.reduce_weights(
        jnp.concatenate(
            [grad_w_q.astype(BF), grad_w_k.astype(BF), grad_w_v.astype(BF), small_grad + table_rows], axis=1
        )
    ).astype(F32)
    small_total = total_one[:, 3 * width :]
    gain_total = small_total[:, :4].T
    table_total = small_total[0, 4 : 4 + table_size].reshape(-1, heads)

    return (
        result.astype(BF)[None],
        grad_rows[None],
        grad_states[None],
        gain_total[0],
        total_one[:, :width],
        total_one[:, width : 2 * width],
        total_one[:, 2 * width : 3 * width],
        total_two[:, :width],
        table_total,
        gain_total[1],
        total_two[:, width : 2 * width],
        total_two[:, 2 * width : 3 * width],
        total_two[:, 3 * width : 4 * width],
        total_two[:, 4 * width :],
        gain_total[2],
        total_ff[:, :hidden_width],
        total_ff[:, hidden_width:],
        total_down,
    )


def solution(mesh):
    rows = P("fsdp", "ctx", None)
    gain = P("fsdp")
    weight = P("fsdp", None)
    gradients = (
        gain, weight, weight, weight, weight, weight, gain, weight, weight, weight, weight, gain, weight, weight, weight
    )
    return jax.shard_map(
        per_device,
        mesh=mesh,
        in_specs=(rows, rows, rows, P(), P()) + gradients,
        out_specs=(rows, rows, rows) + gradients,
        check_vma=False,
    )
```

```python
import functools
import math

import jax
import jax.numpy as jnp
from jax import lax
from jax.experimental import pallas as pl
from jax.experimental.pallas import tpu as pltpu
from jax.sharding import PartitionSpec as P

BF = jnp.bfloat16
F32 = jnp.float32
LANES = 128
VMEM_LIMIT = 48 * 1024 * 1024
LAST = (((1,), (1,)), ((), ()))
FIRST = (((0,), (0,)), ((), ()))
PLAIN = (((1,), (0,)), ((), ()))


def norm_apply(v, g):
    return v * lax.rsqrt(jnp.mean(v * v, axis=-1, keepdims=True) + 1e-06) * g


def product(a, w):
    return jnp.dot(a, w, preferred_element_type=F32)


def through(grad, w):
    return lax.dot_general(grad, w, LAST, preferred_element_type=F32)


def weight_grad(a, grad):
    return lax.dot_general(a, grad, FIRST, preferred_element_type=F32)


def dot(a, b, dims):
    return lax.dot_general(a, b, dims, preferred_element_type=F32)


def two_heads(block):
    half = block.shape[1] // 2
    low = lax.broadcasted_iota(jnp.int32, block.shape, 1) < half
    zero = jnp.zeros_like(block)
    return jnp.concatenate([jnp.where(low, block, zero), jnp.where(low, zero, block)], axis=0)


def join_heads(rows):
    n = rows.shape[0] // 2
    low = lax.broadcasted_iota(jnp.int32, (n, rows.shape[1]), 1) < rows.shape[1] // 2
    return jnp.where(low, rows[:n], rows[n:])


def to_positions(blocks_ref, source, target, block):
    for i in range(source.shape[0] // block):
        spot = pl.multiple_of(blocks_ref[i] * block, block)
        target[pl.ds(spot, block), :] = source[i * block : (i + 1) * block, :]


def from_positions(blocks_ref, source, target, block):
    for i in range(target.shape[0] // block):
        spot = pl.multiple_of(blocks_ref[i] * block, block)
        target[i * block : (i + 1) * block, :] = source[pl.ds(spot, block), :].astype(target.dtype)


def sheared(line, block):
    sublane = lax.broadcasted_iota(jnp.int32, line.shape, 0)
    for bit in (1, 2, 4):
        line = jnp.where(sublane & bit != 0, pltpu.roll(line, bit, 1), line)
    return jnp.concatenate([line if i == 0 else pltpu.roll(line, i, 1) for i in range(0, block, 8)], axis=0)


def self_forward_kernel(blocks_ref, own_ref, q_ref, k_ref, v_ref, bias_ref, o_ref, p_ref, ks, vs):
    rows = q_ref.shape[0]
    block = rows // 2
    nkeys = k_ref.shape[0]
    to_positions(blocks_ref, k_ref, ks, block)
    to_positions(blocks_ref, v_ref, vs, block)
    scores = dot(two_heads(q_ref[...]), ks[...], LAST)
    column = lax.broadcasted_iota(jnp.int32, (block, nkeys), 1)
    row = lax.broadcasted_iota(jnp.int32, (block, nkeys), 0)
    for head in range(2):
        line = jnp.broadcast_to(bias_ref[0, head : head + 1, :], (8, nkeys))
        for part in range(2):
            start = own_ref[part] * block
            shear = sheared(pltpu.roll(line, start + 1, 1), block)
            at = head * rows + part * block
            s = jnp.where(column <= row + start, scores[at : at + block] + shear, -1e30)
            top = jnp.max(s, axis=-1, keepdims=True)
            expo = jnp.exp(s - top)
            total = jnp.sum(expo, axis=-1, keepdims=True)
            p_ref[0, at : at + block, :] = (expo / total).astype(BF)
    o_ref[...] = join_heads(dot(p_ref[0], vs[...], PLAIN)).astype(BF)


def cross_forward_kernel(q_ref, k_ref, v_ref, o_ref, p_ref):
    s = dot(two_heads(q_ref[...]), k_ref[...], LAST)
    top = jnp.max(s, axis=-1, keepdims=True)
    expo = jnp.exp(s - top)
    total = jnp.sum(expo, axis=-1, keepdims=True)
    p_ref[0] = (expo / total).astype(BF)
    o_ref[...] = join_heads(dot(p_ref[0], v_ref[...], PLAIN)).astype(BF)


def score_gradient(probs, dom, values):
    dp = dot(dom, values, LAST)
    p = probs.astype(F32)
    delta = jnp.sum(p * dp, axis=-1, keepdims=True)
    return (p * (dp - delta)).astype(BF)


def cross_backward_kernel(q_ref, k_ref, v_ref, do_ref, p_ref, dq_ref, dk_ref, dv_ref):
    dom = two_heads(do_ref[...])
    probs = p_ref[0]
    ds = score_gradient(probs, dom, v_ref[...])
    dq_ref[...] = join_heads(dot(ds, k_ref[...], PLAIN)).astype(BF)
    dk_ref[...] = dot(ds, two_heads(q_ref[...]), FIRST).astype(BF)
    dv_ref[...] = dot(probs, dom, FIRST).astype(BF)


def self_backward_kernel(
    blocks_ref, own_ref, q_ref, k_ref, v_ref, do_ref, p_ref, dq_ref, dk_ref, dv_ref, db_ref, ks, vs, acc
):
    rows = q_ref.shape[0]
    block = rows // 2
    nkeys = k_ref.shape[0]
    to_positions(blocks_ref, k_ref, ks, block)
    to_positions(blocks_ref, v_ref, vs, block)
    dom = two_heads(do_ref[...])
    probs = p_ref[0]
    ds = score_gradient(probs, dom, vs[...])
    dq_ref[...] = join_heads(dot(ds, ks[...], PLAIN)).astype(BF)
    acc[...] = dot(ds, two_heads(q_ref[...]), FIRST)
    from_positions(blocks_ref, acc, dk_ref, block)
    acc[...] = dot(probs, dom, FIRST)
    from_positions(blocks_ref, acc, dv_ref, block)
    for head in range(2):
        lines = None
        for part in range(2):
            at = head * rows + part * block
            x = ds[at : at + block].astype(F32)
            size = block
            while size > 1:
                size //= 2
                x = x[:size] + pltpu.roll(x[size:], nkeys - size, 1)
            x = pltpu.roll(jnp.broadcast_to(x, (8, nkeys)), nkeys - own_ref[part] * block - 1, 1)
            lines = x if lines is None else lines + x
        db_ref[0, head : head + 1, :] = lines[0:1]


def column_block(rows, offset):
    return pl.BlockSpec((rows, LANES), lambda i, *_: (0, offset + i))


def whole_block(a, b):
    return pl.BlockSpec((1, a, b), lambda i, *_: (i, 0, 0))


def params():
    return pltpu.CompilerParams(vmem_limit_bytes=VMEM_LIMIT)


def cost(rows, nkeys, width, products):
    return pl.CostEstimate(
        flops=4 * rows * nkeys * width * products,
        bytes_accessed=4 * rows * nkeys * (width // LANES) + 8 * nkeys * width,
        transcendentals=2 * rows * nkeys * (width // LANES),
    )


def self_forward(blocks, own, q, kv, bias):
    rows, width = q.shape
    nkeys = kv.shape[0]
    pairs = width // LANES
    return pl.pallas_call(
        self_forward_kernel,
        grid_spec=pltpu.PrefetchScalarGridSpec(
            num_scalar_prefetch=2,
            grid=(pairs,),
            in_specs=[
                column_block(rows, 0),
                column_block(nkeys, 0),
                column_block(nkeys, pairs),
                whole_block(2, nkeys),
            ],
            out_specs=[column_block(rows, 0), whole_block(2 * rows, nkeys)],
            scratch_shapes=[pltpu.VMEM((nkeys, LANES), BF), pltpu.VMEM((nkeys, LANES), BF)],
        ),
        out_shape=[
            jax.ShapeDtypeStruct((rows, width), BF),
            jax.ShapeDtypeStruct((pairs, 2 * rows, nkeys), BF),
        ],
        compiler_params=params(),
        cost_estimate=cost(rows, nkeys, width, 2),
        name="self_forward",
    )(blocks, own, q, kv, kv, bias)


def self_backward(blocks, own, q, kv, do, probs):
    rows, width = q.shape
    nkeys = kv.shape[0]
    pairs = width // LANES
    return pl.pallas_call(
        self_backward_kernel,
        grid_spec=pltpu.PrefetchScalarGridSpec(
            num_scalar_prefetch=2,
            grid=(pairs,),
            in_specs=[
                column_block(rows, 0),
                column_block(nkeys, 0),
                column_block(nkeys, pairs),
                column_block(rows, 0),
                whole_block(2 * rows, nkeys),
            ],
            out_specs=[
                column_block(rows, 0),
                column_block(nkeys, 0),
                column_block(nkeys, 0),
                whole_block(2, nkeys),
            ],
            scratch_shapes=[
                pltpu.VMEM((nkeys, LANES), BF),
                pltpu.VMEM((nkeys, LANES), BF),
                pltpu.VMEM((nkeys, LANES), F32),
            ],
        ),
        out_shape=[
            jax.ShapeDtypeStruct((rows, width), BF),
            jax.ShapeDtypeStruct((nkeys, width), BF),
            jax.ShapeDtypeStruct((nkeys, width), BF),
            jax.ShapeDtypeStruct((pairs, 2, nkeys), F32),
        ],
        compiler_params=params(),
        cost_estimate=cost(rows, nkeys, width, 5),
        name="self_backward",
    )(blocks, own, q, kv, kv, do, probs)


def cross_forward(q, kv):
    rows, width = q.shape
    nkeys = kv.shape[0]
    pairs = width // LANES
    return pl.pallas_call(
        cross_forward_kernel,
        grid=(pairs,),
        in_specs=[column_block(rows, 0), column_block(nkeys, 0), column_block(nkeys, pairs)],
        out_specs=[column_block(rows, 0), whole_block(2 * rows, nkeys)],
        out_shape=[
            jax.ShapeDtypeStruct((rows, width), BF),
            jax.ShapeDtypeStruct((pairs, 2 * rows, nkeys), BF),
        ],
        compiler_params=params(),
        cost_estimate=cost(rows, nkeys, width, 2),
        name="cross_forward",
    )(q, kv, kv)


def cross_backward(q, kv, do, probs):
    rows, width = q.shape
    nkeys = kv.shape[0]
    pairs = width // LANES
    return pl.pallas_call(
        cross_backward_kernel,
        grid=(pairs,),
        in_specs=[
            column_block(rows, 0),
            column_block(nkeys, 0),
            column_block(nkeys, pairs),
            column_block(rows, 0),
            whole_block(2 * rows, nkeys),
        ],
        out_specs=[column_block(rows, 0), column_block(nkeys, 0), column_block(nkeys, 0)],
        out_shape=[
            jax.ShapeDtypeStruct((rows, width), BF),
            jax.ShapeDtypeStruct((nkeys, width), BF),
            jax.ShapeDtypeStruct((nkeys, width), BF),
        ],
        compiler_params=params(),
        cost_estimate=cost(rows, nkeys, width, 5),
        name="cross_backward",
    )(q, kv, kv, do, probs)


def split_kernel(products, nouts, core_ref, *refs):
    even = core_ref[0] == 0
    keep_ref, give_ref = refs[-2:]
    for i, (half, row, column) in enumerate(products):
        full = dot(refs[2 * i][...], refs[2 * i + 1][...], FIRST)
        cols = full.shape[1]
        for j in range(full.shape[0] // (2 * half)):
            low = full[2 * j * half : (2 * j + 1) * half]
            high = full[(2 * j + 1) * half : (2 * j + 2) * half]
            keep_ref[j, row : row + half, column : column + cols] = jnp.where(even, low, high).astype(BF)
            give_ref[j, row : row + half, column : column + cols] = jnp.where(even, high, low).astype(BF)


def split_grads(core, pairs, places, rows, cols):
    pieces = pairs[0][0].shape[1] // (2 * places[0][0])
    shape = jax.ShapeDtypeStruct((pieces, rows, cols), BF)
    if any(half % 8 != 0 or row % 16 != 0 for half, row, _ in places):
        keep, give = [], []
        for (a, g), (half, row, column) in zip(pairs, places):
            full = weight_grad(a, g).astype(BF).reshape(pieces, 2, half, g.shape[1])
            spot = ((0, 0), (row, rows - row - half), (column, cols - column - g.shape[1]))
            keep.append(jnp.pad(lax.dynamic_index_in_dim(full, core, 1, keepdims=False), spot))
            give.append(jnp.pad(lax.dynamic_index_in_dim(full, 1 - core, 1, keepdims=False), spot))
        return sum(keep[1:], keep[0]), sum(give[1:], give[0])
    vmem = pl.BlockSpec(memory_space=pltpu.VMEM)
    flat = [x for pair in pairs for x in pair]
    return pl.pallas_call(
        functools.partial(split_kernel, places, len(places)),
        in_specs=[pl.BlockSpec(memory_space=pltpu.SMEM)] + [vmem] * len(flat),
        out_specs=[vmem, vmem],
        out_shape=[shape, shape],
        compiler_params=params(),
        cost_estimate=pl.CostEstimate(
            flops=sum(2 * a.shape[0] * a.shape[1] * g.shape[1] for a, g in pairs),
            bytes_accessed=4 * pieces * rows * cols + sum(2 * x.size for x in flat),
            transcendentals=0,
        ),
        name="split_grads",
    )(core.reshape(1).astype(jnp.int32), *flat)


def place_kernel(dims, spot_ref, own_ref, other_ref, gate_ref, up_ref, down_ref):
    chips, nz, half, wide, down_half = dims
    for r, ref in enumerate((own_ref, other_ref)):
        core = spot_ref[1] ^ r
        for k in range(chips):
            chip = spot_ref[0] ^ k
            rows = pl.ds(pl.multiple_of(core * half, half), half)
            for i, out in enumerate((gate_ref, up_ref)):
                for z in range(nz):
                    source = (i * nz + z) * wide
                    spot = pl.multiple_of((z * chips + chip) * wide, wide)
                    out[rows, pl.ds(spot, wide)] = ref[k, :half, source : source + wide].astype(F32)
            rows = pl.ds(pl.multiple_of((2 * chip + core) * down_half, down_half), down_half)
            down_ref[rows, :] = ref[k, half : half + down_half, : down_ref.shape[1]].astype(F32)


def place_ff(chip, core, own, other, nz, half, wide, down_half, width):
    chips = own.shape[0]
    hidden = nz * chips * wide
    shapes = [
        jax.ShapeDtypeStruct((2 * half, hidden), F32),
        jax.ShapeDtypeStruct((2 * half, hidden), F32),
        jax.ShapeDtypeStruct((2 * chips * down_half, width), F32),
    ]
    vmem = pl.BlockSpec(memory_space=pltpu.VMEM)
    return pl.pallas_call(
        functools.partial(place_kernel, (chips, nz, half, wide, down_half)),
        in_specs=[pl.BlockSpec(memory_space=pltpu.SMEM), vmem, vmem],
        out_specs=[vmem] * 3,
        out_shape=shapes,
        compiler_params=params(),
        cost_estimate=pl.CostEstimate(flops=0, bytes_accessed=6 * own.size, transcendentals=0),
        name="place_ff",
    )(jnp.stack([chip, core]).astype(jnp.int32), own, other)


def fence(*arrays):
    return lax.optimization_barrier(arrays)


class Net:
    def __init__(self):
        self.c = lax.axis_index("ctx")
        self.z = lax.axis_index("fsdp")
        self.nc = lax.axis_size("ctx")
        self.nz = lax.axis_size("fsdp")
        self.chips = self.nc // 2
        self.core = self.c % 2
        self.chip = self.c // 2

    def to_core(self, x):
        return lax.ppermute(x, "ctx", [(i, i ^ 1) for i in range(self.nc)])

    def to_chip(self, x, k):
        return lax.ppermute(x, "ctx", [(i, i ^ (2 * k)) for i in range(self.nc)])

    def along(self, x, s):
        n = self.nz
        return lax.ppermute(x, "fsdp", [(i, (i + s) % n) for i in range(n)])


    def spread_z(self, x):
        return tuple(self.along(x, s) for s in range(1, self.nz))

    def join_z(self, x, got):
        out = jnp.zeros((self.nz,) + x.shape, x.dtype)
        out = lax.dynamic_update_index_in_dim(out, x, self.z, 0)
        for s, part in enumerate(got, 1):
            out = lax.dynamic_update_index_in_dim(out, part, (self.z + self.nz - s) % self.nz, 0)
        return out

    def spread_chips(self, x):
        return tuple(self.to_chip(x, k) for k in range(1, self.chips))

    def join_chips(self, x, got):
        out = jnp.zeros(x.shape[:1] + (self.chips,) + x.shape[1:], x.dtype)
        for k, part in enumerate((x,) + tuple(got)):
            out = lax.dynamic_update_index_in_dim(out, part, self.chip ^ k, 1)
        return out

    def join_cores(self, x, got):
        even = self.core == 0
        return jnp.stack([jnp.where(even, x, got), jnp.where(even, got, x)], axis=2)


    def give_chips(self, keep, got):
        def term(k):
            spot = self.chip ^ k
            kept = lax.dynamic_index_in_dim(keep, spot, 1, keepdims=False)
            other = lax.dynamic_index_in_dim(got, spot, 1, keepdims=False)
            return (kept.astype(F32) + other.astype(F32)).astype(BF)

        return (term(0),) + tuple(self.to_chip(term(k), k) for k in range(1, self.chips))

    def swap_blocks(self, x):
        return (x[0],) + tuple(self.to_chip(x[k], k) for k in range(1, self.chips))

    def add(self, parts):
        total = parts[0].astype(F32)
        for part in parts[1:]:
            total = total + part.astype(F32)
        return total

    def give_z(self, x):
        own = lax.dynamic_index_in_dim(x, self.z, 0, keepdims=False)
        return (own,) + tuple(
            self.along(lax.dynamic_index_in_dim(x, (self.z + s) % self.nz, 0, keepdims=False), s)
            for s in range(1, self.nz)
        )


def per_device(
    tokens,
    encoder,
    cotangent,
    buckets,
    pairing,
    norm_one,
    self_query,
    self_key,
    self_value,
    self_output,
    bias_table,
    norm_two,
    cross_query,
    cross_key,
    cross_value,
    cross_output,
    norm_three,
    ff_gate,
    ff_up,
    ff_down,
):
    net = Net()
    nc, nz, chips = net.nc, net.nz, net.chips
    mine = net.c
    shard = self_query.shape[0]
    width = self_query.shape[1]
    heads = bias_table.shape[1]
    pairs = width // LANES
    each = shard // nc
    half = shard // 2
    down_shard = ff_down.shape[0]
    wide = down_shard // chips
    down_half = wide // 2
    pack_rows = half + down_half

    def rows_of(w):
        return lax.dynamic_slice_in_dim(w, mine * each, each, 0)

    def flat(x):
        return x.reshape(-1, x.shape[-1])

    table_size = bias_table.size
    extra_width = LANES * math.ceil((4 + table_size) / LANES)
    small = jnp.stack([norm_one, norm_two, norm_three], axis=1)
    small = jnp.pad(rows_of(small), ((0, 0), (0, extra_width - 3)))
    line = jnp.pad(bias_table.reshape(1, -1), ((0, each - 1), (4, extra_width - 4 - table_size)))
    one = jnp.concatenate([rows_of(self_query), rows_of(self_key), rows_of(self_value), small + line], axis=1)
    two = jnp.concatenate(
        [rows_of(w) for w in (self_output, cross_query, cross_key, cross_value, cross_output)], axis=1
    )

    def columns_of(w):
        w = lax.dynamic_slice_in_dim(w, net.core * half, half, 0)
        return [lax.dynamic_slice_in_dim(w, down_shard * z + wide * net.chip, wide, 1) for z in range(nz)]

    three = jnp.concatenate(columns_of(ff_gate) + columns_of(ff_up), axis=1)
    pack_cols = max(three.shape[1], width)
    down = lax.dynamic_slice_in_dim(ff_down, wide * net.chip + down_half * net.core, down_half, 0)
    three = jnp.concatenate(
        [
            jnp.pad(three, ((0, 0), (0, pack_cols - three.shape[1]))),
            jnp.pad(down, ((0, 0), (0, pack_cols - width))),
        ],
        axis=0,
    )
    rows_one = jnp.concatenate([tokens[0], encoder[0]], axis=0)
    incoming = cotangent[0]

    one_z, rows_chips = fence(net.spread_z(one), net.spread_chips(rows_one))
    one = net.join_z(one, one_z)
    rows_mine = jnp.stack((rows_one,) + rows_chips)
    one, rows_mine, two, three = fence(one, rows_mine, two, three)
    one_chips, rows_core, two_z = fence(net.spread_chips(one), net.to_core(rows_mine), net.spread_z(two))
    one = net.join_chips(one, one_chips)
    two = net.join_z(two, two_z)
    one, two, three, incoming = fence(one, two, three, incoming)
    one_core = net.to_core(one)
    three_z = net.spread_z(three)
    two_chips = net.spread_chips(two)
    incoming_chips = net.spread_chips(incoming)
    one = flat(net.join_cores(one, one_core))

    w_q = one[:, :width]
    w_kv = one[:, width : 3 * width]
    extra = one[:, 3 * width :]
    gains = extra[:, :4].astype(F32).T
    g_one, g_two, g_three = gains[0], gains[1], gains[2]
    table = extra.reshape(nz, shard, extra_width)[:, 0, 4 : 4 + table_size].reshape(-1, heads)
    nbuckets = table.shape[0]

    count = tokens.shape[1]
    seq_len = count * nc
    tokens_all = jnp.concatenate([flat(rows_mine[:, :count]), flat(rows_core[:, :count])], axis=0)
    states_all = jnp.concatenate([flat(rows_mine[:, count:]), flat(rows_core[:, count:])], axis=0)
    member = mine ^ jnp.array([2 * k + r for r in range(2) for k in range(chips)], dtype=jnp.int32)
    match = member[:, None] == jnp.arange(nc, dtype=jnp.int32)[None, :]
    paired = jnp.sum(jnp.where(match, pairing[None, :], 0), axis=1)
    blocks = jnp.stack([paired, 2 * nc - 1 - paired], axis=1).reshape(-1).astype(jnp.int32)
    own = blocks[:2]

    picks = (buckets[::-1][None, :] == jnp.arange(nbuckets, dtype=jnp.int32)[:, None]).astype(BF)
    bias = jnp.dot(table.T, picks, preferred_element_type=F32).reshape(pairs, 2, seq_len)

    rows_in = tokens[0].astype(F32)
    a_one, norm_one_back = jax.vjp(norm_apply, rows_in, g_one)
    a_one = a_one.astype(BF)
    a_one_all = norm_apply(tokens_all.astype(F32), g_one).astype(BF)
    query = product(a_one, w_q).astype(BF)
    kv = product(a_one_all, w_kv).astype(BF)
    attended, self_probs = self_forward(blocks, own, query, kv, bias)
    attended, two_chips, three_z, incoming_chips = fence(attended, two_chips, three_z, incoming_chips)
    two = net.join_chips(two, two_chips)
    three = net.join_z(three, three_z)
    two_core = net.to_core(two)
    three_core = net.to_core(three)
    incoming_rows = flat(jnp.stack((incoming,) + incoming_chips))
    two = flat(net.join_cores(two, two_core))
    w_o = two[:, :width]
    c_q = two[:, width : 2 * width]
    c_kv = two[:, 2 * width : 4 * width]
    c_o = two[:, 4 * width :]
    second = rows_in + product(attended, w_o)
    cross_kv = product(states_all, c_kv).astype(BF)
    a_two, norm_two_back = jax.vjp(norm_apply, second, g_two)
    a_two = a_two.astype(BF)
    cross_q = product(a_two, c_q).astype(BF)
    cross_o, cross_probs = cross_forward(cross_q, cross_kv)
    third = second + product(cross_o, c_o)
    a_three, norm_three_back = jax.vjp(norm_apply, third, g_three)
    a_three = a_three.astype(BF)

    a_three_chips = net.spread_chips(a_three)
    even = net.core == 0
    three_low, three_high = jnp.where(even, three, three_core), jnp.where(even, three_core, three)
    w_gu = jnp.stack([three_low[:, :half], three_high[:, :half]], axis=1)[..., : 2 * nz * wide].reshape(nz * shard, -1)
    w_down = flat(jnp.stack([three_low[:, half:], three_high[:, half:]], axis=1)[..., :width])
    w_gu, w_down, incoming_rows, a_three_chips = fence(w_gu, w_down, incoming_rows, a_three_chips)
    a_three_rows = flat(jnp.stack((a_three,) + a_three_chips))
    gate_up = product(a_three_rows, w_gu)
    units = nz * wide
    hidden, geglu_back = jax.vjp(
        lambda left, right: jax.nn.gelu(left, approximate=True) * right, gate_up[:, :units], gate_up[:, units:]
    )
    hidden = hidden.astype(BF)
    grad_gate, grad_up = geglu_back(through(incoming_rows, w_down))
    grad_gate_up = jnp.concatenate([grad_gate.astype(BF), grad_up.astype(BF)], axis=1)
    grad_three_part = through(grad_gate_up, w_gu).astype(BF).reshape(chips, count, width)
    result_part = product(hidden, w_down).astype(BF).reshape(chips, count, width)
    grad_three_terms = net.swap_blocks(grad_three_part)
    three_keep, three_give = split_grads(
        net.core,
        [(a_three_rows, grad_gate_up), (hidden, incoming_rows)],
        [(half, 0, 0), (down_half, half, 0)],
        pack_rows,
        pack_cols,
    )
    grad_three_terms, three_keep, three_give, result_part = fence(
        grad_three_terms, three_keep, three_give, result_part
    )
    three_core = net.to_core(three_give)
    result_terms = net.swap_blocks(result_part)

    part_three, grad_g_three = norm_three_back(net.add(grad_three_terms))
    grad_third = incoming.astype(F32) + part_three
    branch_two = grad_third.astype(BF)
    grad_cross_o = through(branch_two, c_o).astype(BF)
    dcq, dck, dcv = cross_backward(cross_q, cross_kv, grad_cross_o, cross_probs)
    dcq, dck, dcv, three_core, result_terms = fence(dcq, dck, dcv, three_core, result_terms)
    result = third + net.add(result_terms)
    three_terms = net.give_z(net.add((three_keep, three_core)).astype(BF))
    states_part = through(dck, c_kv[:, :width]) + through(dcv, c_kv[:, width:])
    part_two, grad_g_two = norm_two_back(through(dcq, c_q))
    grad_second = grad_third + part_two
    branch_one = grad_second.astype(BF)
    two_keep, two_give = split_grads(
        net.core,
        [
            (attended, branch_one),
            (a_two, dcq),
            (states_all, dck),
            (states_all, dcv),
            (cross_o, branch_two),
        ],
        [(each, 0, i * width) for i in range(5)],
        each,
        5 * width,
    )
    grad_attended = through(branch_one, w_o).astype(BF)
    grad_attended, two_keep, two_give, three_terms = fence(grad_attended, two_keep, two_give, three_terms)
    two_keep = two_keep.reshape(nz, chips, each, -1)
    two_core = net.to_core(two_give.reshape(nz, chips, each, -1))
    three = net.add(three_terms).astype(BF)
    three_chips = net.spread_chips(three)
    dq, dk, dv, bias_grad = self_backward(blocks, own, query, kv, grad_attended, self_probs)
    dq, dk, dv, bias_grad, two_core, three_chips = fence(dq, dk, dv, bias_grad, two_core, three_chips)
    three = jnp.stack((three,) + three_chips)
    two_terms = net.give_chips(two_keep, two_core)
    three_core = net.to_core(three)
    rows_part = (through(dk, w_kv[:, :width]) + through(dv, w_kv[:, width:])).astype(BF).reshape(2, chips, count, width)
    states_part = states_part.astype(BF).reshape(2, chips, -1, width)
    sent_keep, sent_give = (jnp.concatenate([rows_part[r], states_part[r]], axis=1) for r in range(2))
    sent_core = net.to_core(sent_give)
    one_keep, one_give = split_grads(
        net.core,
        [(a_one, dq), (a_one_all, dk), (a_one_all, dv)],
        [(each, 0, i * width) for i in range(3)],
        each,
        3 * width,
    )
    one_keep = one_keep.reshape(nz, chips, each, -1)
    one_core = net.to_core(one_give.reshape(nz, chips, each, -1))
    table_grad = lax.dot_general(
        picks.astype(F32), bias_grad.reshape(heads, seq_len), LAST, precision=lax.Precision.HIGHEST
    )
    sent_core, one_core, two_terms, three_core, table_grad = fence(
        sent_core, one_core, two_terms, three_core, table_grad
    )
    sent_terms = net.swap_blocks((sent_keep.astype(F32) + sent_core.astype(F32)).astype(BF))
    one_terms = net.give_chips(one_keep, one_core)
    two_terms = net.give_z(net.add(two_terms).astype(BF))
    if wide % LANES == 0 and half % 16 == 0 and down_half % 16 == 0:
        total_gate, total_up, total_down = place_ff(
            net.chip, net.core, three, three_core, nz, half, wide, down_half, width
        )
    else:
        joined = net.join_chips(three[:1], three[1:, None])
        joined_other = net.join_chips(three_core[:1], three_core[1:, None])
        joined = net.join_cores(joined, joined_other)[0].astype(F32)
        total_gu = joined[:, :, :half, : 2 * units].reshape(chips, 2, half, 2, nz, wide)
        total_gu = total_gu.transpose(3, 1, 2, 4, 0, 5).reshape(2, shard, -1)
        total_gate, total_up = total_gu[0], total_gu[1]
        total_down = joined[:, :, half:, :width].reshape(-1, width)
    sent_terms, total_gate, total_up, total_down = fence(sent_terms, total_gate, total_up, total_down)
    own_part = net.add(sent_terms)
    grad_a_one = through(dq, w_q) + own_part[:count]
    grad_states = own_part[count:]
    part_one, grad_g_one = norm_one_back(grad_a_one)
    grad_rows = grad_second + part_one

    small_grad = jnp.pad(jnp.stack([grad_g_one, grad_g_two, grad_g_three]), ((0, 1), (0, 0)))
    small_grad = small_grad.reshape(4, nz, shard).swapaxes(0, 1).reshape(nz, -1)
    small_grad = jnp.concatenate([small_grad, table_grad.reshape(nz, table_size)], axis=1).astype(BF)
    small_size = small_grad.shape[1]
    small_cols = math.ceil(small_size / each)
    small_width = LANES * math.ceil(small_cols / LANES)
    small_grad = jnp.pad(small_grad, ((0, 0), (0, each * small_cols - small_size))).reshape(nz, each, small_cols)
    small_grad = jnp.pad(small_grad, ((0, 0), (0, 0), (0, small_width - small_cols)))
    one_terms, two_terms, small_grad = fence(one_terms, two_terms, small_grad)
    one_sum = jnp.concatenate([net.add(one_terms).astype(BF), small_grad], axis=2)
    one_terms = net.give_z(one_sum)
    two = net.add(two_terms).astype(BF)[None]
    two_chips = net.spread_chips(two)
    one_terms, two_chips = fence(one_terms, two_chips)
    one = net.add(one_terms).astype(BF)[None]
    one_chips = net.spread_chips(one)
    two = net.join_chips(two, two_chips)
    two_core = net.to_core(two)
    one_chips, two_core = fence(one_chips, two_core)
    one = net.join_chips(one, one_chips)
    one_core = net.to_core(one)
    total_two = flat(net.join_cores(two, two_core)).astype(F32)
    one = net.join_cores(one, one_core)
    total_one = flat(one[..., : 3 * width]).astype(F32)
    small_total = jnp.sum(one[..., 3 * width : 3 * width + small_cols].reshape(nc, -1).astype(F32), axis=0)
    gain_total = small_total[: 4 * shard].reshape(4, shard)
    table_total = small_total[4 * shard : 4 * shard + table_size].reshape(-1, heads)

    return (
        result.astype(BF)[None],
        grad_rows[None],
        grad_states[None],
        gain_total[0],
        total_one[:, :width],
        total_one[:, width : 2 * width],
        total_one[:, 2 * width : 3 * width],
        total_two[:, :width],
        table_total,
        gain_total[1],
        total_two[:, width : 2 * width],
        total_two[:, 2 * width : 3 * width],
        total_two[:, 3 * width : 4 * width],
        total_two[:, 4 * width :],
        gain_total[2],
        total_gate,
        total_up,
        total_down,
    )


def solution(mesh):
    rows = P("fsdp", "ctx", None)
    gain = P("fsdp")
    weight = P("fsdp", None)
    gradients = (
        gain, weight, weight, weight, weight, weight, gain, weight, weight, weight, weight, gain, weight, weight, weight
    )
    return jax.shard_map(
        per_device,
        mesh=mesh,
        in_specs=(rows, rows, rows, P(), P()) + gradients,
        out_specs=(rows, rows, rows) + gradients,
        check_vma=False,
    )
```

```python
import functools
import math

import jax
import jax.numpy as jnp
from jax import lax
from jax.experimental import pallas as pl
from jax.experimental.pallas import tpu as pltpu
from jax.sharding import PartitionSpec as P

BF = jnp.bfloat16
F32 = jnp.float32
LANES = 128
VMEM_LIMIT = 48 * 1024 * 1024
LAST = (((1,), (1,)), ((), ()))
FIRST = (((0,), (0,)), ((), ()))
PLAIN = (((1,), (0,)), ((), ()))


def norm_apply(v, g):
    return v * lax.rsqrt(jnp.mean(v * v, axis=-1, keepdims=True) + 1e-06) * g


def product(a, w):
    return jnp.dot(a, w, preferred_element_type=F32)


def through(grad, w):
    return lax.dot_general(grad, w, LAST, preferred_element_type=F32)


def weight_grad(a, grad):
    return lax.dot_general(a, grad, FIRST, preferred_element_type=F32)


def dot(a, b, dims):
    return lax.dot_general(a, b, dims, preferred_element_type=F32)


def two_heads(block):
    half = block.shape[1] // 2
    low = lax.broadcasted_iota(jnp.int32, block.shape, 1) < half
    zero = jnp.zeros_like(block)
    return jnp.concatenate([jnp.where(low, block, zero), jnp.where(low, zero, block)], axis=0)


def join_heads(rows):
    n = rows.shape[0] // 2
    low = lax.broadcasted_iota(jnp.int32, (n, rows.shape[1]), 1) < rows.shape[1] // 2
    return jnp.where(low, rows[:n], rows[n:])


def to_positions(blocks_ref, source, target, block):
    for i in range(source.shape[0] // block):
        spot = pl.multiple_of(blocks_ref[i] * block, block)
        target[pl.ds(spot, block), :] = source[i * block : (i + 1) * block, :]


def from_positions(blocks_ref, source, target, block):
    for i in range(target.shape[0] // block):
        spot = pl.multiple_of(blocks_ref[i] * block, block)
        target[i * block : (i + 1) * block, :] = source[pl.ds(spot, block), :].astype(target.dtype)


def sheared(line, block):
    sublane = lax.broadcasted_iota(jnp.int32, line.shape, 0)
    for bit in (1, 2, 4):
        line = jnp.where(sublane & bit != 0, pltpu.roll(line, bit, 1), line)
    return jnp.concatenate([line if i == 0 else pltpu.roll(line, i, 1) for i in range(0, block, 8)], axis=0)


def self_forward_kernel(blocks_ref, own_ref, q_ref, k_ref, v_ref, bias_ref, o_ref, p_ref, ks, vs):
    rows = q_ref.shape[0]
    block = rows // 2
    nkeys = k_ref.shape[0]
    to_positions(blocks_ref, k_ref, ks, block)
    to_positions(blocks_ref, v_ref, vs, block)
    scores = dot(two_heads(q_ref[...]), ks[...], LAST)
    column = lax.broadcasted_iota(jnp.int32, (block, nkeys), 1)
    row = lax.broadcasted_iota(jnp.int32, (block, nkeys), 0)
    for head in range(2):
        line = jnp.broadcast_to(bias_ref[0, head : head + 1, :], (8, nkeys))
        for part in range(2):
            start = own_ref[part] * block
            shear = sheared(pltpu.roll(line, start + 1, 1), block)
            at = head * rows + part * block
            s = jnp.where(column <= row + start, scores[at : at + block] + shear, -1e30)
            top = jnp.max(s, axis=-1, keepdims=True)
            expo = jnp.exp(s - top)
            total = jnp.sum(expo, axis=-1, keepdims=True)
            p_ref[0, at : at + block, :] = (expo / total).astype(BF)
    o_ref[...] = join_heads(dot(p_ref[0], vs[...], PLAIN)).astype(BF)


def cross_forward_kernel(q_ref, k_ref, v_ref, o_ref, p_ref):
    s = dot(two_heads(q_ref[...]), k_ref[...], LAST)
    top = jnp.max(s, axis=-1, keepdims=True)
    expo = jnp.exp(s - top)
    total = jnp.sum(expo, axis=-1, keepdims=True)
    p_ref[0] = (expo / total).astype(BF)
    o_ref[...] = join_heads(dot(p_ref[0], v_ref[...], PLAIN)).astype(BF)


def score_gradient(probs, dom, values):
    dp = dot(dom, values, LAST)
    p = probs.astype(F32)
    delta = jnp.sum(p * dp, axis=-1, keepdims=True)
    return (p * (dp - delta)).astype(BF)


def cross_backward_kernel(q_ref, k_ref, v_ref, do_ref, p_ref, dq_ref, dk_ref, dv_ref):
    dom = two_heads(do_ref[...])
    probs = p_ref[0]
    ds = score_gradient(probs, dom, v_ref[...])
    dq_ref[...] = join_heads(dot(ds, k_ref[...], PLAIN)).astype(BF)
    dk_ref[...] = dot(ds, two_heads(q_ref[...]), FIRST).astype(BF)
    dv_ref[...] = dot(probs, dom, FIRST).astype(BF)


def self_backward_kernel(
    blocks_ref, own_ref, q_ref, k_ref, v_ref, do_ref, p_ref, dq_ref, dk_ref, dv_ref, db_ref, ks, vs, acc
):
    rows = q_ref.shape[0]
    block = rows // 2
    nkeys = k_ref.shape[0]
    to_positions(blocks_ref, k_ref, ks, block)
    to_positions(blocks_ref, v_ref, vs, block)
    dom = two_heads(do_ref[...])
    probs = p_ref[0]
    ds = score_gradient(probs, dom, vs[...])
    dq_ref[...] = join_heads(dot(ds, ks[...], PLAIN)).astype(BF)
    acc[...] = dot(ds, two_heads(q_ref[...]), FIRST)
    from_positions(blocks_ref, acc, dk_ref, block)
    acc[...] = dot(probs, dom, FIRST)
    from_positions(blocks_ref, acc, dv_ref, block)
    for head in range(2):
        lines = None
        for part in range(2):
            at = head * rows + part * block
            x = ds[at : at + block].astype(F32)
            size = block
            while size > 1:
                size //= 2
                x = x[:size] + pltpu.roll(x[size:], nkeys - size, 1)
            x = pltpu.roll(jnp.broadcast_to(x, (8, nkeys)), nkeys - own_ref[part] * block - 1, 1)
            lines = x if lines is None else lines + x
        db_ref[0, head : head + 1, :] = lines[0:1]


def column_block(rows, offset):
    return pl.BlockSpec((rows, LANES), lambda i, *_: (0, offset + i))


def whole_block(a, b):
    return pl.BlockSpec((1, a, b), lambda i, *_: (i, 0, 0))


def params():
    return pltpu.CompilerParams(vmem_limit_bytes=VMEM_LIMIT)


def cost(rows, nkeys, width, weight):
    return pl.CostEstimate(
        flops=2 * rows * nkeys * width * weight,
        bytes_accessed=4 * rows * nkeys * (width // LANES),
        transcendentals=0,
    )


def self_forward(blocks, own, q, kv, bias):
    rows, width = q.shape
    nkeys = kv.shape[0]
    pairs = width // LANES
    return pl.pallas_call(
        self_forward_kernel,
        grid_spec=pltpu.PrefetchScalarGridSpec(
            num_scalar_prefetch=2,
            grid=(pairs,),
            in_specs=[
                column_block(rows, 0),
                column_block(nkeys, 0),
                column_block(nkeys, pairs),
                whole_block(2, nkeys),
            ],
            out_specs=[column_block(rows, 0), whole_block(2 * rows, nkeys)],
            scratch_shapes=[pltpu.VMEM((nkeys, LANES), BF), pltpu.VMEM((nkeys, LANES), BF)],
        ),
        out_shape=[
            jax.ShapeDtypeStruct((rows, width), BF),
            jax.ShapeDtypeStruct((pairs, 2 * rows, nkeys), BF),
        ],
        compiler_params=params(),
        cost_estimate=cost(rows, nkeys, width, 45),
        name="self_forward",
    )(blocks, own, q, kv, kv, bias)


def self_backward(blocks, own, q, kv, do, probs):
    rows, width = q.shape
    nkeys = kv.shape[0]
    pairs = width // LANES
    return pl.pallas_call(
        self_backward_kernel,
        grid_spec=pltpu.PrefetchScalarGridSpec(
            num_scalar_prefetch=2,
            grid=(pairs,),
            in_specs=[
                column_block(rows, 0),
                column_block(nkeys, 0),
                column_block(nkeys, pairs),
                column_block(rows, 0),
                whole_block(2 * rows, nkeys),
            ],
            out_specs=[
                column_block(rows, 0),
                column_block(nkeys, 0),
                column_block(nkeys, 0),
                whole_block(2, nkeys),
            ],
            scratch_shapes=[
                pltpu.VMEM((nkeys, LANES), BF),
                pltpu.VMEM((nkeys, LANES), BF),
                pltpu.VMEM((nkeys, LANES), F32),
            ],
        ),
        out_shape=[
            jax.ShapeDtypeStruct((rows, width), BF),
            jax.ShapeDtypeStruct((nkeys, width), BF),
            jax.ShapeDtypeStruct((nkeys, width), BF),
            jax.ShapeDtypeStruct((pairs, 2, nkeys), F32),
        ],
        compiler_params=params(),
        cost_estimate=pl.CostEstimate(flops=0, bytes_accessed=0, transcendentals=0),
        name="self_backward",
    )(blocks, own, q, kv, kv, do, probs)


def cross_forward(q, kv):
    rows, width = q.shape
    nkeys = kv.shape[0]
    pairs = width // LANES
    return pl.pallas_call(
        cross_forward_kernel,
        grid=(pairs,),
        in_specs=[column_block(rows, 0), column_block(nkeys, 0), column_block(nkeys, pairs)],
        out_specs=[column_block(rows, 0), whole_block(2 * rows, nkeys)],
        out_shape=[
            jax.ShapeDtypeStruct((rows, width), BF),
            jax.ShapeDtypeStruct((pairs, 2 * rows, nkeys), BF),
        ],
        compiler_params=params(),
        cost_estimate=cost(rows, nkeys, width, 40),
        name="cross_forward",
    )(q, kv, kv)


def cross_backward(q, kv, do, probs):
    rows, width = q.shape
    nkeys = kv.shape[0]
    pairs = width // LANES
    return pl.pallas_call(
        cross_backward_kernel,
        grid=(pairs,),
        in_specs=[
            column_block(rows, 0),
            column_block(nkeys, 0),
            column_block(nkeys, pairs),
            column_block(rows, 0),
            whole_block(2 * rows, nkeys),
        ],
        out_specs=[column_block(rows, 0), column_block(nkeys, 0), column_block(nkeys, 0)],
        out_shape=[
            jax.ShapeDtypeStruct((rows, width), BF),
            jax.ShapeDtypeStruct((nkeys, width), BF),
            jax.ShapeDtypeStruct((nkeys, width), BF),
        ],
        compiler_params=params(),
        cost_estimate=cost(rows, nkeys, width, 50),
        name="cross_backward",
    )(q, kv, kv, do, probs)


def split_kernel(products, nouts, core_ref, *refs):
    even = core_ref[0] == 0
    keep_ref, give_ref = refs[-2:]
    chips = keep_ref.shape[1]
    for i, (half, row, column) in enumerate(products):
        full = dot(refs[2 * i][...], refs[2 * i + 1][...], FIRST)
        cols = full.shape[1]
        for j in range(full.shape[0] // (2 * half)):
            low = full[2 * j * half : (2 * j + 1) * half]
            high = full[(2 * j + 1) * half : (2 * j + 2) * half]
            spot = (j // chips, j % chips, slice(row, row + half), slice(column, column + cols))
            keep_ref[spot] = jnp.where(even, low, high).astype(BF)
            give_ref[spot] = jnp.where(even, high, low).astype(BF)


def split_grads(core, pairs, places, chips, rows, cols):
    pieces = pairs[0][0].shape[1] // (2 * places[0][0])
    dims = (pieces // chips, chips, rows, cols)
    shape = jax.ShapeDtypeStruct(dims, BF)
    if any(half % 8 != 0 or row % 16 != 0 for half, row, _ in places):
        keep, give = [], []
        for (a, g), (half, row, column) in zip(pairs, places):
            full = weight_grad(a, g).astype(BF).reshape(pieces, 2, half, g.shape[1])
            spot = ((0, 0), (row, rows - row - half), (column, cols - column - g.shape[1]))
            keep.append(jnp.pad(lax.dynamic_index_in_dim(full, core, 1, keepdims=False), spot))
            give.append(jnp.pad(lax.dynamic_index_in_dim(full, 1 - core, 1, keepdims=False), spot))
        return sum(keep[1:], keep[0]).reshape(dims), sum(give[1:], give[0]).reshape(dims)
    vmem = pl.BlockSpec(memory_space=pltpu.VMEM)
    flat = [x for pair in pairs for x in pair]
    return pl.pallas_call(
        functools.partial(split_kernel, places, len(places)),
        in_specs=[pl.BlockSpec(memory_space=pltpu.SMEM)] + [vmem] * len(flat),
        out_specs=[vmem, vmem],
        out_shape=[shape, shape],
        compiler_params=params(),
        cost_estimate=pl.CostEstimate(flops=0, bytes_accessed=0, transcendentals=0),
        name="split_grads",
    )(core.reshape(1).astype(jnp.int32), *flat)


def pick_kernel(dims, spot_ref, gate_ref, up_ref, down_ref, out_ref):
    chips, nz, half, wide, down_half = dims
    width = down_ref.shape[1]
    rows = pl.ds(pl.multiple_of(spot_ref[1] * half, half), half)
    for i, ref in enumerate((gate_ref, up_ref)):
        for z in range(nz):
            source = pl.multiple_of((z * chips + spot_ref[0]) * wide, wide)
            target = (i * nz + z) * wide
            out_ref[:half, target : target + wide] = ref[rows, pl.ds(source, wide)]
    rows = pl.ds(pl.multiple_of((2 * spot_ref[0] + spot_ref[1]) * down_half, down_half), down_half)
    out_ref[half:, :width] = down_ref[rows, :]
    out_ref[half:, width:] = jnp.zeros((down_half, out_ref.shape[1] - width), out_ref.dtype)


def pick_ff(chip, core, gate, up, down, chips):
    half, wide = gate.shape[0] // 2, down.shape[0] // chips
    nz, down_half, width = gate.shape[1] // down.shape[0], wide // 2, down.shape[1]
    cols = 2 * nz * wide
    if wide % LANES != 0 or half % 16 != 0 or down_half % 16 != 0 or cols < width:
        pieces = []
        for w in (gate, up):
            w = lax.dynamic_slice_in_dim(w, core * half, half, 0)
            for z in range(nz):
                pieces.append(lax.dynamic_slice_in_dim(w, (z * chips + chip) * wide, wide, 1))
        pieces = jnp.concatenate(pieces, axis=1)
        down = lax.dynamic_slice_in_dim(down, (2 * chip + core) * down_half, down_half, 0)
        most = max(cols, width)
        return jnp.concatenate(
            [jnp.pad(pieces, ((0, 0), (0, most - cols))), jnp.pad(down, ((0, 0), (0, most - width)))], axis=0
        )
    vmem = pl.BlockSpec(memory_space=pltpu.VMEM)
    return pl.pallas_call(
        functools.partial(pick_kernel, (chips, nz, half, wide, down_half)),
        in_specs=[pl.BlockSpec(memory_space=pltpu.SMEM), vmem, vmem, vmem],
        out_specs=vmem,
        out_shape=jax.ShapeDtypeStruct((half + down_half, cols), gate.dtype),
        compiler_params=params(),
        cost_estimate=pl.CostEstimate(flops=0, bytes_accessed=6 * gate.size, transcendentals=0),
        name="pick_ff",
    )(jnp.stack([chip, core]).astype(jnp.int32), gate, up, down)


def assemble_kernel(spot_ref, mine_ref, other_ref, out_ref):
    chips, nz = mine_ref.shape[:2]
    for r, ref in enumerate((mine_ref, other_ref)):
        for k in range(chips):
            member = 2 * (spot_ref[0] ^ k) + (spot_ref[1] ^ r)
            for z in range(nz):
                out_ref[z, member] = ref[k, z]


def assemble(chip, core, mine, other):
    chips, nz, rows, cols = mine.shape
    vmem = pl.BlockSpec(memory_space=pltpu.VMEM)
    out = pl.pallas_call(
        assemble_kernel,
        in_specs=[pl.BlockSpec(memory_space=pltpu.SMEM), vmem, vmem],
        out_specs=vmem,
        out_shape=jax.ShapeDtypeStruct((nz, 2 * chips, rows, cols), mine.dtype),
        compiler_params=params(),
        cost_estimate=pl.CostEstimate(flops=0, bytes_accessed=8 * mine.size, transcendentals=0),
        name="assemble",
    )(jnp.stack([chip, core]).astype(jnp.int32), mine, other)
    return out.reshape(-1, cols)


def place_kernel(dims, parts_ref, gate_ref, up_ref, down_ref):
    chips, nz, half, wide, down_half = dims
    for member in range(2 * chips):
        chip, core = member // 2, member % 2
        for i, out in enumerate((gate_ref, up_ref)):
            for z in range(nz):
                source = (i * nz + z) * wide
                spot = (z * chips + chip) * wide
                out[core * half : (core + 1) * half, spot : spot + wide] = parts_ref[
                    member, :half, source : source + wide
                ].astype(F32)
        down_ref[member * down_half : (member + 1) * down_half, :] = parts_ref[
            member, half : half + down_half, : down_ref.shape[1]
        ].astype(F32)


def place_ff(parts, nz, half, wide, down_half, width):
    members = parts.shape[0]
    chips = members // 2
    hidden = nz * chips * wide
    if wide % LANES != 0 or half % 16 != 0 or down_half % 16 != 0:
        both = parts[:, :half, : 2 * nz * wide].astype(F32).reshape(chips, 2, half, 2, nz, wide)
        both = both.transpose(3, 1, 2, 4, 0, 5).reshape(2, 2 * half, hidden)
        return both[0], both[1], parts[:, half:, :width].astype(F32).reshape(-1, width)
    vmem = pl.BlockSpec(memory_space=pltpu.VMEM)
    return pl.pallas_call(
        functools.partial(place_kernel, (chips, nz, half, wide, down_half)),
        in_specs=[vmem],
        out_specs=[vmem] * 3,
        out_shape=[
            jax.ShapeDtypeStruct((2 * half, hidden), F32),
            jax.ShapeDtypeStruct((2 * half, hidden), F32),
            jax.ShapeDtypeStruct((members * down_half, width), F32),
        ],
        compiler_params=params(),
        cost_estimate=pl.CostEstimate(flops=0, bytes_accessed=6 * parts.size, transcendentals=0),
        name="place_ff",
    )(parts)


def fence(*arrays):
    return lax.optimization_barrier(arrays)


def vmem_call(kernel, scalars, arrays, shapes, name, scratch=()):
    vmem = pl.BlockSpec(memory_space=pltpu.VMEM)
    return pl.pallas_call(
        kernel,
        in_specs=[pl.BlockSpec(memory_space=pltpu.SMEM)] + [vmem] * len(arrays),
        out_specs=[vmem] * len(shapes),
        out_shape=shapes,
        scratch_shapes=list(scratch),
        compiler_params=params(),
        cost_estimate=pl.CostEstimate(flops=0, bytes_accessed=2 * sum(x.size for x in arrays), transcendentals=0),
        name=name,
    )(jnp.stack(scalars).astype(jnp.int32), *arrays)


def chip_bit(chips, step, h):
    return 1 << ((step + h) % (chips.bit_length() - 1))


def held_before(chips, step, h):
    spots = list(range(chips))
    for i in range(step):
        spots = [k for k in spots if not k & chip_bit(chips, i, h)]
    return spots


def first_kernel(more, spot_ref, keep_ref, got_ref, *refs):
    rows_ref = refs[0] if more else None
    outs = refs[-4:]
    nz, chips = keep_ref.shape[:2]
    for h in range(2):
        b = chip_bit(chips, 0, h)
        stays = [k for k in range(chips) if not k & b]
        for k in range(chips):
            out = outs[h] if k & b else outs[2 + h]
            i = stays.index(k & ~b)
            for zz in range(nz // 2):
                z = h * (nz // 2) + zz
                chip = spot_ref[0] ^ k
                total = keep_ref[z, chip].astype(F32) + got_ref[z, chip].astype(F32)
                out[i, zz, more:, :] = total.astype(BF)
                if more:
                    out[i, zz, :more, :] = rows_ref[k, z]


def next_kernel(chips, step, spot_ref, kept0, kept1, got0, got1, give0, give1, keep0, keep1):
    for h, (kept, got, give, keep) in enumerate(((kept0, got0, give0, keep0), (kept1, got1, give1, keep1))):
        b = chip_bit(chips, step, h)
        spots = held_before(chips, step, h)
        stays = [k for k in spots if not k & b]
        for i, k in enumerate(spots):
            total = (kept[i].astype(F32) + got[i].astype(F32)).astype(BF)
            if k & b:
                give[stays.index(k & ~b)] = total
            else:
                keep[stays.index(k)] = total


def half_sum(kept, got, z):
    return (kept[0, z].astype(F32) + got[0, z].astype(F32)).astype(BF)


def last_kernel(more, spot_ref, kept0, kept1, got0, got1, *outs):
    n = kept0.shape[1]
    for h, (kept, got) in enumerate(((kept0, got0), (kept1, got1))):
        for zz in range(n):
            total = half_sum(kept, got, zz)
            outs[0][h * n + zz] = total[more:]
            if more:
                outs[1][h * n + zz] = total[:more]


def last_z_kernel(spot_ref, kept0, kept1, got0, got1, *refs):
    outs, total = refs[:-1], refs[-1]
    n = kept0.shape[1]
    for h, (kept, got) in enumerate(((kept0, got0), (kept1, got1))):
        for zz in range(n):
            total[h * n + zz] = half_sum(kept, got, zz)
    for s, out in enumerate(outs):
        out[...] = total[lax.rem(spot_ref[0] + s, 2 * n)]


def split_z_kernel(spot_ref, x_ref, y_ref, *outs):
    nz, _, cols = x_ref.shape
    for s, out in enumerate(outs):
        z = lax.rem(spot_ref[0] + s, nz)
        out[:, :cols] = x_ref[z]
        out[:, cols:] = y_ref[z]


class Net:
    def __init__(self):
        self.c = lax.axis_index("ctx")
        self.z = lax.axis_index("fsdp")
        self.nc = lax.axis_size("ctx")
        self.nz = lax.axis_size("fsdp")
        self.chips = self.nc // 2
        self.core = self.c % 2
        self.chip = self.c // 2

    def to_core(self, x):
        return lax.ppermute(x, "ctx", [(i, i ^ 1) for i in range(self.nc)])

    def to_chip(self, x, k):
        return lax.ppermute(x, "ctx", [(i, i ^ (2 * k)) for i in range(self.nc)])

    def along(self, x, s):
        n = self.nz
        return lax.ppermute(x, "fsdp", [(i, (i + s) % n) for i in range(n)])


    def gather_z(self, x):
        return lax.all_gather(x, "fsdp", axis=0)

    def gather_ctx(self, x):
        return lax.all_gather(x, "ctx", axis=0)

    def sum_z(self, x):
        return lax.psum_scatter(x, "fsdp", scatter_dimension=0, tiled=False)

    def spread_chips(self, x):
        return tuple(self.to_chip(x, k) for k in range(1, self.chips))

    def join_chips(self, x, got):
        out = jnp.zeros(x.shape[:1] + (self.chips,) + x.shape[1:], x.dtype)
        for k, part in enumerate((x,) + tuple(got)):
            out = lax.dynamic_update_index_in_dim(out, part, self.chip ^ k, 1)
        return out

    def join_cores(self, x, got):
        even = self.core == 0
        return jnp.stack([jnp.where(even, x, got), jnp.where(even, got, x)], axis=2)


    def swap_blocks(self, x):
        return (x[0],) + tuple(self.to_chip(x[k], k) for k in range(1, self.chips))


    def send_half(self, give, step):
        return tuple(self.to_chip(x, chip_bit(self.chips, step, h)) for h, x in enumerate(give))

    def first_half(self, keep, got, rows=None):
        nz, chips, each, cols = keep.shape
        more = 0 if rows is None else rows.shape[2]
        shape = jax.ShapeDtypeStruct((chips // 2, nz // 2, more + each, cols), BF)
        extra = () if rows is None else (rows,)
        out = vmem_call(
            functools.partial(first_kernel, more), [self.chip], (keep, got) + extra, [shape] * 4, "first_half"
        )
        return out[:2], out[2:]

    def next_half(self, kept, got, step):
        shape = kept[0].shape
        shape = jax.ShapeDtypeStruct((shape[0] // 2,) + shape[1:], BF)
        kernel = functools.partial(next_kernel, self.chips, step)
        out = vmem_call(kernel, [self.chip], tuple(kept) + tuple(got), [shape] * 4, "next_half")
        return out[:2], out[2:]

    def sum_chips(self, give, kept, first=None):
        steps = self.chips.bit_length() - 1
        got = self.send_half(give, 0) if first is None else first
        for step in range(1, steps):
            give, kept = self.next_half(kept, got, step)
            got = self.send_half(give, step)
        return tuple(kept) + tuple(got)

    def last_half(self, parts, more=0):
        nz, rows, cols = 2 * parts[0].shape[1], parts[0].shape[2], parts[0].shape[3]
        shapes = [jax.ShapeDtypeStruct((nz, rows - more, cols), BF)]
        if more:
            shapes.append(jax.ShapeDtypeStruct((nz, more, cols), BF))
        return vmem_call(functools.partial(last_kernel, more), [self.z], parts, shapes, "last_half")

    def last_z(self, parts):
        nz, rows, cols = 2 * parts[0].shape[1], parts[0].shape[2], parts[0].shape[3]
        shapes = [jax.ShapeDtypeStruct((rows, cols), BF)] * nz
        scratch = [pltpu.VMEM((nz, rows, cols), BF)]
        return vmem_call(last_z_kernel, [self.z], parts, shapes, "last_z", scratch)

    def split_z(self, x, y):
        nz, rows, cols = x.shape
        shapes = [jax.ShapeDtypeStruct((rows, cols + y.shape[2]), BF)] * nz
        return vmem_call(split_z_kernel, [self.z], (x, y), shapes, "split_z")

    def send_z(self, parts):
        return (parts[0],) + tuple(self.along(x, s) for s, x in enumerate(parts[1:], 1))

    def add(self, parts):
        total = parts[0].astype(F32)
        for part in parts[1:]:
            total = total + part.astype(F32)
        return total


def per_device(
    tokens,
    encoder,
    cotangent,
    buckets,
    pairing,
    norm_one,
    self_query,
    self_key,
    self_value,
    self_output,
    bias_table,
    norm_two,
    cross_query,
    cross_key,
    cross_value,
    cross_output,
    norm_three,
    ff_gate,
    ff_up,
    ff_down,
):
    net = Net()
    nc, nz, chips = net.nc, net.nz, net.chips
    mine = net.c
    shard = self_query.shape[0]
    width = self_query.shape[1]
    heads = bias_table.shape[1]
    pairs = width // LANES
    each = shard // nc
    half = shard // 2
    down_shard = ff_down.shape[0]
    wide = down_shard // chips
    down_half = wide // 2
    pack_rows = half + down_half

    def rows_of(w):
        return lax.dynamic_slice_in_dim(w, mine * each, each, 0)

    def flat(x):
        return x.reshape(-1, x.shape[-1])

    table_size = bias_table.size
    extra_width = LANES * math.ceil((4 + table_size) / LANES)
    small = jnp.stack([norm_one, norm_two, norm_three], axis=1)
    small = jnp.pad(rows_of(small), ((0, 0), (0, extra_width - 3)))
    line = jnp.pad(bias_table.reshape(1, -1), ((0, each - 1), (4, extra_width - 4 - table_size)))
    one = jnp.concatenate([rows_of(self_query), rows_of(self_key), rows_of(self_value), small + line], axis=1)
    rows_one = jnp.concatenate([tokens[0], encoder[0]], axis=0)
    incoming = cotangent[0]
    rows_chips = net.spread_chips(rows_one)
    one, rows_chips = fence(net.gather_z(one), rows_chips)
    one, self_output, cross_query, cross_key, cross_value, cross_output, ff_gate, ff_up, ff_down = fence(
        one, self_output, cross_query, cross_key, cross_value, cross_output, ff_gate, ff_up, ff_down
    )
    one_chips = net.spread_chips(one)
    two = jnp.concatenate(
        [rows_of(w) for w in (self_output, cross_query, cross_key, cross_value, cross_output)], axis=1
    )
    two = net.gather_z(two)
    one_chips, two = fence(one_chips, two)

    three = pick_ff(net.chip, net.core, ff_gate, ff_up, ff_down, chips)
    pack_cols = three.shape[1]
    two, three = fence(two, three)
    three = net.gather_z(three)
    rows_mine = jnp.stack((rows_one,) + rows_chips)
    one_mine = jnp.stack((one,) + one_chips)
    one_core = net.to_core(one_mine)
    rows_core = net.to_core(rows_mine)
    two_chips = net.spread_chips(two)
    one = assemble(net.chip, net.core, one_mine, one_core)

    w_q = one[:, :width]
    w_kv = one[:, width : 3 * width]
    extra = one[:, 3 * width :]
    gains = extra[:, :4].astype(F32).T
    g_one, g_two, g_three = gains[0], gains[1], gains[2]
    table = extra.reshape(nz, shard, extra_width)[:, 0, 4 : 4 + table_size].reshape(-1, heads)
    nbuckets = table.shape[0]

    count = tokens.shape[1]
    seq_len = count * nc
    tokens_all = jnp.concatenate([flat(rows_mine[:, :count]), flat(rows_core[:, :count])], axis=0)
    states_all = jnp.concatenate([flat(rows_mine[:, count:]), flat(rows_core[:, count:])], axis=0)
    member = mine ^ jnp.array([2 * k + r for r in range(2) for k in range(chips)], dtype=jnp.int32)
    match = member[:, None] == jnp.arange(nc, dtype=jnp.int32)[None, :]
    paired = jnp.sum(jnp.where(match, pairing[None, :], 0), axis=1)
    blocks = jnp.stack([paired, 2 * nc - 1 - paired], axis=1).reshape(-1).astype(jnp.int32)
    own = blocks[:2]

    picks = (buckets[::-1][None, :] == jnp.arange(nbuckets, dtype=jnp.int32)[:, None]).astype(BF)
    bias = jnp.dot(table.T, picks, preferred_element_type=F32).reshape(pairs, 2, seq_len)

    rows_in = tokens[0].astype(F32)
    a_one, norm_one_back = jax.vjp(norm_apply, rows_in, g_one)
    a_one = a_one.astype(BF)
    a_one_all = norm_apply(tokens_all.astype(F32), g_one).astype(BF)
    query = product(a_one, w_q).astype(BF)
    kv = product(a_one_all, w_kv).astype(BF)
    attended, self_probs = self_forward(blocks, own, query, kv, bias)
    attended, two_chips, three, incoming = fence(attended, two_chips, three, incoming)
    two_mine = jnp.stack((two,) + two_chips)
    two_core = net.to_core(two_mine)
    three_core = net.to_core(three)
    incoming_chips = net.spread_chips(incoming)
    incoming_rows = flat(jnp.stack((incoming,) + incoming_chips))
    two = assemble(net.chip, net.core, two_mine, two_core)
    w_o = two[:, :width]
    c_q = two[:, width : 2 * width]
    c_kv = two[:, 2 * width : 4 * width]
    c_o = two[:, 4 * width :]
    second = rows_in + product(attended, w_o)
    cross_kv = product(states_all, c_kv).astype(BF)
    a_two, norm_two_back = jax.vjp(norm_apply, second, g_two)
    a_two = a_two.astype(BF)
    cross_q = product(a_two, c_q).astype(BF)
    cross_o, cross_probs = cross_forward(cross_q, cross_kv)
    third = second + product(cross_o, c_o)
    a_three, norm_three_back = jax.vjp(norm_apply, third, g_three)
    a_three = a_three.astype(BF)

    a_three_chips = net.spread_chips(a_three)
    even = net.core == 0
    three_low, three_high = jnp.where(even, three, three_core), jnp.where(even, three_core, three)
    w_gu = jnp.stack([three_low[:, :half], three_high[:, :half]], axis=1)[..., : 2 * nz * wide].reshape(nz * shard, -1)
    w_down = flat(jnp.stack([three_low[:, half:], three_high[:, half:]], axis=1)[..., :width])
    w_gu, w_down, incoming_rows, a_three_chips = fence(w_gu, w_down, incoming_rows, a_three_chips)
    a_three_rows = flat(jnp.stack((a_three,) + a_three_chips))
    gate_up = product(a_three_rows, w_gu)
    units = nz * wide
    hidden, geglu_back = jax.vjp(
        lambda left, right: jax.nn.gelu(left, approximate=True) * right, gate_up[:, :units], gate_up[:, units:]
    )
    hidden = hidden.astype(BF)
    grad_gate, grad_up = geglu_back(through(incoming_rows, w_down))
    grad_gate_up = jnp.concatenate([grad_gate.astype(BF), grad_up.astype(BF)], axis=1)
    grad_three_part = through(grad_gate_up, w_gu).astype(BF).reshape(chips, count, width)
    result_part = product(hidden, w_down).astype(BF).reshape(chips, count, width)
    grad_three_terms = net.swap_blocks(grad_three_part)
    three_keep, three_give = split_grads(
        net.core,
        [(a_three_rows, grad_gate_up), (hidden, incoming_rows)],
        [(half, 0, 0), (down_half, half, 0)],
        1,
        pack_rows,
        pack_cols,
    )
    grad_three_terms, three_keep, three_give, result_part = fence(
        grad_three_terms, three_keep, three_give, result_part
    )
    three_core = net.to_core(three_give)
    result_terms = net.swap_blocks(result_part)

    part_three, grad_g_three = norm_three_back(net.add(grad_three_terms))
    grad_third = incoming.astype(F32) + part_three
    branch_two = grad_third.astype(BF)
    grad_cross_o = through(branch_two, c_o).astype(BF)
    dcq, dck, dcv = cross_backward(cross_q, cross_kv, grad_cross_o, cross_probs)
    dcq, dck, dcv, three_core, result_terms = fence(dcq, dck, dcv, three_core, result_terms)
    result = third + net.add(result_terms)
    three = net.sum_z(net.add((three_keep[:, 0], three_core[:, 0])).astype(BF))
    states_part = through(dck, c_kv[:, :width]) + through(dcv, c_kv[:, width:])
    part_two, grad_g_two = norm_two_back(through(dcq, c_q))
    grad_second = grad_third + part_two
    branch_one = grad_second.astype(BF)
    two_keep, two_give = split_grads(
        net.core,
        [
            (attended, branch_one),
            (a_two, dcq),
            (states_all, dck),
            (states_all, dcv),
            (cross_o, branch_two),
        ],
        [(each, 0, i * width) for i in range(5)],
        chips,
        each,
        5 * width,
    )
    grad_attended = through(branch_one, w_o).astype(BF)
    two_core = net.to_core(two_give)
    grad_attended, two_core = fence(grad_attended, two_core)
    two_give, two_kept = net.first_half(two_keep, two_core)
    two_got = net.send_half(two_give, 0)
    dq, dk, dv, bias_grad = self_backward(blocks, own, query, kv, grad_attended, self_probs)
    dq, dk, dv, bias_grad, two_got, three = fence(dq, dk, dv, bias_grad, two_got, three)
    three = net.gather_ctx(three)
    two_parts = net.sum_chips(two_give, two_kept, two_got)
    rows_part = (through(dk, w_kv[:, :width]) + through(dv, w_kv[:, width:])).astype(BF).reshape(2, chips, count, width)
    states_part = states_part.astype(BF).reshape(2, chips, -1, width)
    sent_keep, sent_give = (jnp.concatenate([rows_part[r], states_part[r]], axis=1) for r in range(2))
    sent_core = net.to_core(sent_give)
    one_keep, one_give = split_grads(
        net.core,
        [(a_one, dq), (a_one_all, dk), (a_one_all, dv)],
        [(each, 0, i * width) for i in range(3)],
        chips,
        each,
        3 * width,
    )
    one_core = net.to_core(one_give)
    table_grad = lax.dot_general(
        picks.astype(F32), bias_grad.reshape(heads, seq_len), LAST, precision=lax.Precision.HIGHEST
    )
    sent_core, one_core, two_parts, table_grad = fence(sent_core, one_core, two_parts, table_grad)
    sent = sent_keep.astype(F32) + sent_core.astype(F32)
    fold = one_keep.shape[-1] // width
    sent_rows = nz * math.ceil(sent.shape[1] / (fold * nz))
    sent = jnp.pad(sent, ((0, 0), (0, fold * sent_rows - sent.shape[1]), (0, 0)))
    sent = jnp.concatenate([sent[:, i * sent_rows : (i + 1) * sent_rows] for i in range(fold)], axis=2)
    sent = sent.astype(BF).reshape(chips, nz, sent_rows // nz, fold * width)
    one_give, one_kept = net.first_half(one_keep, one_core, sent)
    one_got = net.send_half(one_give, 0)
    two_terms = net.send_z(net.last_z(two_parts))
    one_parts = net.sum_chips(one_give, one_kept, one_got)
    one_parts, two_terms, three = fence(one_parts, two_terms, three)
    two = net.gather_ctx(net.add(two_terms).astype(BF))
    one_sum, own_part = net.last_half(one_parts, sent_rows // nz)
    own_part = own_part.astype(F32).reshape(sent_rows, fold * width)
    own_part = jnp.concatenate([own_part[:, i * width : (i + 1) * width] for i in range(fold)], axis=0)
    grad_a_one = through(dq, w_q) + own_part[:count]
    grad_states = own_part[count : count + encoder.shape[1]]
    part_one, grad_g_one = norm_one_back(grad_a_one)
    grad_rows = grad_second + part_one

    small_grad = jnp.pad(jnp.stack([grad_g_one, grad_g_two, grad_g_three]), ((0, 1), (0, 0)))
    small_grad = small_grad.reshape(4, nz, shard).swapaxes(0, 1).reshape(nz, -1)
    small_grad = jnp.concatenate([small_grad, table_grad.reshape(nz, table_size)], axis=1).astype(BF)
    small_size = small_grad.shape[1]
    small_cols = math.ceil(small_size / each)
    small_width = LANES * math.ceil(small_cols / LANES)
    small_grad = jnp.pad(small_grad, ((0, 0), (0, each * small_cols - small_size))).reshape(nz, each, small_cols)
    small_grad = jnp.pad(small_grad, ((0, 0), (0, 0), (0, small_width - small_cols)))
    one_terms = net.send_z(net.split_z(one_sum, small_grad))
    one = net.gather_ctx(net.add(one_terms).astype(BF))
    total_two = flat(two).astype(F32)
    total_one = flat(one[..., : 3 * width]).astype(F32)
    total_gate, total_up, total_down = place_ff(three, nz, half, wide, down_half, width)
    small_total = jnp.sum(one[..., 3 * width : 3 * width + small_cols].reshape(nc, -1).astype(F32), axis=0)
    gain_total = small_total[: 4 * shard].reshape(4, shard)
    table_total = small_total[4 * shard : 4 * shard + table_size].reshape(-1, heads)

    return (
        result.astype(BF)[None],
        grad_rows[None],
        grad_states[None],
        gain_total[0],
        total_one[:, :width],
        total_one[:, width : 2 * width],
        total_one[:, 2 * width : 3 * width],
        total_two[:, :width],
        table_total,
        gain_total[1],
        total_two[:, width : 2 * width],
        total_two[:, 2 * width : 3 * width],
        total_two[:, 3 * width : 4 * width],
        total_two[:, 4 * width :],
        gain_total[2],
        total_gate,
        total_up,
        total_down,
    )


def solution(mesh):
    rows = P("fsdp", "ctx", None)
    gain = P("fsdp")
    weight = P("fsdp", None)
    gradients = (
        gain, weight, weight, weight, weight, weight, gain, weight, weight, weight, weight, gain, weight, weight, weight
    )
    return jax.shard_map(
        per_device,
        mesh=mesh,
        in_specs=(rows, rows, rows, P(), P()) + gradients,
        out_specs=(rows, rows, rows) + gradients,
        check_vma=False,
    )
```

```python
import functools
import math

import jax
import jax.numpy as jnp
from jax import lax
from jax.experimental import pallas as pl
from jax.experimental.pallas import tpu as pltpu
from jax.sharding import PartitionSpec as P

BF = jnp.bfloat16
F32 = jnp.float32
LANES = 128
VMEM_LIMIT = 48 * 1024 * 1024
LAST = (((1,), (1,)), ((), ()))
FIRST = (((0,), (0,)), ((), ()))
PLAIN = (((1,), (0,)), ((), ()))


def norm_apply(v, g):
    return v * lax.rsqrt(jnp.mean(v * v, axis=-1, keepdims=True) + 1e-06) * g


def product(a, w):
    return jnp.dot(a, w, preferred_element_type=F32)


def through(grad, w):
    return lax.dot_general(grad, w, LAST, preferred_element_type=F32)


def weight_grad(a, grad):
    return lax.dot_general(a, grad, FIRST, preferred_element_type=F32)


def dot(a, b, dims):
    return lax.dot_general(a, b, dims, preferred_element_type=F32)


def two_heads(block):
    half = block.shape[1] // 2
    low = lax.broadcasted_iota(jnp.int32, block.shape, 1) < half
    zero = jnp.zeros_like(block)
    return jnp.concatenate([jnp.where(low, block, zero), jnp.where(low, zero, block)], axis=0)


def join_heads(rows):
    n = rows.shape[0] // 2
    low = lax.broadcasted_iota(jnp.int32, (n, rows.shape[1]), 1) < rows.shape[1] // 2
    return jnp.where(low, rows[:n], rows[n:])


def to_positions(blocks_ref, source, target, block):
    for i in range(source.shape[0] // block):
        spot = pl.multiple_of(blocks_ref[i] * block, block)
        target[pl.ds(spot, block), :] = source[i * block : (i + 1) * block, :]


def from_positions(blocks_ref, source, target, block):
    for i in range(target.shape[0] // block):
        spot = pl.multiple_of(blocks_ref[i] * block, block)
        target[i * block : (i + 1) * block, :] = source[pl.ds(spot, block), :].astype(target.dtype)


def sheared(line, block):
    sublane = lax.broadcasted_iota(jnp.int32, line.shape, 0)
    for bit in (1, 2, 4):
        line = jnp.where(sublane & bit != 0, pltpu.roll(line, bit, 1), line)
    return jnp.concatenate([line if i == 0 else pltpu.roll(line, i, 1) for i in range(0, block, 8)], axis=0)


def self_forward_kernel(blocks_ref, own_ref, q_ref, k_ref, v_ref, bias_ref, o_ref, p_ref, ks, vs):
    rows = q_ref.shape[0]
    block = rows // 2
    nkeys = k_ref.shape[0]
    to_positions(blocks_ref, k_ref, ks, block)
    to_positions(blocks_ref, v_ref, vs, block)
    scores = dot(two_heads(q_ref[...]), ks[...], LAST)
    column = lax.broadcasted_iota(jnp.int32, (block, nkeys), 1)
    row = lax.broadcasted_iota(jnp.int32, (block, nkeys), 0)
    for head in range(2):
        line = jnp.broadcast_to(bias_ref[0, head : head + 1, :], (8, nkeys))
        for part in range(2):
            start = own_ref[part] * block
            shear = sheared(pltpu.roll(line, start + 1, 1), block)
            at = head * rows + part * block
            s = jnp.where(column <= row + start, scores[at : at + block] + shear, -1e30)
            top = jnp.max(s, axis=-1, keepdims=True)
            expo = jnp.exp(s - top)
            total = jnp.sum(expo, axis=-1, keepdims=True)
            p_ref[0, at : at + block, :] = (expo / total).astype(BF)
    o_ref[...] = join_heads(dot(p_ref[0], vs[...], PLAIN)).astype(BF)


def cross_forward_kernel(q_ref, k_ref, v_ref, o_ref, p_ref):
    s = dot(two_heads(q_ref[...]), k_ref[...], LAST)
    top = jnp.max(s, axis=-1, keepdims=True)
    expo = jnp.exp(s - top)
    total = jnp.sum(expo, axis=-1, keepdims=True)
    p_ref[0] = (expo / total).astype(BF)
    o_ref[...] = join_heads(dot(p_ref[0], v_ref[...], PLAIN)).astype(BF)


def score_gradient(probs, dom, values):
    dp = dot(dom, values, LAST)
    p = probs.astype(F32)
    delta = jnp.sum(p * dp, axis=-1, keepdims=True)
    return (p * (dp - delta)).astype(BF)


def cross_backward_kernel(q_ref, k_ref, v_ref, do_ref, p_ref, dq_ref, dk_ref, dv_ref):
    dom = two_heads(do_ref[...])
    probs = p_ref[0]
    ds = score_gradient(probs, dom, v_ref[...])
    dq_ref[...] = join_heads(dot(ds, k_ref[...], PLAIN)).astype(BF)
    dk_ref[...] = dot(ds, two_heads(q_ref[...]), FIRST).astype(BF)
    dv_ref[...] = dot(probs, dom, FIRST).astype(BF)


def self_backward_kernel(
    blocks_ref, own_ref, q_ref, k_ref, v_ref, do_ref, p_ref, dq_ref, dk_ref, dv_ref, db_ref, ks, vs, acc
):
    rows = q_ref.shape[0]
    block = rows // 2
    nkeys = k_ref.shape[0]
    to_positions(blocks_ref, k_ref, ks, block)
    to_positions(blocks_ref, v_ref, vs, block)
    dom = two_heads(do_ref[...])
    probs = p_ref[0]
    ds = score_gradient(probs, dom, vs[...])
    dq_ref[...] = join_heads(dot(ds, ks[...], PLAIN)).astype(BF)
    acc[...] = dot(ds, two_heads(q_ref[...]), FIRST)
    from_positions(blocks_ref, acc, dk_ref, block)
    acc[...] = dot(probs, dom, FIRST)
    from_positions(blocks_ref, acc, dv_ref, block)
    for head in range(2):
        lines = None
        for part in range(2):
            at = head * rows + part * block
            x = ds[at : at + block].astype(F32)
            size = block
            while size > 1:
                size //= 2
                x = x[:size] + pltpu.roll(x[size:], nkeys - size, 1)
            x = pltpu.roll(jnp.broadcast_to(x, (8, nkeys)), nkeys - own_ref[part] * block - 1, 1)
            lines = x if lines is None else lines + x
        db_ref[0, head : head + 1, :] = lines[0:1]


def column_block(rows, offset):
    return pl.BlockSpec((rows, LANES), lambda i, *_: (0, offset + i))


def whole_block(a, b):
    return pl.BlockSpec((1, a, b), lambda i, *_: (i, 0, 0))


def params():
    return pltpu.CompilerParams(vmem_limit_bytes=VMEM_LIMIT)


def cost(rows, nkeys, width, weight):
    return pl.CostEstimate(
        flops=2 * rows * nkeys * width * weight,
        bytes_accessed=4 * rows * nkeys * (width // LANES),
        transcendentals=0,
    )


def self_forward(blocks, own, q, kv, bias):
    rows, width = q.shape
    nkeys = kv.shape[0]
    pairs = width // LANES
    return pl.pallas_call(
        self_forward_kernel,
        grid_spec=pltpu.PrefetchScalarGridSpec(
            num_scalar_prefetch=2,
            grid=(pairs,),
            in_specs=[
                column_block(rows, 0),
                column_block(nkeys, 0),
                column_block(nkeys, pairs),
                whole_block(2, nkeys),
            ],
            out_specs=[column_block(rows, 0), whole_block(2 * rows, nkeys)],
            scratch_shapes=[pltpu.VMEM((nkeys, LANES), BF), pltpu.VMEM((nkeys, LANES), BF)],
        ),
        out_shape=[
            jax.ShapeDtypeStruct((rows, width), BF),
            jax.ShapeDtypeStruct((pairs, 2 * rows, nkeys), BF),
        ],
        compiler_params=params(),
        cost_estimate=cost(rows, nkeys, width, 45),
        name="self_forward",
    )(blocks, own, q, kv, kv, bias)


def self_backward(blocks, own, q, kv, do, probs):
    rows, width = q.shape
    nkeys = kv.shape[0]
    pairs = width // LANES
    return pl.pallas_call(
        self_backward_kernel,
        grid_spec=pltpu.PrefetchScalarGridSpec(
            num_scalar_prefetch=2,
            grid=(pairs,),
            in_specs=[
                column_block(rows, 0),
                column_block(nkeys, 0),
                column_block(nkeys, pairs),
                column_block(rows, 0),
                whole_block(2 * rows, nkeys),
            ],
            out_specs=[
                column_block(rows, 0),
                column_block(nkeys, 0),
                column_block(nkeys, 0),
                whole_block(2, nkeys),
            ],
            scratch_shapes=[
                pltpu.VMEM((nkeys, LANES), BF),
                pltpu.VMEM((nkeys, LANES), BF),
                pltpu.VMEM((nkeys, LANES), F32),
            ],
        ),
        out_shape=[
            jax.ShapeDtypeStruct((rows, width), BF),
            jax.ShapeDtypeStruct((nkeys, width), BF),
            jax.ShapeDtypeStruct((nkeys, width), BF),
            jax.ShapeDtypeStruct((pairs, 2, nkeys), F32),
        ],
        compiler_params=params(),
        cost_estimate=pl.CostEstimate(flops=0, bytes_accessed=0, transcendentals=0),
        name="self_backward",
    )(blocks, own, q, kv, kv, do, probs)


def cross_forward(q, kv):
    rows, width = q.shape
    nkeys = kv.shape[0]
    pairs = width // LANES
    return pl.pallas_call(
        cross_forward_kernel,
        grid=(pairs,),
        in_specs=[column_block(rows, 0), column_block(nkeys, 0), column_block(nkeys, pairs)],
        out_specs=[column_block(rows, 0), whole_block(2 * rows, nkeys)],
        out_shape=[
            jax.ShapeDtypeStruct((rows, width), BF),
            jax.ShapeDtypeStruct((pairs, 2 * rows, nkeys), BF),
        ],
        compiler_params=params(),
        cost_estimate=cost(rows, nkeys, width, 40),
        name="cross_forward",
    )(q, kv, kv)


def cross_backward(q, kv, do, probs):
    rows, width = q.shape
    nkeys = kv.shape[0]
    pairs = width // LANES
    return pl.pallas_call(
        cross_backward_kernel,
        grid=(pairs,),
        in_specs=[
            column_block(rows, 0),
            column_block(nkeys, 0),
            column_block(nkeys, pairs),
            column_block(rows, 0),
            whole_block(2 * rows, nkeys),
        ],
        out_specs=[column_block(rows, 0), column_block(nkeys, 0), column_block(nkeys, 0)],
        out_shape=[
            jax.ShapeDtypeStruct((rows, width), BF),
            jax.ShapeDtypeStruct((nkeys, width), BF),
            jax.ShapeDtypeStruct((nkeys, width), BF),
        ],
        compiler_params=params(),
        cost_estimate=cost(rows, nkeys, width, 50),
        name="cross_backward",
    )(q, kv, kv, do, probs)


def split_kernel(products, nouts, core_ref, *refs):
    even = core_ref[0] == 0
    keep_ref, give_ref = refs[-2:]
    chips = keep_ref.shape[1]
    for i, (half, row, column) in enumerate(products):
        full = dot(refs[2 * i][...], refs[2 * i + 1][...], FIRST)
        cols = full.shape[1]
        for j in range(full.shape[0] // (2 * half)):
            low = full[2 * j * half : (2 * j + 1) * half]
            high = full[(2 * j + 1) * half : (2 * j + 2) * half]
            spot = (j // chips, j % chips, slice(row, row + half), slice(column, column + cols))
            keep_ref[spot] = jnp.where(even, low, high).astype(BF)
            give_ref[spot] = jnp.where(even, high, low).astype(BF)


def split_grads(core, pairs, places, chips, rows, cols):
    pieces = pairs[0][0].shape[1] // (2 * places[0][0])
    dims = (pieces // chips, chips, rows, cols)
    shape = jax.ShapeDtypeStruct(dims, BF)
    if any(half % 8 != 0 or row % 16 != 0 for half, row, _ in places):
        keep, give = [], []
        for (a, g), (half, row, column) in zip(pairs, places):
            full = weight_grad(a, g).astype(BF).reshape(pieces, 2, half, g.shape[1])
            spot = ((0, 0), (row, rows - row - half), (column, cols - column - g.shape[1]))
            keep.append(jnp.pad(lax.dynamic_index_in_dim(full, core, 1, keepdims=False), spot))
            give.append(jnp.pad(lax.dynamic_index_in_dim(full, 1 - core, 1, keepdims=False), spot))
        return sum(keep[1:], keep[0]).reshape(dims), sum(give[1:], give[0]).reshape(dims)
    vmem = pl.BlockSpec(memory_space=pltpu.VMEM)
    flat = [x for pair in pairs for x in pair]
    return pl.pallas_call(
        functools.partial(split_kernel, places, len(places)),
        in_specs=[pl.BlockSpec(memory_space=pltpu.SMEM)] + [vmem] * len(flat),
        out_specs=[vmem, vmem],
        out_shape=[shape, shape],
        compiler_params=params(),
        cost_estimate=pl.CostEstimate(flops=0, bytes_accessed=0, transcendentals=0),
        name="split_grads",
    )(core.reshape(1).astype(jnp.int32), *flat)


def pick_kernel(dims, spot_ref, gate_ref, up_ref, down_ref, out_ref):
    chips, nz, half, wide, down_half = dims
    width = down_ref.shape[1]
    rows = pl.ds(pl.multiple_of(spot_ref[1] * half, half), half)
    for i, ref in enumerate((gate_ref, up_ref)):
        for z in range(nz):
            source = pl.multiple_of((z * chips + spot_ref[0]) * wide, wide)
            target = (i * nz + z) * wide
            out_ref[:half, target : target + wide] = ref[rows, pl.ds(source, wide)]
    rows = pl.ds(pl.multiple_of((2 * spot_ref[0] + spot_ref[1]) * down_half, down_half), down_half)
    out_ref[half:, :width] = down_ref[rows, :]
    out_ref[half:, width:] = jnp.zeros((down_half, out_ref.shape[1] - width), out_ref.dtype)


def pick_ff(chip, core, gate, up, down, chips):
    half, wide = gate.shape[0] // 2, down.shape[0] // chips
    nz, down_half, width = gate.shape[1] // down.shape[0], wide // 2, down.shape[1]
    cols = 2 * nz * wide
    if wide % LANES != 0 or half % 16 != 0 or down_half % 16 != 0 or cols < width:
        pieces = []
        for w in (gate, up):
            w = lax.dynamic_slice_in_dim(w, core * half, half, 0)
            for z in range(nz):
                pieces.append(lax.dynamic_slice_in_dim(w, (z * chips + chip) * wide, wide, 1))
        pieces = jnp.concatenate(pieces, axis=1)
        down = lax.dynamic_slice_in_dim(down, (2 * chip + core) * down_half, down_half, 0)
        most = max(cols, width)
        return jnp.concatenate(
            [jnp.pad(pieces, ((0, 0), (0, most - cols))), jnp.pad(down, ((0, 0), (0, most - width)))], axis=0
        )
    vmem = pl.BlockSpec(memory_space=pltpu.VMEM)
    return pl.pallas_call(
        functools.partial(pick_kernel, (chips, nz, half, wide, down_half)),
        in_specs=[pl.BlockSpec(memory_space=pltpu.SMEM), vmem, vmem, vmem],
        out_specs=vmem,
        out_shape=jax.ShapeDtypeStruct((half + down_half, cols), gate.dtype),
        compiler_params=params(),
        cost_estimate=pl.CostEstimate(flops=0, bytes_accessed=6 * gate.size, transcendentals=0),
        name="pick_ff",
    )(jnp.stack([chip, core]).astype(jnp.int32), gate, up, down)


def assemble_kernel(spot_ref, mine_ref, other_ref, out_ref):
    chips, nz = mine_ref.shape[:2]
    for r, ref in enumerate((mine_ref, other_ref)):
        for k in range(chips):
            member = 2 * (spot_ref[0] ^ k) + (spot_ref[1] ^ r)
            for z in range(nz):
                out_ref[z, member] = ref[k, z]


def assemble(chip, core, mine, other):
    chips, nz, rows, cols = mine.shape
    vmem = pl.BlockSpec(memory_space=pltpu.VMEM)
    out = pl.pallas_call(
        assemble_kernel,
        in_specs=[pl.BlockSpec(memory_space=pltpu.SMEM), vmem, vmem],
        out_specs=vmem,
        out_shape=jax.ShapeDtypeStruct((nz, 2 * chips, rows, cols), mine.dtype),
        compiler_params=params(),
        cost_estimate=pl.CostEstimate(flops=0, bytes_accessed=8 * mine.size, transcendentals=0),
        name="assemble",
    )(jnp.stack([chip, core]).astype(jnp.int32), mine, other)
    return out.reshape(-1, cols)


def place_kernel(dims, parts_ref, gate_ref, up_ref, down_ref):
    chips, nz, half, wide, down_half = dims
    for member in range(2 * chips):
        chip, core = member // 2, member % 2
        for i, out in enumerate((gate_ref, up_ref)):
            for z in range(nz):
                source = (i * nz + z) * wide
                spot = (z * chips + chip) * wide
                out[core * half : (core + 1) * half, spot : spot + wide] = parts_ref[
                    member, :half, source : source + wide
                ].astype(F32)
        down_ref[member * down_half : (member + 1) * down_half, :] = parts_ref[
            member, half : half + down_half, : down_ref.shape[1]
        ].astype(F32)


def place_ff(parts, nz, half, wide, down_half, width):
    members = parts.shape[0]
    chips = members // 2
    hidden = nz * chips * wide
    if wide % LANES != 0 or half % 16 != 0 or down_half % 16 != 0:
        both = parts[:, :half, : 2 * nz * wide].astype(F32).reshape(chips, 2, half, 2, nz, wide)
        both = both.transpose(3, 1, 2, 4, 0, 5).reshape(2, 2 * half, hidden)
        return both[0], both[1], parts[:, half:, :width].astype(F32).reshape(-1, width)
    vmem = pl.BlockSpec(memory_space=pltpu.VMEM)
    return pl.pallas_call(
        functools.partial(place_kernel, (chips, nz, half, wide, down_half)),
        in_specs=[vmem],
        out_specs=[vmem] * 3,
        out_shape=[
            jax.ShapeDtypeStruct((2 * half, hidden), F32),
            jax.ShapeDtypeStruct((2 * half, hidden), F32),
            jax.ShapeDtypeStruct((members * down_half, width), F32),
        ],
        compiler_params=params(),
        cost_estimate=pl.CostEstimate(flops=0, bytes_accessed=6 * parts.size, transcendentals=0),
        name="place_ff",
    )(parts)


def fence(*arrays):
    return lax.optimization_barrier(arrays)


def vmem_call(kernel, scalars, arrays, shapes, name, scratch=()):
    vmem = pl.BlockSpec(memory_space=pltpu.VMEM)
    return pl.pallas_call(
        kernel,
        in_specs=[pl.BlockSpec(memory_space=pltpu.SMEM)] + [vmem] * len(arrays),
        out_specs=[vmem] * len(shapes),
        out_shape=shapes,
        scratch_shapes=list(scratch),
        compiler_params=params(),
        cost_estimate=pl.CostEstimate(flops=0, bytes_accessed=2 * sum(x.size for x in arrays), transcendentals=0),
        name=name,
    )(jnp.stack(scalars).astype(jnp.int32), *arrays)


def chip_bit(chips, step, h):
    return 1 << ((step + h) % (chips.bit_length() - 1))


def held_before(chips, step, h):
    spots = list(range(chips))
    for i in range(step):
        spots = [k for k in spots if not k & chip_bit(chips, i, h)]
    return spots


def first_kernel(more, spot_ref, keep_ref, got_ref, *refs):
    rows_ref = refs[0] if more else None
    outs = refs[-4:]
    nz, chips = keep_ref.shape[:2]
    for h in range(2):
        b = chip_bit(chips, 0, h)
        stays = [k for k in range(chips) if not k & b]
        for k in range(chips):
            out = outs[h] if k & b else outs[2 + h]
            i = stays.index(k & ~b)
            for zz in range(nz // 2):
                z = h * (nz // 2) + zz
                chip = spot_ref[0] ^ k
                total = keep_ref[z, chip].astype(F32) + got_ref[z, chip].astype(F32)
                out[i, zz, more:, :] = total.astype(BF)
                if more:
                    out[i, zz, :more, :] = rows_ref[k, z]


def next_kernel(chips, step, spot_ref, kept0, kept1, got0, got1, give0, give1, keep0, keep1):
    for h, (kept, got, give, keep) in enumerate(((kept0, got0, give0, keep0), (kept1, got1, give1, keep1))):
        b = chip_bit(chips, step, h)
        spots = held_before(chips, step, h)
        stays = [k for k in spots if not k & b]
        for i, k in enumerate(spots):
            total = (kept[i].astype(F32) + got[i].astype(F32)).astype(BF)
            if k & b:
                give[stays.index(k & ~b)] = total
            else:
                keep[stays.index(k)] = total


def half_sum(kept, got, z):
    return (kept[0, z].astype(F32) + got[0, z].astype(F32)).astype(BF)


def last_kernel(more, spot_ref, kept0, kept1, got0, got1, *outs):
    n = kept0.shape[1]
    for h, (kept, got) in enumerate(((kept0, got0), (kept1, got1))):
        for zz in range(n):
            total = half_sum(kept, got, zz)
            outs[0][h * n + zz] = total[more:]
            if more:
                outs[1][h * n + zz] = total[:more]


def last_z_kernel(spot_ref, kept0, kept1, got0, got1, *refs):
    outs, total = refs[:-1], refs[-1]
    n = kept0.shape[1]
    for h, (kept, got) in enumerate(((kept0, got0), (kept1, got1))):
        for zz in range(n):
            total[h * n + zz] = half_sum(kept, got, zz)
    for s, out in enumerate(outs):
        out[...] = total[lax.rem(spot_ref[0] + s, 2 * n)]


def split_z_kernel(spot_ref, x_ref, y_ref, *outs):
    nz, _, cols = x_ref.shape
    for s, out in enumerate(outs):
        z = lax.rem(spot_ref[0] + s, nz)
        out[:, :cols] = x_ref[z]
        out[:, cols:] = y_ref[z]


class Net:
    def __init__(self):
        self.c = lax.axis_index("ctx")
        self.z = lax.axis_index("fsdp")
        self.nc = lax.axis_size("ctx")
        self.nz = lax.axis_size("fsdp")
        self.chips = self.nc // 2
        self.core = self.c % 2
        self.chip = self.c // 2

    def to_core(self, x):
        return lax.ppermute(x, "ctx", [(i, i ^ 1) for i in range(self.nc)])

    def to_chip(self, x, k):
        return lax.ppermute(x, "ctx", [(i, i ^ (2 * k)) for i in range(self.nc)])

    def along(self, x, s):
        n = self.nz
        return lax.ppermute(x, "fsdp", [(i, (i + s) % n) for i in range(n)])


    def gather_z(self, x):
        return lax.all_gather(x, "fsdp", axis=0)

    def gather_ctx(self, x):
        return lax.all_gather(x, "ctx", axis=0)

    def sum_z(self, x):
        return lax.psum_scatter(x, "fsdp", scatter_dimension=0, tiled=False)

    def spread_chips(self, x):
        return tuple(self.to_chip(x, k) for k in range(1, self.chips))

    def join_chips(self, x, got):
        out = jnp.zeros(x.shape[:1] + (self.chips,) + x.shape[1:], x.dtype)
        for k, part in enumerate((x,) + tuple(got)):
            out = lax.dynamic_update_index_in_dim(out, part, self.chip ^ k, 1)
        return out

    def join_cores(self, x, got):
        even = self.core == 0
        return jnp.stack([jnp.where(even, x, got), jnp.where(even, got, x)], axis=2)


    def swap_blocks(self, x):
        return (x[0],) + tuple(self.to_chip(x[k], k) for k in range(1, self.chips))


    def send_half(self, give, step):
        return tuple(self.to_chip(x, chip_bit(self.chips, step, h)) for h, x in enumerate(give))

    def first_half(self, keep, got, rows=None):
        nz, chips, each, cols = keep.shape
        more = 0 if rows is None else rows.shape[2]
        shape = jax.ShapeDtypeStruct((chips // 2, nz // 2, more + each, cols), BF)
        extra = () if rows is None else (rows,)
        out = vmem_call(
            functools.partial(first_kernel, more), [self.chip], (keep, got) + extra, [shape] * 4, "first_half"
        )
        return out[:2], out[2:]

    def next_half(self, kept, got, step):
        shape = kept[0].shape
        shape = jax.ShapeDtypeStruct((shape[0] // 2,) + shape[1:], BF)
        kernel = functools.partial(next_kernel, self.chips, step)
        out = vmem_call(kernel, [self.chip], tuple(kept) + tuple(got), [shape] * 4, "next_half")
        return out[:2], out[2:]

    def sum_chips(self, give, kept, first=None):
        steps = self.chips.bit_length() - 1
        got = self.send_half(give, 0) if first is None else first
        for step in range(1, steps):
            give, kept = self.next_half(kept, got, step)
            got = self.send_half(give, step)
        return tuple(kept) + tuple(got)

    def last_half(self, parts, more=0):
        nz, rows, cols = 2 * parts[0].shape[1], parts[0].shape[2], parts[0].shape[3]
        shapes = [jax.ShapeDtypeStruct((nz, rows - more, cols), BF)]
        if more:
            shapes.append(jax.ShapeDtypeStruct((nz, more, cols), BF))
        return vmem_call(functools.partial(last_kernel, more), [self.z], parts, shapes, "last_half")

    def last_z(self, parts):
        nz, rows, cols = 2 * parts[0].shape[1], parts[0].shape[2], parts[0].shape[3]
        shapes = [jax.ShapeDtypeStruct((rows, cols), BF)] * nz
        scratch = [pltpu.VMEM((nz, rows, cols), BF)]
        return vmem_call(last_z_kernel, [self.z], parts, shapes, "last_z", scratch)

    def split_z(self, x, y):
        nz, rows, cols = x.shape
        shapes = [jax.ShapeDtypeStruct((rows, cols + y.shape[2]), BF)] * nz
        return vmem_call(split_z_kernel, [self.z], (x, y), shapes, "split_z")

    def send_z(self, parts):
        return (parts[0],) + tuple(self.along(x, s) for s, x in enumerate(parts[1:], 1))

    def add(self, parts):
        total = parts[0].astype(F32)
        for part in parts[1:]:
            total = total + part.astype(F32)
        return total


def per_device(
    tokens,
    encoder,
    cotangent,
    buckets,
    pairing,
    norm_one,
    self_query,
    self_key,
    self_value,
    self_output,
    bias_table,
    norm_two,
    cross_query,
    cross_key,
    cross_value,
    cross_output,
    norm_three,
    ff_gate,
    ff_up,
    ff_down,
):
    net = Net()
    nc, nz, chips = net.nc, net.nz, net.chips
    mine = net.c
    shard = self_query.shape[0]
    width = self_query.shape[1]
    heads = bias_table.shape[1]
    pairs = width // LANES
    each = shard // nc
    half = shard // 2
    down_shard = ff_down.shape[0]
    wide = down_shard // chips
    down_half = wide // 2
    pack_rows = half + down_half

    def rows_of(w):
        return lax.dynamic_slice_in_dim(w, mine * each, each, 0)

    def flat(x):
        return x.reshape(-1, x.shape[-1])

    table_size = bias_table.size
    extra_width = LANES * math.ceil((4 + table_size) / LANES)
    small = jnp.stack([norm_one, norm_two, norm_three], axis=1)
    small = jnp.pad(rows_of(small), ((0, 0), (0, extra_width - 3)))
    line = jnp.pad(bias_table.reshape(1, -1), ((0, each - 1), (4, extra_width - 4 - table_size)))
    one = jnp.concatenate([rows_of(self_query), rows_of(self_key), rows_of(self_value), small + line], axis=1)
    rows_one = jnp.concatenate([tokens[0], encoder[0]], axis=0)
    incoming = cotangent[0]
    rows_chips = net.spread_chips(rows_one)
    one, rows_chips = fence(net.gather_z(one), rows_chips)
    one, self_output, cross_query, cross_key, cross_value, cross_output, ff_gate, ff_up, ff_down = fence(
        one, self_output, cross_query, cross_key, cross_value, cross_output, ff_gate, ff_up, ff_down
    )
    one_chips = net.spread_chips(one)
    two = jnp.concatenate(
        [rows_of(w) for w in (self_output, cross_query, cross_key, cross_value, cross_output)], axis=1
    )
    two = net.gather_z(two)
    three = pick_ff(net.chip, net.core, ff_gate, ff_up, ff_down, chips)
    pack_cols = three.shape[1]
    one_chips, two, three = fence(one_chips, two, three)
    three = net.gather_z(three)

    one_mine = jnp.stack((one,) + one_chips)
    one_core = net.to_core(one_mine)
    two_chips = net.spread_chips(two)
    one_core, rows_chips = fence(one_core, rows_chips)
    rows_mine = jnp.stack((rows_one,) + rows_chips)
    rows_core = net.to_core(rows_mine)
    one = assemble(net.chip, net.core, one_mine, one_core)

    w_q = one[:, :width]
    w_kv = one[:, width : 3 * width]
    extra = one[:, 3 * width :]
    gains = extra[:, :4].astype(F32).T
    g_one, g_two, g_three = gains[0], gains[1], gains[2]
    table = extra.reshape(nz, shard, extra_width)[:, 0, 4 : 4 + table_size].reshape(-1, heads)
    nbuckets = table.shape[0]

    count = tokens.shape[1]
    seq_len = count * nc
    tokens_all = jnp.concatenate([flat(rows_mine[:, :count]), flat(rows_core[:, :count])], axis=0)
    states_all = jnp.concatenate([flat(rows_mine[:, count:]), flat(rows_core[:, count:])], axis=0)
    member = mine ^ jnp.array([2 * k + r for r in range(2) for k in range(chips)], dtype=jnp.int32)
    match = member[:, None] == jnp.arange(nc, dtype=jnp.int32)[None, :]
    paired = jnp.sum(jnp.where(match, pairing[None, :], 0), axis=1)
    blocks = jnp.stack([paired, 2 * nc - 1 - paired], axis=1).reshape(-1).astype(jnp.int32)
    own = blocks[:2]

    picks = (buckets[::-1][None, :] == jnp.arange(nbuckets, dtype=jnp.int32)[:, None]).astype(BF)
    bias = jnp.dot(table.T, picks, preferred_element_type=F32).reshape(pairs, 2, seq_len)

    rows_in = tokens[0].astype(F32)
    a_one, norm_one_back = jax.vjp(norm_apply, rows_in, g_one)
    a_one = a_one.astype(BF)
    a_one_all = norm_apply(tokens_all.astype(F32), g_one).astype(BF)
    query = product(a_one, w_q).astype(BF)
    kv = product(a_one_all, w_kv).astype(BF)
    attended, self_probs = self_forward(blocks, own, query, kv, bias)
    attended, two_chips, incoming, three = fence(attended, two_chips, incoming, three)
    two_mine = jnp.stack((two,) + two_chips)
    two_core = net.to_core(two_mine)
    incoming_chips = net.spread_chips(incoming)
    incoming_rows = flat(jnp.stack((incoming,) + incoming_chips))
    two = assemble(net.chip, net.core, two_mine, two_core)
    w_o = two[:, :width]
    second = rows_in + product(attended, w_o)
    two, second, three = fence(two, second, three)
    three_core = net.to_core(three)
    c_q = two[:, width : 2 * width]
    c_kv = two[:, 2 * width : 4 * width]
    c_o = two[:, 4 * width :]
    cross_kv = product(states_all, c_kv).astype(BF)
    a_two, norm_two_back = jax.vjp(norm_apply, second, g_two)
    a_two = a_two.astype(BF)
    cross_q = product(a_two, c_q).astype(BF)
    cross_o, cross_probs = cross_forward(cross_q, cross_kv)
    third = second + product(cross_o, c_o)
    a_three, norm_three_back = jax.vjp(norm_apply, third, g_three)
    a_three = a_three.astype(BF)

    a_three_chips = net.spread_chips(a_three)
    even = net.core == 0
    three_low, three_high = jnp.where(even, three, three_core), jnp.where(even, three_core, three)
    w_gu = jnp.stack([three_low[:, :half], three_high[:, :half]], axis=1)[..., : 2 * nz * wide].reshape(nz * shard, -1)
    w_down = flat(jnp.stack([three_low[:, half:], three_high[:, half:]], axis=1)[..., :width])
    w_gu, w_down, incoming_rows, a_three_chips = fence(w_gu, w_down, incoming_rows, a_three_chips)
    a_three_rows = flat(jnp.stack((a_three,) + a_three_chips))
    gate_up = product(a_three_rows, w_gu)
    units = nz * wide
    hidden, geglu_back = jax.vjp(
        lambda left, right: jax.nn.gelu(left, approximate=True) * right, gate_up[:, :units], gate_up[:, units:]
    )
    hidden = hidden.astype(BF)
    grad_gate, grad_up = geglu_back(through(incoming_rows, w_down))
    grad_gate_up = jnp.concatenate([grad_gate.astype(BF), grad_up.astype(BF)], axis=1)
    grad_three_part = through(grad_gate_up, w_gu).astype(BF).reshape(chips, count, width)
    result_part = product(hidden, w_down).astype(BF).reshape(chips, count, width)
    grad_three_terms = net.swap_blocks(grad_three_part)
    three_keep, three_give = split_grads(
        net.core,
        [(a_three_rows, grad_gate_up), (hidden, incoming_rows)],
        [(half, 0, 0), (down_half, half, 0)],
        1,
        pack_rows,
        pack_cols,
    )
    grad_three_terms, three_keep, three_give, result_part = fence(
        grad_three_terms, three_keep, three_give, result_part
    )
    three_core = net.to_core(three_give)
    result_terms = net.swap_blocks(result_part)

    part_three, grad_g_three = norm_three_back(net.add(grad_three_terms))
    grad_third = incoming.astype(F32) + part_three
    branch_two = grad_third.astype(BF)
    grad_cross_o = through(branch_two, c_o).astype(BF)
    grad_cross_o, three_core = fence(grad_cross_o, three_core)
    dcq, dck, dcv = cross_backward(cross_q, cross_kv, grad_cross_o, cross_probs)
    dcq, result_terms = fence(dcq, result_terms)
    result = third + net.add(result_terms)
    three = net.sum_z(net.add((three_keep[:, 0], three_core[:, 0])).astype(BF))
    part_two, grad_g_two = norm_two_back(through(dcq, c_q))
    grad_second = grad_third + part_two
    branch_one = grad_second.astype(BF)
    two_keep, two_give = split_grads(
        net.core,
        [
            (attended, branch_one),
            (a_two, dcq),
            (states_all, dck),
            (states_all, dcv),
            (cross_o, branch_two),
        ],
        [(each, 0, i * width) for i in range(5)],
        chips,
        each,
        5 * width,
    )
    grad_attended = through(branch_one, w_o).astype(BF)
    two_core = net.to_core(two_give)
    grad_attended, two_core = fence(grad_attended, two_core)
    two_give, two_kept = net.first_half(two_keep, two_core)
    two_got = net.send_half(two_give, 0)
    dq, dk, dv, bias_grad = self_backward(blocks, own, query, kv, grad_attended, self_probs)
    dq, dk, dv, bias_grad, two_got, dck, dcv = fence(dq, dk, dv, bias_grad, two_got, dck, dcv)
    steps = chips.bit_length() - 1
    for step in range(1, steps):
        two_give, two_kept = net.next_half(two_kept, two_got, step)
        two_give, two_kept, dk, dv, dck, dcv = fence(two_give, two_kept, dk, dv, dck, dcv)
        two_got = net.send_half(two_give, step)
    rows_part = (through(dk, w_kv[:, :width]) + through(dv, w_kv[:, width:])).astype(BF).reshape(2, chips, count, width)
    states_part = through(dck, c_kv[:, :width]) + through(dcv, c_kv[:, width:])
    states_part = states_part.astype(BF).reshape(2, chips, -1, width)
    sent_keep, sent_give = (jnp.concatenate([rows_part[r], states_part[r]], axis=1) for r in range(2))
    sent_keep, sent_give, two_got, three = fence(sent_keep, sent_give, two_got, three)
    three = net.gather_ctx(three)
    sent_core = net.to_core(sent_give)
    one_keep, one_give = split_grads(
        net.core,
        [(a_one, dq), (a_one_all, dk), (a_one_all, dv)],
        [(each, 0, i * width) for i in range(3)],
        chips,
        each,
        3 * width,
    )
    sent_core, one_keep, one_give = fence(sent_core, one_keep, one_give)
    sent_terms = net.swap_blocks((sent_keep.astype(F32) + sent_core.astype(F32)).astype(BF))
    one_core = net.to_core(one_give)
    table_grad = lax.dot_general(
        picks.astype(F32), bias_grad.reshape(heads, seq_len), LAST, precision=lax.Precision.HIGHEST
    )
    one_core, table_grad = fence(one_core, table_grad)
    one_give, one_kept = net.first_half(one_keep, one_core)
    one_got = net.send_half(one_give, 0)
    sent_terms, one_kept, two_got = fence(sent_terms, one_kept, two_got)
    two_terms = net.send_z(net.last_z(tuple(two_kept) + tuple(two_got)))
    own_part = net.add(sent_terms)
    grad_a_one = through(dq, w_q) + own_part[:count]
    grad_states = own_part[count:]
    part_one, grad_g_one = norm_one_back(grad_a_one)
    grad_rows = grad_second + part_one

    small_grad = jnp.pad(jnp.stack([grad_g_one, grad_g_two, grad_g_three]), ((0, 1), (0, 0)))
    small_grad = small_grad.reshape(4, nz, shard).swapaxes(0, 1).reshape(nz, -1)
    small_grad = jnp.concatenate([small_grad, table_grad.reshape(nz, table_size)], axis=1).astype(BF)
    small_size = small_grad.shape[1]
    small_cols = math.ceil(small_size / each)
    small_width = LANES * math.ceil(small_cols / LANES)
    small_grad = jnp.pad(small_grad, ((0, 0), (0, each * small_cols - small_size))).reshape(nz, each, small_cols)
    small_grad = jnp.pad(small_grad, ((0, 0), (0, 0), (0, small_width - small_cols)))
    one_got, small_grad = fence(one_got, small_grad)
    one_parts = net.sum_chips(one_give, one_kept, one_got)
    one_parts, two_terms, three = fence(one_parts, two_terms, three)
    two = net.gather_ctx(net.add(two_terms).astype(BF))
    one_sum = net.last_half(one_parts)[0]
    one_terms = net.send_z(net.split_z(one_sum, small_grad))
    one = net.gather_ctx(net.add(one_terms).astype(BF))
    total_two = flat(two).astype(F32)
    total_one = flat(one[..., : 3 * width]).astype(F32)
    total_gate, total_up, total_down = place_ff(three, nz, half, wide, down_half, width)
    small_total = jnp.sum(one[..., 3 * width : 3 * width + small_cols].reshape(nc, -1).astype(F32), axis=0)
    gain_total = small_total[: 4 * shard].reshape(4, shard)
    table_total = small_total[4 * shard : 4 * shard + table_size].reshape(-1, heads)

    return (
        result.astype(BF)[None],
        grad_rows[None],
        grad_states[None],
        gain_total[0],
        total_one[:, :width],
        total_one[:, width : 2 * width],
        total_one[:, 2 * width : 3 * width],
        total_two[:, :width],
        table_total,
        gain_total[1],
        total_two[:, width : 2 * width],
        total_two[:, 2 * width : 3 * width],
        total_two[:, 3 * width : 4 * width],
        total_two[:, 4 * width :],
        gain_total[2],
        total_gate,
        total_up,
        total_down,
    )


def solution(mesh):
    rows = P("fsdp", "ctx", None)
    gain = P("fsdp")
    weight = P("fsdp", None)
    gradients = (
        gain, weight, weight, weight, weight, weight, gain, weight, weight, weight, weight, gain, weight, weight, weight
    )
    return jax.shard_map(
        per_device,
        mesh=mesh,
        in_specs=(rows, rows, rows, P(), P()) + gradients,
        out_specs=(rows, rows, rows) + gradients,
        check_vma=False,
    )
```

```python
import functools
import math

import jax
import jax.numpy as jnp
from jax import lax
from jax.experimental import pallas as pl
from jax.experimental.pallas import tpu as pltpu
from jax.sharding import PartitionSpec as P

BF = jnp.bfloat16
F32 = jnp.float32
LANES = 128
VMEM_LIMIT = 48 * 1024 * 1024
LAST = (((1,), (1,)), ((), ()))
FIRST = (((0,), (0,)), ((), ()))
PLAIN = (((1,), (0,)), ((), ()))


def norm_apply(v, g):
    return v * lax.rsqrt(jnp.mean(v * v, axis=-1, keepdims=True) + 1e-06) * g


def product(a, w):
    return jnp.dot(a, w, preferred_element_type=F32)


def through(grad, w):
    return lax.dot_general(grad, w, LAST, preferred_element_type=F32)


def weight_grad(a, grad):
    return lax.dot_general(a, grad, FIRST, preferred_element_type=F32)


def dot(a, b, dims):
    return lax.dot_general(a, b, dims, preferred_element_type=F32)


def two_heads(block):
    half = block.shape[1] // 2
    low = lax.broadcasted_iota(jnp.int32, block.shape, 1) < half
    zero = jnp.zeros_like(block)
    return jnp.concatenate([jnp.where(low, block, zero), jnp.where(low, zero, block)], axis=0)


def join_heads(rows):
    n = rows.shape[0] // 2
    low = lax.broadcasted_iota(jnp.int32, (n, rows.shape[1]), 1) < rows.shape[1] // 2
    return jnp.where(low, rows[:n], rows[n:])


def to_positions(blocks_ref, source, target, block):
    for i in range(source.shape[0] // block):
        spot = pl.multiple_of(blocks_ref[i] * block, block)
        target[pl.ds(spot, block), :] = source[i * block : (i + 1) * block, :]


def from_positions(blocks_ref, source, target, block):
    for i in range(target.shape[0] // block):
        spot = pl.multiple_of(blocks_ref[i] * block, block)
        target[i * block : (i + 1) * block, :] = source[pl.ds(spot, block), :].astype(target.dtype)


def sheared(line, block):
    sublane = lax.broadcasted_iota(jnp.int32, line.shape, 0)
    for bit in (1, 2, 4):
        line = jnp.where(sublane & bit != 0, pltpu.roll(line, bit, 1), line)
    return jnp.concatenate([line if i == 0 else pltpu.roll(line, i, 1) for i in range(0, block, 8)], axis=0)


def self_forward_kernel(blocks_ref, own_ref, q_ref, k_ref, v_ref, bias_ref, o_ref, p_ref, ks, vs):
    rows = q_ref.shape[0]
    block = rows // 2
    nkeys = k_ref.shape[0]
    to_positions(blocks_ref, k_ref, ks, block)
    to_positions(blocks_ref, v_ref, vs, block)
    scores = dot(two_heads(q_ref[...]), ks[...], LAST)
    column = lax.broadcasted_iota(jnp.int32, (block, nkeys), 1)
    row = lax.broadcasted_iota(jnp.int32, (block, nkeys), 0)
    for head in range(2):
        line = jnp.broadcast_to(bias_ref[0, head : head + 1, :], (8, nkeys))
        for part in range(2):
            start = own_ref[part] * block
            shear = sheared(pltpu.roll(line, start + 1, 1), block)
            at = head * rows + part * block
            s = jnp.where(column <= row + start, scores[at : at + block] + shear, -1e30)
            top = jnp.max(s, axis=-1, keepdims=True)
            expo = jnp.exp(s - top)
            total = jnp.sum(expo, axis=-1, keepdims=True)
            p_ref[0, at : at + block, :] = (expo / total).astype(BF)
    o_ref[...] = join_heads(dot(p_ref[0], vs[...], PLAIN)).astype(BF)


def cross_forward_kernel(q_ref, k_ref, v_ref, o_ref, p_ref):
    s = dot(two_heads(q_ref[...]), k_ref[...], LAST)
    top = jnp.max(s, axis=-1, keepdims=True)
    expo = jnp.exp(s - top)
    total = jnp.sum(expo, axis=-1, keepdims=True)
    p_ref[0] = (expo / total).astype(BF)
    o_ref[...] = join_heads(dot(p_ref[0], v_ref[...], PLAIN)).astype(BF)


def score_gradient(probs, dom, values):
    dp = dot(dom, values, LAST)
    p = probs.astype(F32)
    delta = jnp.sum(p * dp, axis=-1, keepdims=True)
    return (p * (dp - delta)).astype(BF)


def cross_backward_kernel(q_ref, k_ref, v_ref, do_ref, p_ref, dq_ref, dk_ref, dv_ref):
    dom = two_heads(do_ref[...])
    probs = p_ref[0]
    ds = score_gradient(probs, dom, v_ref[...])
    dq_ref[...] = join_heads(dot(ds, k_ref[...], PLAIN)).astype(BF)
    dk_ref[...] = dot(ds, two_heads(q_ref[...]), FIRST).astype(BF)
    dv_ref[...] = dot(probs, dom, FIRST).astype(BF)


def self_backward_kernel(
    blocks_ref, own_ref, q_ref, k_ref, v_ref, do_ref, p_ref, dq_ref, dk_ref, dv_ref, db_ref, ks, vs, acc
):
    rows = q_ref.shape[0]
    block = rows // 2
    nkeys = k_ref.shape[0]
    to_positions(blocks_ref, k_ref, ks, block)
    to_positions(blocks_ref, v_ref, vs, block)
    dom = two_heads(do_ref[...])
    probs = p_ref[0]
    ds = score_gradient(probs, dom, vs[...])
    dq_ref[...] = join_heads(dot(ds, ks[...], PLAIN)).astype(BF)
    acc[...] = dot(ds, two_heads(q_ref[...]), FIRST)
    from_positions(blocks_ref, acc, dk_ref, block)
    acc[...] = dot(probs, dom, FIRST)
    from_positions(blocks_ref, acc, dv_ref, block)
    for head in range(2):
        lines = None
        for part in range(2):
            at = head * rows + part * block
            x = ds[at : at + block].astype(F32)
            size = block
            while size > 1:
                size //= 2
                x = x[:size] + pltpu.roll(x[size:], nkeys - size, 1)
            x = pltpu.roll(jnp.broadcast_to(x, (8, nkeys)), nkeys - own_ref[part] * block - 1, 1)
            lines = x if lines is None else lines + x
        db_ref[0, head : head + 1, :] = lines[0:1]


def column_block(rows, offset):
    return pl.BlockSpec((rows, LANES), lambda i, *_: (0, offset + i))


def whole_block(a, b):
    return pl.BlockSpec((1, a, b), lambda i, *_: (i, 0, 0))


def params():
    return pltpu.CompilerParams(vmem_limit_bytes=VMEM_LIMIT)


def cost(rows, nkeys, width, weight):
    return pl.CostEstimate(
        flops=2 * rows * nkeys * width * weight,
        bytes_accessed=4 * rows * nkeys * (width // LANES),
        transcendentals=0,
    )


def self_forward(blocks, own, q, kv, bias):
    rows, width = q.shape
    nkeys = kv.shape[0]
    pairs = width // LANES
    return pl.pallas_call(
        self_forward_kernel,
        grid_spec=pltpu.PrefetchScalarGridSpec(
            num_scalar_prefetch=2,
            grid=(pairs,),
            in_specs=[
                column_block(rows, 0),
                column_block(nkeys, 0),
                column_block(nkeys, pairs),
                whole_block(2, nkeys),
            ],
            out_specs=[column_block(rows, 0), whole_block(2 * rows, nkeys)],
            scratch_shapes=[pltpu.VMEM((nkeys, LANES), BF), pltpu.VMEM((nkeys, LANES), BF)],
        ),
        out_shape=[
            jax.ShapeDtypeStruct((rows, width), BF),
            jax.ShapeDtypeStruct((pairs, 2 * rows, nkeys), BF),
        ],
        compiler_params=params(),
        cost_estimate=cost(rows, nkeys, width, 45),
        name="self_forward",
    )(blocks, own, q, kv, kv, bias)


def self_backward(blocks, own, q, kv, do, probs):
    rows, width = q.shape
    nkeys = kv.shape[0]
    pairs = width // LANES
    return pl.pallas_call(
        self_backward_kernel,
        grid_spec=pltpu.PrefetchScalarGridSpec(
            num_scalar_prefetch=2,
            grid=(pairs,),
            in_specs=[
                column_block(rows, 0),
                column_block(nkeys, 0),
                column_block(nkeys, pairs),
                column_block(rows, 0),
                whole_block(2 * rows, nkeys),
            ],
            out_specs=[
                column_block(rows, 0),
                column_block(nkeys, 0),
                column_block(nkeys, 0),
                whole_block(2, nkeys),
            ],
            scratch_shapes=[
                pltpu.VMEM((nkeys, LANES), BF),
                pltpu.VMEM((nkeys, LANES), BF),
                pltpu.VMEM((nkeys, LANES), F32),
            ],
        ),
        out_shape=[
            jax.ShapeDtypeStruct((rows, width), BF),
            jax.ShapeDtypeStruct((nkeys, width), BF),
            jax.ShapeDtypeStruct((nkeys, width), BF),
            jax.ShapeDtypeStruct((pairs, 2, nkeys), F32),
        ],
        compiler_params=params(),
        cost_estimate=pl.CostEstimate(flops=0, bytes_accessed=0, transcendentals=0),
        name="self_backward",
    )(blocks, own, q, kv, kv, do, probs)


def cross_forward(q, kv):
    rows, width = q.shape
    nkeys = kv.shape[0]
    pairs = width // LANES
    return pl.pallas_call(
        cross_forward_kernel,
        grid=(pairs,),
        in_specs=[column_block(rows, 0), column_block(nkeys, 0), column_block(nkeys, pairs)],
        out_specs=[column_block(rows, 0), whole_block(2 * rows, nkeys)],
        out_shape=[
            jax.ShapeDtypeStruct((rows, width), BF),
            jax.ShapeDtypeStruct((pairs, 2 * rows, nkeys), BF),
        ],
        compiler_params=params(),
        cost_estimate=cost(rows, nkeys, width, 40),
        name="cross_forward",
    )(q, kv, kv)


def cross_backward(q, kv, do, probs):
    rows, width = q.shape
    nkeys = kv.shape[0]
    pairs = width // LANES
    return pl.pallas_call(
        cross_backward_kernel,
        grid=(pairs,),
        in_specs=[
            column_block(rows, 0),
            column_block(nkeys, 0),
            column_block(nkeys, pairs),
            column_block(rows, 0),
            whole_block(2 * rows, nkeys),
        ],
        out_specs=[column_block(rows, 0), column_block(nkeys, 0), column_block(nkeys, 0)],
        out_shape=[
            jax.ShapeDtypeStruct((rows, width), BF),
            jax.ShapeDtypeStruct((nkeys, width), BF),
            jax.ShapeDtypeStruct((nkeys, width), BF),
        ],
        compiler_params=params(),
        cost_estimate=cost(rows, nkeys, width, 50),
        name="cross_backward",
    )(q, kv, kv, do, probs)


def split_kernel(products, nouts, core_ref, *refs):
    even = core_ref[0] == 0
    keep_ref, give_ref = refs[-2:]
    chips = keep_ref.shape[1]
    for i, (half, row, column) in enumerate(products):
        full = dot(refs[2 * i][...], refs[2 * i + 1][...], FIRST)
        cols = full.shape[1]
        for j in range(full.shape[0] // (2 * half)):
            low = full[2 * j * half : (2 * j + 1) * half]
            high = full[(2 * j + 1) * half : (2 * j + 2) * half]
            spot = (j // chips, j % chips, slice(row, row + half), slice(column, column + cols))
            keep_ref[spot] = jnp.where(even, low, high).astype(BF)
            give_ref[spot] = jnp.where(even, high, low).astype(BF)


def split_grads(core, pairs, places, chips, rows, cols):
    pieces = pairs[0][0].shape[1] // (2 * places[0][0])
    dims = (pieces // chips, chips, rows, cols)
    shape = jax.ShapeDtypeStruct(dims, BF)
    if any(half % 8 != 0 or row % 16 != 0 for half, row, _ in places):
        keep, give = [], []
        for (a, g), (half, row, column) in zip(pairs, places):
            full = weight_grad(a, g).astype(BF).reshape(pieces, 2, half, g.shape[1])
            spot = ((0, 0), (row, rows - row - half), (column, cols - column - g.shape[1]))
            keep.append(jnp.pad(lax.dynamic_index_in_dim(full, core, 1, keepdims=False), spot))
            give.append(jnp.pad(lax.dynamic_index_in_dim(full, 1 - core, 1, keepdims=False), spot))
        return sum(keep[1:], keep[0]).reshape(dims), sum(give[1:], give[0]).reshape(dims)
    vmem = pl.BlockSpec(memory_space=pltpu.VMEM)
    flat = [x for pair in pairs for x in pair]
    return pl.pallas_call(
        functools.partial(split_kernel, places, len(places)),
        in_specs=[pl.BlockSpec(memory_space=pltpu.SMEM)] + [vmem] * len(flat),
        out_specs=[vmem, vmem],
        out_shape=[shape, shape],
        compiler_params=params(),
        cost_estimate=pl.CostEstimate(flops=0, bytes_accessed=0, transcendentals=0),
        name="split_grads",
    )(core.reshape(1).astype(jnp.int32), *flat)


def pick_kernel(dims, spot_ref, gate_ref, up_ref, down_ref, out_ref):
    chips, nz, half, wide, down_half = dims
    width = down_ref.shape[1]
    rows = pl.ds(pl.multiple_of(spot_ref[1] * half, half), half)
    for i, ref in enumerate((gate_ref, up_ref)):
        for z in range(nz):
            source = pl.multiple_of((z * chips + spot_ref[0]) * wide, wide)
            target = (i * nz + z) * wide
            out_ref[:half, target : target + wide] = ref[rows, pl.ds(source, wide)]
    rows = pl.ds(pl.multiple_of((2 * spot_ref[0] + spot_ref[1]) * down_half, down_half), down_half)
    out_ref[half:, :width] = down_ref[rows, :]
    out_ref[half:, width:] = jnp.zeros((down_half, out_ref.shape[1] - width), out_ref.dtype)


def pick_ff(chip, core, gate, up, down, chips):
    half, wide = gate.shape[0] // 2, down.shape[0] // chips
    nz, down_half, width = gate.shape[1] // down.shape[0], wide // 2, down.shape[1]
    cols = 2 * nz * wide
    if wide % LANES != 0 or half % 16 != 0 or down_half % 16 != 0 or cols < width:
        pieces = []
        for w in (gate, up):
            w = lax.dynamic_slice_in_dim(w, core * half, half, 0)
            for z in range(nz):
                pieces.append(lax.dynamic_slice_in_dim(w, (z * chips + chip) * wide, wide, 1))
        pieces = jnp.concatenate(pieces, axis=1)
        down = lax.dynamic_slice_in_dim(down, (2 * chip + core) * down_half, down_half, 0)
        most = max(cols, width)
        return jnp.concatenate(
            [jnp.pad(pieces, ((0, 0), (0, most - cols))), jnp.pad(down, ((0, 0), (0, most - width)))], axis=0
        )
    vmem = pl.BlockSpec(memory_space=pltpu.VMEM)
    return pl.pallas_call(
        functools.partial(pick_kernel, (chips, nz, half, wide, down_half)),
        in_specs=[pl.BlockSpec(memory_space=pltpu.SMEM), vmem, vmem, vmem],
        out_specs=vmem,
        out_shape=jax.ShapeDtypeStruct((half + down_half, cols), gate.dtype),
        compiler_params=params(),
        cost_estimate=pl.CostEstimate(flops=0, bytes_accessed=6 * gate.size, transcendentals=0),
        name="pick_ff",
    )(jnp.stack([chip, core]).astype(jnp.int32), gate, up, down)


def assemble_kernel(spot_ref, mine_ref, other_ref, out_ref):
    chips, nz = mine_ref.shape[:2]
    for r, ref in enumerate((mine_ref, other_ref)):
        for k in range(chips):
            member = 2 * (spot_ref[0] ^ k) + (spot_ref[1] ^ r)
            for z in range(nz):
                out_ref[z, member] = ref[k, z]


def assemble(chip, core, mine, other):
    chips, nz, rows, cols = mine.shape
    vmem = pl.BlockSpec(memory_space=pltpu.VMEM)
    out = pl.pallas_call(
        assemble_kernel,
        in_specs=[pl.BlockSpec(memory_space=pltpu.SMEM), vmem, vmem],
        out_specs=vmem,
        out_shape=jax.ShapeDtypeStruct((nz, 2 * chips, rows, cols), mine.dtype),
        compiler_params=params(),
        cost_estimate=pl.CostEstimate(flops=0, bytes_accessed=8 * mine.size, transcendentals=0),
        name="assemble",
    )(jnp.stack([chip, core]).astype(jnp.int32), mine, other)
    return out.reshape(-1, cols)


def place_kernel(dims, parts_ref, gate_ref, up_ref, down_ref):
    chips, nz, half, wide, down_half = dims
    for member in range(2 * chips):
        chip, core = member // 2, member % 2
        for i, out in enumerate((gate_ref, up_ref)):
            for z in range(nz):
                source = (i * nz + z) * wide
                spot = (z * chips + chip) * wide
                out[core * half : (core + 1) * half, spot : spot + wide] = parts_ref[
                    member, :half, source : source + wide
                ].astype(F32)
        down_ref[member * down_half : (member + 1) * down_half, :] = parts_ref[
            member, half : half + down_half, : down_ref.shape[1]
        ].astype(F32)


def place_ff(parts, nz, half, wide, down_half, width):
    members = parts.shape[0]
    chips = members // 2
    hidden = nz * chips * wide
    if wide % LANES != 0 or half % 16 != 0 or down_half % 16 != 0:
        both = parts[:, :half, : 2 * nz * wide].astype(F32).reshape(chips, 2, half, 2, nz, wide)
        both = both.transpose(3, 1, 2, 4, 0, 5).reshape(2, 2 * half, hidden)
        return both[0], both[1], parts[:, half:, :width].astype(F32).reshape(-1, width)
    vmem = pl.BlockSpec(memory_space=pltpu.VMEM)
    return pl.pallas_call(
        functools.partial(place_kernel, (chips, nz, half, wide, down_half)),
        in_specs=[vmem],
        out_specs=[vmem] * 3,
        out_shape=[
            jax.ShapeDtypeStruct((2 * half, hidden), F32),
            jax.ShapeDtypeStruct((2 * half, hidden), F32),
            jax.ShapeDtypeStruct((members * down_half, width), F32),
        ],
        compiler_params=params(),
        cost_estimate=pl.CostEstimate(flops=0, bytes_accessed=6 * parts.size, transcendentals=0),
        name="place_ff",
    )(parts)


def fence(*arrays):
    return lax.optimization_barrier(arrays)


def vmem_call(kernel, scalars, arrays, shapes, name, scratch=()):
    vmem = pl.BlockSpec(memory_space=pltpu.VMEM)
    return pl.pallas_call(
        kernel,
        in_specs=[pl.BlockSpec(memory_space=pltpu.SMEM)] + [vmem] * len(arrays),
        out_specs=[vmem] * len(shapes),
        out_shape=shapes,
        scratch_shapes=list(scratch),
        compiler_params=params(),
        cost_estimate=pl.CostEstimate(flops=0, bytes_accessed=2 * sum(x.size for x in arrays), transcendentals=0),
        name=name,
    )(jnp.stack(scalars).astype(jnp.int32), *arrays)


def chip_bit(chips, step, h):
    return 1 << ((step + h) % (chips.bit_length() - 1))


def held_before(chips, step, h):
    spots = list(range(chips))
    for i in range(step):
        spots = [k for k in spots if not k & chip_bit(chips, i, h)]
    return spots


def first_kernel(more, spot_ref, keep_ref, got_ref, *refs):
    rows_ref = refs[0] if more else None
    outs = refs[-4:]
    nz, chips = keep_ref.shape[:2]
    for h in range(2):
        b = chip_bit(chips, 0, h)
        stays = [k for k in range(chips) if not k & b]
        for k in range(chips):
            out = outs[h] if k & b else outs[2 + h]
            i = stays.index(k & ~b)
            for zz in range(nz // 2):
                z = h * (nz // 2) + zz
                chip = spot_ref[0] ^ k
                total = keep_ref[z, chip].astype(F32) + got_ref[z, chip].astype(F32)
                out[i, zz, more:, :] = total.astype(BF)
                if more:
                    out[i, zz, :more, :] = rows_ref[k, z]


def next_kernel(chips, step, spot_ref, kept0, kept1, got0, got1, give0, give1, keep0, keep1):
    for h, (kept, got, give, keep) in enumerate(((kept0, got0, give0, keep0), (kept1, got1, give1, keep1))):
        b = chip_bit(chips, step, h)
        spots = held_before(chips, step, h)
        stays = [k for k in spots if not k & b]
        for i, k in enumerate(spots):
            total = (kept[i].astype(F32) + got[i].astype(F32)).astype(BF)
            if k & b:
                give[stays.index(k & ~b)] = total
            else:
                keep[stays.index(k)] = total


def half_sum(kept, got, z):
    return (kept[0, z].astype(F32) + got[0, z].astype(F32)).astype(BF)


def last_kernel(more, spot_ref, kept0, kept1, got0, got1, *outs):
    n = kept0.shape[1]
    for h, (kept, got) in enumerate(((kept0, got0), (kept1, got1))):
        for zz in range(n):
            total = half_sum(kept, got, zz)
            outs[0][h * n + zz] = total[more:]
            if more:
                outs[1][h * n + zz] = total[:more]


def last_z_kernel(spot_ref, kept0, kept1, got0, got1, *refs):
    outs, total = refs[:-1], refs[-1]
    n = kept0.shape[1]
    for h, (kept, got) in enumerate(((kept0, got0), (kept1, got1))):
        for zz in range(n):
            total[h * n + zz] = half_sum(kept, got, zz)
    for s, out in enumerate(outs):
        out[...] = total[lax.rem(spot_ref[0] + s, 2 * n)]


def split_z_kernel(spot_ref, x_ref, y_ref, *outs):
    nz, _, cols = x_ref.shape
    for s, out in enumerate(outs):
        z = lax.rem(spot_ref[0] + s, nz)
        out[:, :cols] = x_ref[z]
        out[:, cols:] = y_ref[z]


class Net:
    def __init__(self):
        self.c = lax.axis_index("ctx")
        self.z = lax.axis_index("fsdp")
        self.nc = lax.axis_size("ctx")
        self.nz = lax.axis_size("fsdp")
        self.chips = self.nc // 2
        self.core = self.c % 2
        self.chip = self.c // 2

    def to_core(self, x):
        return lax.ppermute(x, "ctx", [(i, i ^ 1) for i in range(self.nc)])

    def to_chip(self, x, k):
        return lax.ppermute(x, "ctx", [(i, i ^ (2 * k)) for i in range(self.nc)])

    def along(self, x, s):
        n = self.nz
        return lax.ppermute(x, "fsdp", [(i, (i + s) % n) for i in range(n)])


    def gather_z(self, x):
        return lax.all_gather(x, "fsdp", axis=0)

    def gather_ctx(self, x):
        return lax.all_gather(x, "ctx", axis=0)

    def sum_z(self, x):
        return lax.psum_scatter(x, "fsdp", scatter_dimension=0, tiled=False)

    def spread_chips(self, x):
        return tuple(self.to_chip(x, k) for k in range(1, self.chips))

    def join_chips(self, x, got):
        out = jnp.zeros(x.shape[:1] + (self.chips,) + x.shape[1:], x.dtype)
        for k, part in enumerate((x,) + tuple(got)):
            out = lax.dynamic_update_index_in_dim(out, part, self.chip ^ k, 1)
        return out

    def join_cores(self, x, got):
        even = self.core == 0
        return jnp.stack([jnp.where(even, x, got), jnp.where(even, got, x)], axis=2)


    def swap_blocks(self, x):
        return (x[0],) + tuple(self.to_chip(x[k], k) for k in range(1, self.chips))


    def send_half(self, give, step):
        return tuple(self.to_chip(x, chip_bit(self.chips, step, h)) for h, x in enumerate(give))

    def first_half(self, keep, got, rows=None):
        nz, chips, each, cols = keep.shape
        more = 0 if rows is None else rows.shape[2]
        shape = jax.ShapeDtypeStruct((chips // 2, nz // 2, more + each, cols), BF)
        extra = () if rows is None else (rows,)
        out = vmem_call(
            functools.partial(first_kernel, more), [self.chip], (keep, got) + extra, [shape] * 4, "first_half"
        )
        return out[:2], out[2:]

    def next_half(self, kept, got, step):
        shape = kept[0].shape
        shape = jax.ShapeDtypeStruct((shape[0] // 2,) + shape[1:], BF)
        kernel = functools.partial(next_kernel, self.chips, step)
        out = vmem_call(kernel, [self.chip], tuple(kept) + tuple(got), [shape] * 4, "next_half")
        return out[:2], out[2:]

    def sum_chips(self, give, kept, first=None):
        steps = self.chips.bit_length() - 1
        got = self.send_half(give, 0) if first is None else first
        for step in range(1, steps):
            give, kept = self.next_half(kept, got, step)
            got = self.send_half(give, step)
        return tuple(kept) + tuple(got)

    def last_half(self, parts, more=0):
        nz, rows, cols = 2 * parts[0].shape[1], parts[0].shape[2], parts[0].shape[3]
        shapes = [jax.ShapeDtypeStruct((nz, rows - more, cols), BF)]
        if more:
            shapes.append(jax.ShapeDtypeStruct((nz, more, cols), BF))
        return vmem_call(functools.partial(last_kernel, more), [self.z], parts, shapes, "last_half")

    def last_z(self, parts):
        nz, rows, cols = 2 * parts[0].shape[1], parts[0].shape[2], parts[0].shape[3]
        shapes = [jax.ShapeDtypeStruct((rows, cols), BF)] * nz
        scratch = [pltpu.VMEM((nz, rows, cols), BF)]
        return vmem_call(last_z_kernel, [self.z], parts, shapes, "last_z", scratch)

    def split_z(self, x, y):
        nz, rows, cols = x.shape
        shapes = [jax.ShapeDtypeStruct((rows, cols + y.shape[2]), BF)] * nz
        return vmem_call(split_z_kernel, [self.z], (x, y), shapes, "split_z")

    def send_z(self, parts):
        return (parts[0],) + tuple(self.along(x, s) for s, x in enumerate(parts[1:], 1))

    def add(self, parts):
        total = parts[0].astype(F32)
        for part in parts[1:]:
            total = total + part.astype(F32)
        return total


def per_device(
    tokens,
    encoder,
    cotangent,
    buckets,
    pairing,
    norm_one,
    self_query,
    self_key,
    self_value,
    self_output,
    bias_table,
    norm_two,
    cross_query,
    cross_key,
    cross_value,
    cross_output,
    norm_three,
    ff_gate,
    ff_up,
    ff_down,
):
    net = Net()
    nc, nz, chips = net.nc, net.nz, net.chips
    mine = net.c
    shard = self_query.shape[0]
    width = self_query.shape[1]
    heads = bias_table.shape[1]
    pairs = width // LANES
    each = shard // nc
    half = shard // 2
    down_shard = ff_down.shape[0]
    wide = down_shard // chips
    down_half = wide // 2
    pack_rows = half + down_half

    def rows_of(w):
        return lax.dynamic_slice_in_dim(w, mine * each, each, 0)

    def flat(x):
        return x.reshape(-1, x.shape[-1])

    table_size = bias_table.size
    extra_width = LANES * math.ceil((4 + table_size) / LANES)
    small = jnp.stack([norm_one, norm_two, norm_three], axis=1)
    small = jnp.pad(rows_of(small), ((0, 0), (0, extra_width - 3)))
    line = jnp.pad(bias_table.reshape(1, -1), ((0, each - 1), (4, extra_width - 4 - table_size)))
    one = jnp.concatenate([rows_of(self_query), rows_of(self_key), rows_of(self_value), small + line], axis=1)
    rows_one = jnp.concatenate([tokens[0], encoder[0]], axis=0)
    incoming = cotangent[0]
    rows_chips = net.spread_chips(rows_one)
    one, rows_chips = fence(net.gather_z(one), rows_chips)
    one, self_output, cross_query, cross_key, cross_value, cross_output, ff_gate, ff_up, ff_down = fence(
        one, self_output, cross_query, cross_key, cross_value, cross_output, ff_gate, ff_up, ff_down
    )
    one_chips = net.spread_chips(one)
    two = jnp.concatenate(
        [rows_of(w) for w in (self_output, cross_query, cross_key, cross_value, cross_output)], axis=1
    )
    two = net.gather_z(two)
    three = pick_ff(net.chip, net.core, ff_gate, ff_up, ff_down, chips)
    pack_cols = three.shape[1]
    one_chips, two, three = fence(one_chips, two, three)
    three = net.gather_z(three)

    one_mine = jnp.stack((one,) + one_chips)
    one_core = net.to_core(one_mine)
    two_chips = net.spread_chips(two)
    one_core, rows_chips = fence(one_core, rows_chips)
    rows_mine = jnp.stack((rows_one,) + rows_chips)
    rows_core = net.to_core(rows_mine)
    one = assemble(net.chip, net.core, one_mine, one_core)

    w_q = one[:, :width]
    w_kv = one[:, width : 3 * width]
    extra = one[:, 3 * width :]
    gains = extra[:, :4].astype(F32).T
    g_one, g_two, g_three = gains[0], gains[1], gains[2]
    table = extra.reshape(nz, shard, extra_width)[:, 0, 4 : 4 + table_size].reshape(-1, heads)
    nbuckets = table.shape[0]

    count = tokens.shape[1]
    seq_len = count * nc
    tokens_all = jnp.concatenate([flat(rows_mine[:, :count]), flat(rows_core[:, :count])], axis=0)
    states_all = jnp.concatenate([flat(rows_mine[:, count:]), flat(rows_core[:, count:])], axis=0)
    member = mine ^ jnp.array([2 * k + r for r in range(2) for k in range(chips)], dtype=jnp.int32)
    match = member[:, None] == jnp.arange(nc, dtype=jnp.int32)[None, :]
    paired = jnp.sum(jnp.where(match, pairing[None, :], 0), axis=1)
    blocks = jnp.stack([paired, 2 * nc - 1 - paired], axis=1).reshape(-1).astype(jnp.int32)
    own = blocks[:2]

    picks = (buckets[::-1][None, :] == jnp.arange(nbuckets, dtype=jnp.int32)[:, None]).astype(BF)
    bias = jnp.dot(table.T, picks, preferred_element_type=F32).reshape(pairs, 2, seq_len)

    rows_in = tokens[0].astype(F32)
    a_one, norm_one_back = jax.vjp(norm_apply, rows_in, g_one)
    a_one = a_one.astype(BF)
    a_one_all = norm_apply(tokens_all.astype(F32), g_one).astype(BF)
    query = product(a_one, w_q).astype(BF)
    kv = product(a_one_all, w_kv).astype(BF)
    attended, self_probs = self_forward(blocks, own, query, kv, bias)
    attended, two_chips, incoming, three = fence(attended, two_chips, incoming, three)
    two_mine = jnp.stack((two,) + two_chips)
    two_core = net.to_core(two_mine)
    incoming_chips = net.spread_chips(incoming)
    incoming_rows = flat(jnp.stack((incoming,) + incoming_chips))
    two = assemble(net.chip, net.core, two_mine, two_core)
    w_o = two[:, :width]
    second = rows_in + product(attended, w_o)
    two, second, three = fence(two, second, three)
    three_core = net.to_core(three)
    c_q = two[:, width : 2 * width]
    c_kv = two[:, 2 * width : 4 * width]
    c_o = two[:, 4 * width :]
    cross_kv = product(states_all, c_kv).astype(BF)
    a_two, norm_two_back = jax.vjp(norm_apply, second, g_two)
    a_two = a_two.astype(BF)
    cross_q = product(a_two, c_q).astype(BF)
    cross_o, cross_probs = cross_forward(cross_q, cross_kv)
    third = second + product(cross_o, c_o)
    a_three, norm_three_back = jax.vjp(norm_apply, third, g_three)
    a_three = a_three.astype(BF)

    a_three_chips = net.spread_chips(a_three)
    even = net.core == 0
    three_low, three_high = jnp.where(even, three, three_core), jnp.where(even, three_core, three)
    w_gu = jnp.stack([three_low[:, :half], three_high[:, :half]], axis=1)[..., : 2 * nz * wide].reshape(nz * shard, -1)
    w_down = flat(jnp.stack([three_low[:, half:], three_high[:, half:]], axis=1)[..., :width])
    w_gu, w_down, incoming_rows, a_three_chips = fence(w_gu, w_down, incoming_rows, a_three_chips)
    a_three_rows = flat(jnp.stack((a_three,) + a_three_chips))
    gate_up = product(a_three_rows, w_gu)
    units = nz * wide
    hidden, geglu_back = jax.vjp(
        lambda left, right: jax.nn.gelu(left, approximate=True) * right, gate_up[:, :units], gate_up[:, units:]
    )
    hidden = hidden.astype(BF)
    grad_gate, grad_up = geglu_back(through(incoming_rows, w_down))
    grad_gate_up = jnp.concatenate([grad_gate.astype(BF), grad_up.astype(BF)], axis=1)
    grad_three_part = through(grad_gate_up, w_gu).astype(BF).reshape(chips, count, width)
    result_part = product(hidden, w_down).astype(BF).reshape(chips, count, width)
    grad_three_terms = net.swap_blocks(grad_three_part)
    three_keep, three_give = split_grads(
        net.core,
        [(a_three_rows, grad_gate_up), (hidden, incoming_rows)],
        [(half, 0, 0), (down_half, half, 0)],
        1,
        pack_rows,
        pack_cols,
    )
    grad_three_terms, three_keep, three_give, result_part = fence(
        grad_three_terms, three_keep, three_give, result_part
    )
    three_core = net.to_core(three_give)
    result_terms = net.swap_blocks(result_part)

    part_three, grad_g_three = norm_three_back(net.add(grad_three_terms))
    grad_third = incoming.astype(F32) + part_three
    branch_two = grad_third.astype(BF)
    grad_cross_o = through(branch_two, c_o).astype(BF)
    grad_cross_o, three_core = fence(grad_cross_o, three_core)
    dcq, dck, dcv = cross_backward(cross_q, cross_kv, grad_cross_o, cross_probs)
    dcq, result_terms = fence(dcq, result_terms)
    result = third + net.add(result_terms)
    three = net.sum_z(net.add((three_keep[:, 0], three_core[:, 0])).astype(BF))
    part_two, grad_g_two = norm_two_back(through(dcq, c_q))
    grad_second = grad_third + part_two
    branch_one = grad_second.astype(BF)
    two_keep, two_give = split_grads(
        net.core,
        [
            (attended, branch_one),
            (a_two, dcq),
            (states_all, dck),
            (states_all, dcv),
            (cross_o, branch_two),
        ],
        [(each, 0, i * width) for i in range(5)],
        chips,
        each,
        5 * width,
    )
    grad_attended = through(branch_one, w_o).astype(BF)
    two_core = net.to_core(two_give)
    grad_attended, two_core = fence(grad_attended, two_core)
    two_give, two_kept = net.first_half(two_keep, two_core)
    two_got = net.send_half(two_give, 0)
    dq, dk, dv, bias_grad = self_backward(blocks, own, query, kv, grad_attended, self_probs)
    states_part = (through(dck, c_kv[:, :width]) + through(dcv, c_kv[:, width:])).astype(BF)
    dq, dk, dv, bias_grad, two_got, states_part = fence(dq, dk, dv, bias_grad, two_got, states_part)
    steps = chips.bit_length() - 1
    for step in range(1, steps):
        two_give, two_kept = net.next_half(two_kept, two_got, step)
        two_give, two_kept, dk, dv = fence(two_give, two_kept, dk, dv)
        two_got = net.send_half(two_give, step)
    rows_part = (through(dk, w_kv[:, :width]) + through(dv, w_kv[:, width:])).astype(BF).reshape(2, chips, count, width)
    states_part = states_part.reshape(2, chips, -1, width)
    sent_keep, sent_give = (jnp.concatenate([rows_part[r], states_part[r]], axis=1) for r in range(2))
    sent_keep, sent_give, two_got, three = fence(sent_keep, sent_give, two_got, three)
    three = net.gather_ctx(three)
    sent_core = net.to_core(sent_give)
    one_keep, one_give = split_grads(
        net.core,
        [(a_one, dq), (a_one_all, dk), (a_one_all, dv)],
        [(each, 0, i * width) for i in range(3)],
        chips,
        each,
        3 * width,
    )
    sent_core, one_keep, one_give = fence(sent_core, one_keep, one_give)
    sent_terms = net.swap_blocks((sent_keep.astype(F32) + sent_core.astype(F32)).astype(BF))
    one_core = net.to_core(one_give)
    table_grad = lax.dot_general(
        picks.astype(F32), bias_grad.reshape(heads, seq_len), LAST, precision=lax.Precision.HIGHEST
    )
    one_core, table_grad = fence(one_core, table_grad)
    one_give, one_kept = net.first_half(one_keep, one_core)
    one_give, nearest = fence(one_give, sent_terms[1])
    one_got = net.send_half(one_give, 0)
    sent_terms = (sent_terms[0], nearest) + tuple(sent_terms[2:])
    sent_terms, one_kept, two_got = fence(sent_terms, one_kept, two_got)
    two_terms = net.send_z(net.last_z(tuple(two_kept) + tuple(two_got)))
    own_part = net.add(sent_terms)
    grad_a_one = through(dq, w_q) + own_part[:count]
    grad_states = own_part[count:]
    part_one, grad_g_one = norm_one_back(grad_a_one)
    grad_rows = grad_second + part_one

    small_grad = jnp.pad(jnp.stack([grad_g_one, grad_g_two, grad_g_three]), ((0, 1), (0, 0)))
    small_grad = small_grad.reshape(4, nz, shard).swapaxes(0, 1).reshape(nz, -1)
    small_grad = jnp.concatenate([small_grad, table_grad.reshape(nz, table_size)], axis=1).astype(BF)
    small_size = small_grad.shape[1]
    small_cols = math.ceil(small_size / each)
    small_width = LANES * math.ceil(small_cols / LANES)
    small_grad = jnp.pad(small_grad, ((0, 0), (0, each * small_cols - small_size))).reshape(nz, each, small_cols)
    small_grad = jnp.pad(small_grad, ((0, 0), (0, 0), (0, small_width - small_cols)))
    one_got, small_grad = fence(one_got, small_grad)
    one_parts = net.sum_chips(one_give, one_kept, one_got)
    one_parts, two_terms, three = fence(one_parts, two_terms, three)
    two = net.gather_ctx(net.add(two_terms).astype(BF))
    one_sum = net.last_half(one_parts)[0]
    one_terms = net.send_z(net.split_z(one_sum, small_grad))
    one = net.gather_ctx(net.add(one_terms).astype(BF))
    total_two = flat(two).astype(F32)
    total_one = flat(one[..., : 3 * width]).astype(F32)
    total_gate, total_up, total_down = place_ff(three, nz, half, wide, down_half, width)
    small_total = jnp.sum(one[..., 3 * width : 3 * width + small_cols].reshape(nc, -1).astype(F32), axis=0)
    gain_total = small_total[: 4 * shard].reshape(4, shard)
    table_total = small_total[4 * shard : 4 * shard + table_size].reshape(-1, heads)

    return (
        result.astype(BF)[None],
        grad_rows[None],
        grad_states[None],
        gain_total[0],
        total_one[:, :width],
        total_one[:, width : 2 * width],
        total_one[:, 2 * width : 3 * width],
        total_two[:, :width],
        table_total,
        gain_total[1],
        total_two[:, width : 2 * width],
        total_two[:, 2 * width : 3 * width],
        total_two[:, 3 * width : 4 * width],
        total_two[:, 4 * width :],
        gain_total[2],
        total_gate,
        total_up,
        total_down,
    )


def solution(mesh):
    rows = P("fsdp", "ctx", None)
    gain = P("fsdp")
    weight = P("fsdp", None)
    gradients = (
        gain, weight, weight, weight, weight, weight, gain, weight, weight, weight, weight, gain, weight, weight, weight
    )
    return jax.shard_map(
        per_device,
        mesh=mesh,
        in_specs=(rows, rows, rows, P(), P()) + gradients,
        out_specs=(rows, rows, rows) + gradients,
        check_vma=False,
    )
```

```python
import functools
import math

import jax
import jax.numpy as jnp
from jax import lax
from jax.experimental import pallas as pl
from jax.experimental.pallas import tpu as pltpu
from jax.sharding import PartitionSpec as P

BF = jnp.bfloat16
F32 = jnp.float32
LANES = 128
VMEM_LIMIT = 48 * 1024 * 1024
LAST = (((1,), (1,)), ((), ()))
FIRST = (((0,), (0,)), ((), ()))
PLAIN = (((1,), (0,)), ((), ()))


def norm_apply(v, g):
    return v * lax.rsqrt(jnp.mean(v * v, axis=-1, keepdims=True) + 1e-06) * g


def product(a, w):
    return jnp.dot(a, w, preferred_element_type=F32)


def through(grad, w):
    return lax.dot_general(grad, w, LAST, preferred_element_type=F32)


def weight_grad(a, grad):
    return lax.dot_general(a, grad, FIRST, preferred_element_type=F32)


def dot(a, b, dims):
    return lax.dot_general(a, b, dims, preferred_element_type=F32)


def two_heads(block):
    half = block.shape[1] // 2
    low = lax.broadcasted_iota(jnp.int32, block.shape, 1) < half
    zero = jnp.zeros_like(block)
    return jnp.concatenate([jnp.where(low, block, zero), jnp.where(low, zero, block)], axis=0)


def join_heads(rows):
    n = rows.shape[0] // 2
    low = lax.broadcasted_iota(jnp.int32, (n, rows.shape[1]), 1) < rows.shape[1] // 2
    return jnp.where(low, rows[:n], rows[n:])


def to_positions(blocks_ref, source, target, block):
    for i in range(source.shape[0] // block):
        spot = pl.multiple_of(blocks_ref[i] * block, block)
        target[pl.ds(spot, block), :] = source[i * block : (i + 1) * block, :]


def from_positions(blocks_ref, source, target, block):
    for i in range(target.shape[0] // block):
        spot = pl.multiple_of(blocks_ref[i] * block, block)
        target[i * block : (i + 1) * block, :] = source[pl.ds(spot, block), :].astype(target.dtype)


def sheared(line, block):
    sublane = lax.broadcasted_iota(jnp.int32, line.shape, 0)
    for bit in (1, 2, 4):
        line = jnp.where(sublane & bit != 0, pltpu.roll(line, bit, 1), line)
    return jnp.concatenate([line if i == 0 else pltpu.roll(line, i, 1) for i in range(0, block, 8)], axis=0)


def self_forward_kernel(blocks_ref, own_ref, q_ref, k_ref, v_ref, bias_ref, o_ref, p_ref, ks, vs):
    rows = q_ref.shape[0]
    block = rows // 2
    nkeys = k_ref.shape[0]
    to_positions(blocks_ref, k_ref, ks, block)
    to_positions(blocks_ref, v_ref, vs, block)
    scores = dot(two_heads(q_ref[...]), ks[...], LAST)
    column = lax.broadcasted_iota(jnp.int32, (block, nkeys), 1)
    row = lax.broadcasted_iota(jnp.int32, (block, nkeys), 0)
    for head in range(2):
        line = jnp.broadcast_to(bias_ref[0, head : head + 1, :], (8, nkeys))
        for part in range(2):
            start = own_ref[part] * block
            shear = sheared(pltpu.roll(line, start + 1, 1), block)
            at = head * rows + part * block
            s = jnp.where(column <= row + start, scores[at : at + block] + shear, -1e30)
            top = jnp.max(s, axis=-1, keepdims=True)
            expo = jnp.exp(s - top)
            total = jnp.sum(expo, axis=-1, keepdims=True)
            p_ref[0, at : at + block, :] = (expo / total).astype(BF)
    o_ref[...] = join_heads(dot(p_ref[0], vs[...], PLAIN)).astype(BF)


def cross_forward_kernel(q_ref, k_ref, v_ref, o_ref, p_ref):
    s = dot(two_heads(q_ref[...]), k_ref[...], LAST)
    top = jnp.max(s, axis=-1, keepdims=True)
    expo = jnp.exp(s - top)
    total = jnp.sum(expo, axis=-1, keepdims=True)
    p_ref[0] = (expo / total).astype(BF)
    o_ref[...] = join_heads(dot(p_ref[0], v_ref[...], PLAIN)).astype(BF)


def score_gradient(probs, dom, values):
    dp = dot(dom, values, LAST)
    p = probs.astype(F32)
    delta = jnp.sum(p * dp, axis=-1, keepdims=True)
    return (p * (dp - delta)).astype(BF)


def cross_backward_kernel(q_ref, k_ref, v_ref, do_ref, p_ref, dq_ref, dk_ref, dv_ref):
    dom = two_heads(do_ref[...])
    probs = p_ref[0]
    ds = score_gradient(probs, dom, v_ref[...])
    dq_ref[...] = join_heads(dot(ds, k_ref[...], PLAIN)).astype(BF)
    dk_ref[...] = dot(ds, two_heads(q_ref[...]), FIRST).astype(BF)
    dv_ref[...] = dot(probs, dom, FIRST).astype(BF)


def self_backward_kernel(
    blocks_ref, own_ref, q_ref, k_ref, v_ref, do_ref, p_ref, dq_ref, dk_ref, dv_ref, db_ref, ks, vs, acc
):
    rows = q_ref.shape[0]
    block = rows // 2
    nkeys = k_ref.shape[0]
    to_positions(blocks_ref, k_ref, ks, block)
    to_positions(blocks_ref, v_ref, vs, block)
    dom = two_heads(do_ref[...])
    probs = p_ref[0]
    ds = score_gradient(probs, dom, vs[...])
    dq_ref[...] = join_heads(dot(ds, ks[...], PLAIN)).astype(BF)
    acc[...] = dot(ds, two_heads(q_ref[...]), FIRST)
    from_positions(blocks_ref, acc, dk_ref, block)
    acc[...] = dot(probs, dom, FIRST)
    from_positions(blocks_ref, acc, dv_ref, block)
    for head in range(2):
        lines = None
        for part in range(2):
            at = head * rows + part * block
            x = ds[at : at + block].astype(F32)
            size = block
            while size > 1:
                size //= 2
                x = x[:size] + pltpu.roll(x[size:], nkeys - size, 1)
            x = pltpu.roll(jnp.broadcast_to(x, (8, nkeys)), nkeys - own_ref[part] * block - 1, 1)
            lines = x if lines is None else lines + x
        db_ref[0, head : head + 1, :] = lines[0:1]


def column_block(rows, offset):
    return pl.BlockSpec((rows, LANES), lambda i, *_: (0, offset + i))


def whole_block(a, b):
    return pl.BlockSpec((1, a, b), lambda i, *_: (i, 0, 0))


def params():
    return pltpu.CompilerParams(vmem_limit_bytes=VMEM_LIMIT)


def cost(rows, nkeys, width, weight):
    return pl.CostEstimate(
        flops=2 * rows * nkeys * width * weight,
        bytes_accessed=4 * rows * nkeys * (width // LANES),
        transcendentals=0,
    )


def self_forward(blocks, own, q, kv, bias):
    rows, width = q.shape
    nkeys = kv.shape[0]
    pairs = width // LANES
    return pl.pallas_call(
        self_forward_kernel,
        grid_spec=pltpu.PrefetchScalarGridSpec(
            num_scalar_prefetch=2,
            grid=(pairs,),
            in_specs=[
                column_block(rows, 0),
                column_block(nkeys, 0),
                column_block(nkeys, pairs),
                whole_block(2, nkeys),
            ],
            out_specs=[column_block(rows, 0), whole_block(2 * rows, nkeys)],
            scratch_shapes=[pltpu.VMEM((nkeys, LANES), BF), pltpu.VMEM((nkeys, LANES), BF)],
        ),
        out_shape=[
            jax.ShapeDtypeStruct((rows, width), BF),
            jax.ShapeDtypeStruct((pairs, 2 * rows, nkeys), BF),
        ],
        compiler_params=params(),
        cost_estimate=cost(rows, nkeys, width, 45),
        name="self_forward",
    )(blocks, own, q, kv, kv, bias)


def self_backward(blocks, own, q, kv, do, probs):
    rows, width = q.shape
    nkeys = kv.shape[0]
    pairs = width // LANES
    return pl.pallas_call(
        self_backward_kernel,
        grid_spec=pltpu.PrefetchScalarGridSpec(
            num_scalar_prefetch=2,
            grid=(pairs,),
            in_specs=[
                column_block(rows, 0),
                column_block(nkeys, 0),
                column_block(nkeys, pairs),
                column_block(rows, 0),
                whole_block(2 * rows, nkeys),
            ],
            out_specs=[
                column_block(rows, 0),
                column_block(nkeys, 0),
                column_block(nkeys, 0),
                whole_block(2, nkeys),
            ],
            scratch_shapes=[
                pltpu.VMEM((nkeys, LANES), BF),
                pltpu.VMEM((nkeys, LANES), BF),
                pltpu.VMEM((nkeys, LANES), F32),
            ],
        ),
        out_shape=[
            jax.ShapeDtypeStruct((rows, width), BF),
            jax.ShapeDtypeStruct((nkeys, width), BF),
            jax.ShapeDtypeStruct((nkeys, width), BF),
            jax.ShapeDtypeStruct((pairs, 2, nkeys), F32),
        ],
        compiler_params=params(),
        cost_estimate=pl.CostEstimate(flops=0, bytes_accessed=0, transcendentals=0),
        name="self_backward",
    )(blocks, own, q, kv, kv, do, probs)


def cross_forward(q, kv):
    rows, width = q.shape
    nkeys = kv.shape[0]
    pairs = width // LANES
    return pl.pallas_call(
        cross_forward_kernel,
        grid=(pairs,),
        in_specs=[column_block(rows, 0), column_block(nkeys, 0), column_block(nkeys, pairs)],
        out_specs=[column_block(rows, 0), whole_block(2 * rows, nkeys)],
        out_shape=[
            jax.ShapeDtypeStruct((rows, width), BF),
            jax.ShapeDtypeStruct((pairs, 2 * rows, nkeys), BF),
        ],
        compiler_params=params(),
        cost_estimate=cost(rows, nkeys, width, 40),
        name="cross_forward",
    )(q, kv, kv)


def cross_backward(q, kv, do, probs):
    rows, width = q.shape
    nkeys = kv.shape[0]
    pairs = width // LANES
    return pl.pallas_call(
        cross_backward_kernel,
        grid=(pairs,),
        in_specs=[
            column_block(rows, 0),
            column_block(nkeys, 0),
            column_block(nkeys, pairs),
            column_block(rows, 0),
            whole_block(2 * rows, nkeys),
        ],
        out_specs=[column_block(rows, 0), column_block(nkeys, 0), column_block(nkeys, 0)],
        out_shape=[
            jax.ShapeDtypeStruct((rows, width), BF),
            jax.ShapeDtypeStruct((nkeys, width), BF),
            jax.ShapeDtypeStruct((nkeys, width), BF),
        ],
        compiler_params=params(),
        cost_estimate=cost(rows, nkeys, width, 50),
        name="cross_backward",
    )(q, kv, kv, do, probs)


def split_kernel(products, nouts, core_ref, *refs):
    even = core_ref[0] == 0
    keep_ref, give_ref = refs[-2:]
    chips = keep_ref.shape[1]
    for i, (half, row, column) in enumerate(products):
        full = dot(refs[2 * i][...], refs[2 * i + 1][...], FIRST)
        cols = full.shape[1]
        for j in range(full.shape[0] // (2 * half)):
            low = full[2 * j * half : (2 * j + 1) * half]
            high = full[(2 * j + 1) * half : (2 * j + 2) * half]
            spot = (j // chips, j % chips, slice(row, row + half), slice(column, column + cols))
            keep_ref[spot] = jnp.where(even, low, high).astype(BF)
            give_ref[spot] = jnp.where(even, high, low).astype(BF)


def split_grads(core, pairs, places, chips, rows, cols):
    pieces = pairs[0][0].shape[1] // (2 * places[0][0])
    dims = (pieces // chips, chips, rows, cols)
    shape = jax.ShapeDtypeStruct(dims, BF)
    if any(half % 8 != 0 or row % 16 != 0 for half, row, _ in places):
        keep, give = [], []
        for (a, g), (half, row, column) in zip(pairs, places):
            full = weight_grad(a, g).astype(BF).reshape(pieces, 2, half, g.shape[1])
            spot = ((0, 0), (row, rows - row - half), (column, cols - column - g.shape[1]))
            keep.append(jnp.pad(lax.dynamic_index_in_dim(full, core, 1, keepdims=False), spot))
            give.append(jnp.pad(lax.dynamic_index_in_dim(full, 1 - core, 1, keepdims=False), spot))
        return sum(keep[1:], keep[0]).reshape(dims), sum(give[1:], give[0]).reshape(dims)
    vmem = pl.BlockSpec(memory_space=pltpu.VMEM)
    flat = [x for pair in pairs for x in pair]
    return pl.pallas_call(
        functools.partial(split_kernel, places, len(places)),
        in_specs=[pl.BlockSpec(memory_space=pltpu.SMEM)] + [vmem] * len(flat),
        out_specs=[vmem, vmem],
        out_shape=[shape, shape],
        compiler_params=params(),
        cost_estimate=pl.CostEstimate(flops=0, bytes_accessed=0, transcendentals=0),
        name="split_grads",
    )(core.reshape(1).astype(jnp.int32), *flat)


def pick_kernel(dims, spot_ref, gate_ref, up_ref, down_ref, out_ref):
    chips, nz, half, wide, down_half = dims
    width = down_ref.shape[1]
    rows = pl.ds(pl.multiple_of(spot_ref[1] * half, half), half)
    for i, ref in enumerate((gate_ref, up_ref)):
        for z in range(nz):
            source = pl.multiple_of((z * chips + spot_ref[0]) * wide, wide)
            target = (i * nz + z) * wide
            out_ref[:half, target : target + wide] = ref[rows, pl.ds(source, wide)]
    rows = pl.ds(pl.multiple_of((2 * spot_ref[0] + spot_ref[1]) * down_half, down_half), down_half)
    out_ref[half:, :width] = down_ref[rows, :]
    out_ref[half:, width:] = jnp.zeros((down_half, out_ref.shape[1] - width), out_ref.dtype)


def pick_ff(chip, core, gate, up, down, chips):
    half, wide = gate.shape[0] // 2, down.shape[0] // chips
    nz, down_half, width = gate.shape[1] // down.shape[0], wide // 2, down.shape[1]
    cols = 2 * nz * wide
    if wide % LANES != 0 or half % 16 != 0 or down_half % 16 != 0 or cols < width:
        pieces = []
        for w in (gate, up):
            w = lax.dynamic_slice_in_dim(w, core * half, half, 0)
            for z in range(nz):
                pieces.append(lax.dynamic_slice_in_dim(w, (z * chips + chip) * wide, wide, 1))
        pieces = jnp.concatenate(pieces, axis=1)
        down = lax.dynamic_slice_in_dim(down, (2 * chip + core) * down_half, down_half, 0)
        most = max(cols, width)
        return jnp.concatenate(
            [jnp.pad(pieces, ((0, 0), (0, most - cols))), jnp.pad(down, ((0, 0), (0, most - width)))], axis=0
        )
    vmem = pl.BlockSpec(memory_space=pltpu.VMEM)
    return pl.pallas_call(
        functools.partial(pick_kernel, (chips, nz, half, wide, down_half)),
        in_specs=[pl.BlockSpec(memory_space=pltpu.SMEM), vmem, vmem, vmem],
        out_specs=vmem,
        out_shape=jax.ShapeDtypeStruct((half + down_half, cols), gate.dtype),
        compiler_params=params(),
        cost_estimate=pl.CostEstimate(flops=0, bytes_accessed=6 * gate.size, transcendentals=0),
        name="pick_ff",
    )(jnp.stack([chip, core]).astype(jnp.int32), gate, up, down)


def assemble_kernel(spot_ref, mine_ref, other_ref, out_ref):
    chips, nz = mine_ref.shape[:2]
    for r, ref in enumerate((mine_ref, other_ref)):
        for k in range(chips):
            member = 2 * (spot_ref[0] ^ k) + (spot_ref[1] ^ r)
            for z in range(nz):
                out_ref[z, member] = ref[k, z]


def assemble(chip, core, mine, other):
    chips, nz, rows, cols = mine.shape
    vmem = pl.BlockSpec(memory_space=pltpu.VMEM)
    out = pl.pallas_call(
        assemble_kernel,
        in_specs=[pl.BlockSpec(memory_space=pltpu.SMEM), vmem, vmem],
        out_specs=vmem,
        out_shape=jax.ShapeDtypeStruct((nz, 2 * chips, rows, cols), mine.dtype),
        compiler_params=params(),
        cost_estimate=pl.CostEstimate(flops=0, bytes_accessed=8 * mine.size, transcendentals=0),
        name="assemble",
    )(jnp.stack([chip, core]).astype(jnp.int32), mine, other)
    return out.reshape(-1, cols)


def place_kernel(dims, parts_ref, gate_ref, up_ref, down_ref):
    chips, nz, half, wide, down_half = dims
    for member in range(2 * chips):
        chip, core = member // 2, member % 2
        for i, out in enumerate((gate_ref, up_ref)):
            for z in range(nz):
                source = (i * nz + z) * wide
                spot = (z * chips + chip) * wide
                out[core * half : (core + 1) * half, spot : spot + wide] = parts_ref[
                    member, :half, source : source + wide
                ].astype(F32)
        down_ref[member * down_half : (member + 1) * down_half, :] = parts_ref[
            member, half : half + down_half, : down_ref.shape[1]
        ].astype(F32)


def place_ff(parts, nz, half, wide, down_half, width):
    members = parts.shape[0]
    chips = members // 2
    hidden = nz * chips * wide
    if wide % LANES != 0 or half % 16 != 0 or down_half % 16 != 0:
        both = parts[:, :half, : 2 * nz * wide].astype(F32).reshape(chips, 2, half, 2, nz, wide)
        both = both.transpose(3, 1, 2, 4, 0, 5).reshape(2, 2 * half, hidden)
        return both[0], both[1], parts[:, half:, :width].astype(F32).reshape(-1, width)
    vmem = pl.BlockSpec(memory_space=pltpu.VMEM)
    return pl.pallas_call(
        functools.partial(place_kernel, (chips, nz, half, wide, down_half)),
        in_specs=[vmem],
        out_specs=[vmem] * 3,
        out_shape=[
            jax.ShapeDtypeStruct((2 * half, hidden), F32),
            jax.ShapeDtypeStruct((2 * half, hidden), F32),
            jax.ShapeDtypeStruct((members * down_half, width), F32),
        ],
        compiler_params=params(),
        cost_estimate=pl.CostEstimate(flops=0, bytes_accessed=6 * parts.size, transcendentals=0),
        name="place_ff",
    )(parts)


def fence(*arrays):
    return lax.optimization_barrier(arrays)


def vmem_call(kernel, scalars, arrays, shapes, name, scratch=()):
    vmem = pl.BlockSpec(memory_space=pltpu.VMEM)
    return pl.pallas_call(
        kernel,
        in_specs=[pl.BlockSpec(memory_space=pltpu.SMEM)] + [vmem] * len(arrays),
        out_specs=[vmem] * len(shapes),
        out_shape=shapes,
        scratch_shapes=list(scratch),
        compiler_params=params(),
        cost_estimate=pl.CostEstimate(flops=0, bytes_accessed=2 * sum(x.size for x in arrays), transcendentals=0),
        name=name,
    )(jnp.stack(scalars).astype(jnp.int32), *arrays)


def chip_bit(chips, step, h):
    return 1 << ((step + h) % (chips.bit_length() - 1))


def held_before(chips, step, h):
    spots = list(range(chips))
    for i in range(step):
        spots = [k for k in spots if not k & chip_bit(chips, i, h)]
    return spots


def first_kernel(more, spot_ref, keep_ref, got_ref, *refs):
    rows_ref = refs[0] if more else None
    outs = refs[-4:]
    nz, chips = keep_ref.shape[:2]
    for h in range(2):
        b = chip_bit(chips, 0, h)
        stays = [k for k in range(chips) if not k & b]
        for k in range(chips):
            out = outs[h] if k & b else outs[2 + h]
            i = stays.index(k & ~b)
            for zz in range(nz // 2):
                z = h * (nz // 2) + zz
                chip = spot_ref[0] ^ k
                total = keep_ref[z, chip].astype(F32) + got_ref[z, chip].astype(F32)
                out[i, zz, more:, :] = total.astype(BF)
                if more:
                    out[i, zz, :more, :] = rows_ref[k, z]


def next_kernel(chips, step, spot_ref, kept0, kept1, got0, got1, give0, give1, keep0, keep1):
    for h, (kept, got, give, keep) in enumerate(((kept0, got0, give0, keep0), (kept1, got1, give1, keep1))):
        b = chip_bit(chips, step, h)
        spots = held_before(chips, step, h)
        stays = [k for k in spots if not k & b]
        for i, k in enumerate(spots):
            total = (kept[i].astype(F32) + got[i].astype(F32)).astype(BF)
            if k & b:
                give[stays.index(k & ~b)] = total
            else:
                keep[stays.index(k)] = total


def half_sum(kept, got, z):
    return (kept[0, z].astype(F32) + got[0, z].astype(F32)).astype(BF)


def last_kernel(more, spot_ref, kept0, kept1, got0, got1, *outs):
    n = kept0.shape[1]
    for h, (kept, got) in enumerate(((kept0, got0), (kept1, got1))):
        for zz in range(n):
            total = half_sum(kept, got, zz)
            outs[0][h * n + zz] = total[more:]
            if more:
                outs[1][h * n + zz] = total[:more]


def last_z_kernel(spot_ref, kept0, kept1, got0, got1, *refs):
    outs, total = refs[:-1], refs[-1]
    n = kept0.shape[1]
    for h, (kept, got) in enumerate(((kept0, got0), (kept1, got1))):
        for zz in range(n):
            total[h * n + zz] = half_sum(kept, got, zz)
    for s, out in enumerate(outs):
        out[...] = total[lax.rem(spot_ref[0] + s, 2 * n)]


def split_z_kernel(spot_ref, x_ref, y_ref, *outs):
    nz, _, cols = x_ref.shape
    for s, out in enumerate(outs):
        z = lax.rem(spot_ref[0] + s, nz)
        out[:, :cols] = x_ref[z]
        out[:, cols:] = y_ref[z]


class Net:
    def __init__(self):
        self.c = lax.axis_index("ctx")
        self.z = lax.axis_index("fsdp")
        self.nc = lax.axis_size("ctx")
        self.nz = lax.axis_size("fsdp")
        self.chips = self.nc // 2
        self.core = self.c % 2
        self.chip = self.c // 2

    def to_core(self, x):
        return lax.ppermute(x, "ctx", [(i, i ^ 1) for i in range(self.nc)])

    def to_chip(self, x, k):
        return lax.ppermute(x, "ctx", [(i, i ^ (2 * k)) for i in range(self.nc)])

    def along(self, x, s):
        n = self.nz
        return lax.ppermute(x, "fsdp", [(i, (i + s) % n) for i in range(n)])


    def gather_z(self, x):
        return lax.all_gather(x, "fsdp", axis=0)

    def gather_ctx(self, x):
        return lax.all_gather(x, "ctx", axis=0)

    def sum_z(self, x):
        return lax.psum_scatter(x, "fsdp", scatter_dimension=0, tiled=False)

    def spread_chips(self, x):
        return tuple(self.to_chip(x, k) for k in range(1, self.chips))

    def join_chips(self, x, got):
        out = jnp.zeros(x.shape[:1] + (self.chips,) + x.shape[1:], x.dtype)
        for k, part in enumerate((x,) + tuple(got)):
            out = lax.dynamic_update_index_in_dim(out, part, self.chip ^ k, 1)
        return out

    def join_cores(self, x, got):
        even = self.core == 0
        return jnp.stack([jnp.where(even, x, got), jnp.where(even, got, x)], axis=2)


    def swap_blocks(self, x):
        return (x[0],) + tuple(self.to_chip(x[k], k) for k in range(1, self.chips))


    def send_half(self, give, step):
        return tuple(self.to_chip(x, chip_bit(self.chips, step, h)) for h, x in enumerate(give))

    def first_half(self, keep, got, rows=None):
        nz, chips, each, cols = keep.shape
        more = 0 if rows is None else rows.shape[2]
        shape = jax.ShapeDtypeStruct((chips // 2, nz // 2, more + each, cols), BF)
        extra = () if rows is None else (rows,)
        out = vmem_call(
            functools.partial(first_kernel, more), [self.chip], (keep, got) + extra, [shape] * 4, "first_half"
        )
        return out[:2], out[2:]

    def next_half(self, kept, got, step):
        shape = kept[0].shape
        shape = jax.ShapeDtypeStruct((shape[0] // 2,) + shape[1:], BF)
        kernel = functools.partial(next_kernel, self.chips, step)
        out = vmem_call(kernel, [self.chip], tuple(kept) + tuple(got), [shape] * 4, "next_half")
        return out[:2], out[2:]

    def sum_chips(self, give, kept, first=None):
        steps = self.chips.bit_length() - 1
        got = self.send_half(give, 0) if first is None else first
        for step in range(1, steps):
            give, kept = self.next_half(kept, got, step)
            got = self.send_half(give, step)
        return tuple(kept) + tuple(got)

    def last_half(self, parts, more=0):
        nz, rows, cols = 2 * parts[0].shape[1], parts[0].shape[2], parts[0].shape[3]
        shapes = [jax.ShapeDtypeStruct((nz, rows - more, cols), BF)]
        if more:
            shapes.append(jax.ShapeDtypeStruct((nz, more, cols), BF))
        return vmem_call(functools.partial(last_kernel, more), [self.z], parts, shapes, "last_half")

    def last_z(self, parts):
        nz, rows, cols = 2 * parts[0].shape[1], parts[0].shape[2], parts[0].shape[3]
        shapes = [jax.ShapeDtypeStruct((rows, cols), BF)] * nz
        scratch = [pltpu.VMEM((nz, rows, cols), BF)]
        return vmem_call(last_z_kernel, [self.z], parts, shapes, "last_z", scratch)

    def split_z(self, x, y):
        nz, rows, cols = x.shape
        shapes = [jax.ShapeDtypeStruct((rows, cols + y.shape[2]), BF)] * nz
        return vmem_call(split_z_kernel, [self.z], (x, y), shapes, "split_z")

    def send_z(self, parts):
        return (parts[0],) + tuple(self.along(x, s) for s, x in enumerate(parts[1:], 1))

    def add(self, parts):
        total = parts[0].astype(F32)
        for part in parts[1:]:
            total = total + part.astype(F32)
        return total


def per_device(
    tokens,
    encoder,
    cotangent,
    buckets,
    pairing,
    norm_one,
    self_query,
    self_key,
    self_value,
    self_output,
    bias_table,
    norm_two,
    cross_query,
    cross_key,
    cross_value,
    cross_output,
    norm_three,
    ff_gate,
    ff_up,
    ff_down,
):
    net = Net()
    nc, nz, chips = net.nc, net.nz, net.chips
    mine = net.c
    shard = self_query.shape[0]
    width = self_query.shape[1]
    heads = bias_table.shape[1]
    pairs = width // LANES
    each = shard // nc
    half = shard // 2
    down_shard = ff_down.shape[0]
    wide = down_shard // chips
    down_half = wide // 2
    pack_rows = half + down_half

    def rows_of(w):
        return lax.dynamic_slice_in_dim(w, mine * each, each, 0)

    def flat(x):
        return x.reshape(-1, x.shape[-1])

    table_size = bias_table.size
    extra_width = LANES * math.ceil((4 + table_size) / LANES)
    small = jnp.stack([norm_one, norm_two, norm_three], axis=1)
    small = jnp.pad(rows_of(small), ((0, 0), (0, extra_width - 3)))
    line = jnp.pad(bias_table.reshape(1, -1), ((0, each - 1), (4, extra_width - 4 - table_size)))
    one = jnp.concatenate([rows_of(self_query), rows_of(self_key), rows_of(self_value), small + line], axis=1)
    rows_one = jnp.concatenate([tokens[0], encoder[0]], axis=0)
    incoming = cotangent[0]
    rows_chips = net.spread_chips(rows_one)
    one, rows_chips = fence(net.gather_z(one), rows_chips)
    one, self_output, cross_query, cross_key, cross_value, cross_output, ff_gate, ff_up, ff_down = fence(
        one, self_output, cross_query, cross_key, cross_value, cross_output, ff_gate, ff_up, ff_down
    )
    one_chips = net.spread_chips(one)
    two = jnp.concatenate(
        [rows_of(w) for w in (self_output, cross_query, cross_key, cross_value, cross_output)], axis=1
    )
    two = net.gather_z(two)
    three = pick_ff(net.chip, net.core, ff_gate, ff_up, ff_down, chips)
    pack_cols = three.shape[1]
    one_chips, two, three = fence(one_chips, two, three)
    three = net.gather_z(three)

    one_mine = jnp.stack((one,) + one_chips)
    one_core = net.to_core(one_mine)
    two_chips = net.spread_chips(two)
    one_core, rows_chips = fence(one_core, rows_chips)
    rows_mine = jnp.stack((rows_one,) + rows_chips)
    rows_core = net.to_core(rows_mine)
    one = assemble(net.chip, net.core, one_mine, one_core)

    w_q = one[:, :width]
    w_kv = one[:, width : 3 * width]
    extra = one[:, 3 * width :]
    gains = extra[:, :4].astype(F32).T
    g_one, g_two, g_three = gains[0], gains[1], gains[2]
    table = extra.reshape(nz, shard, extra_width)[:, 0, 4 : 4 + table_size].reshape(-1, heads)
    nbuckets = table.shape[0]

    count = tokens.shape[1]
    seq_len = count * nc
    tokens_all = jnp.concatenate([flat(rows_mine[:, :count]), flat(rows_core[:, :count])], axis=0)
    states_all = jnp.concatenate([flat(rows_mine[:, count:]), flat(rows_core[:, count:])], axis=0)
    member = mine ^ jnp.array([2 * k + r for r in range(2) for k in range(chips)], dtype=jnp.int32)
    match = member[:, None] == jnp.arange(nc, dtype=jnp.int32)[None, :]
    paired = jnp.sum(jnp.where(match, pairing[None, :], 0), axis=1)
    blocks = jnp.stack([paired, 2 * nc - 1 - paired], axis=1).reshape(-1).astype(jnp.int32)
    own = blocks[:2]

    picks = (buckets[::-1][None, :] == jnp.arange(nbuckets, dtype=jnp.int32)[:, None]).astype(BF)
    bias = jnp.dot(table.T, picks, preferred_element_type=F32).reshape(pairs, 2, seq_len)

    rows_in = tokens[0].astype(F32)
    a_one, norm_one_back = jax.vjp(norm_apply, rows_in, g_one)
    a_one = a_one.astype(BF)
    a_one_all = norm_apply(tokens_all.astype(F32), g_one).astype(BF)
    query = product(a_one, w_q).astype(BF)
    kv = product(a_one_all, w_kv).astype(BF)
    attended, self_probs = self_forward(blocks, own, query, kv, bias)
    attended, two_chips, incoming, three = fence(attended, two_chips, incoming, three)
    two_mine = jnp.stack((two,) + two_chips)
    two_core = net.to_core(two_mine)
    incoming_chips = net.spread_chips(incoming)
    incoming_rows = flat(jnp.stack((incoming,) + incoming_chips))
    two = assemble(net.chip, net.core, two_mine, two_core)
    w_o = two[:, :width]
    second = rows_in + product(attended, w_o)
    two, second, three = fence(two, second, three)
    three_core = net.to_core(three)
    c_q = two[:, width : 2 * width]
    c_kv = two[:, 2 * width : 4 * width]
    c_o = two[:, 4 * width :]
    cross_kv = product(states_all, c_kv).astype(BF)
    a_two, norm_two_back = jax.vjp(norm_apply, second, g_two)
    a_two = a_two.astype(BF)
    cross_q = product(a_two, c_q).astype(BF)
    cross_o, cross_probs = cross_forward(cross_q, cross_kv)
    third = second + product(cross_o, c_o)
    a_three, norm_three_back = jax.vjp(norm_apply, third, g_three)
    a_three = a_three.astype(BF)

    a_three_chips = net.spread_chips(a_three)
    even = net.core == 0
    three_low, three_high = jnp.where(even, three, three_core), jnp.where(even, three_core, three)
    w_gu = jnp.stack([three_low[:, :half], three_high[:, :half]], axis=1)[..., : 2 * nz * wide].reshape(nz * shard, -1)
    w_down = flat(jnp.stack([three_low[:, half:], three_high[:, half:]], axis=1)[..., :width])
    w_gu, w_down, incoming_rows, a_three_chips = fence(w_gu, w_down, incoming_rows, a_three_chips)
    a_three_rows = flat(jnp.stack((a_three,) + a_three_chips))
    gate_up = product(a_three_rows, w_gu)
    units = nz * wide
    hidden, geglu_back = jax.vjp(
        lambda left, right: jax.nn.gelu(left, approximate=True) * right, gate_up[:, :units], gate_up[:, units:]
    )
    hidden = hidden.astype(BF)
    grad_gate, grad_up = geglu_back(through(incoming_rows, w_down))
    grad_gate_up = jnp.concatenate([grad_gate.astype(BF), grad_up.astype(BF)], axis=1)
    grad_three_part = through(grad_gate_up, w_gu).astype(BF).reshape(chips, count, width)
    result_part = product(hidden, w_down).astype(BF).reshape(chips, count, width)
    grad_three_terms = net.swap_blocks(grad_three_part)
    three_keep, three_give = split_grads(
        net.core,
        [(a_three_rows, grad_gate_up), (hidden, incoming_rows)],
        [(half, 0, 0), (down_half, half, 0)],
        1,
        pack_rows,
        pack_cols,
    )
    grad_three_terms, three_keep, three_give, result_part = fence(
        grad_three_terms, three_keep, three_give, result_part
    )
    three_core = net.to_core(three_give)
    result_terms = net.swap_blocks(result_part)

    part_three, grad_g_three = norm_three_back(net.add(grad_three_terms))
    grad_third = incoming.astype(F32) + part_three
    branch_two = grad_third.astype(BF)
    grad_cross_o = through(branch_two, c_o).astype(BF)
    grad_cross_o, three_core = fence(grad_cross_o, three_core)
    dcq, dck, dcv = cross_backward(cross_q, cross_kv, grad_cross_o, cross_probs)
    dcq, result_terms = fence(dcq, result_terms)
    result = third + net.add(result_terms)
    three = net.sum_z(net.add((three_keep[:, 0], three_core[:, 0])).astype(BF))
    part_two, grad_g_two = norm_two_back(through(dcq, c_q))
    grad_second = grad_third + part_two
    branch_one = grad_second.astype(BF)
    two_keep, two_give = split_grads(
        net.core,
        [
            (attended, branch_one),
            (a_two, dcq),
            (states_all, dck),
            (states_all, dcv),
            (cross_o, branch_two),
        ],
        [(each, 0, i * width) for i in range(5)],
        chips,
        each,
        5 * width,
    )
    grad_attended = through(branch_one, w_o).astype(BF)
    two_core = net.to_core(two_give)
    grad_attended, two_core = fence(grad_attended, two_core)
    two_give, two_kept = net.first_half(two_keep, two_core)
    two_got = net.send_half(two_give, 0)
    dq, dk, dv, bias_grad = self_backward(blocks, own, query, kv, grad_attended, self_probs)
    states_part = (through(dck, c_kv[:, :width]) + through(dcv, c_kv[:, width:])).astype(BF)
    dq, dk, dv, bias_grad, two_got, states_part = fence(dq, dk, dv, bias_grad, two_got, states_part)
    steps = chips.bit_length() - 1
    for step in range(1, steps):
        two_give, two_kept = net.next_half(two_kept, two_got, step)
        two_give, two_kept, dk, dv = fence(two_give, two_kept, dk, dv)
        two_got = net.send_half(two_give, step)
    rows_part = (through(dk, w_kv[:, :width]) + through(dv, w_kv[:, width:])).astype(BF).reshape(2, chips, count, width)
    states_part = states_part.reshape(2, chips, -1, width)
    sent_keep, sent_give = (jnp.concatenate([rows_part[r], states_part[r]], axis=1) for r in range(2))
    sent_keep, sent_give, two_got, three = fence(sent_keep, sent_give, two_got, three)
    three = net.gather_ctx(three)
    sent_core = net.to_core(sent_give)
    one_keep, one_give = split_grads(
        net.core,
        [(a_one, dq), (a_one_all, dk), (a_one_all, dv)],
        [(each, 0, i * width) for i in range(3)],
        chips,
        each,
        3 * width,
    )
    sent_core, one_keep, one_give = fence(sent_core, one_keep, one_give)
    sent_terms = net.swap_blocks((sent_keep.astype(F32) + sent_core.astype(F32)).astype(BF))
    one_core = net.to_core(one_give)
    table_grad = lax.dot_general(
        picks.astype(F32), bias_grad.reshape(heads, seq_len), LAST, precision=lax.Precision.HIGHEST
    )
    one_core, table_grad = fence(one_core, table_grad)
    one_give, one_kept = net.first_half(one_keep, one_core)
    one_give, nearest = fence(one_give, sent_terms[1])
    one_got = net.send_half(one_give, 0)
    sent_terms = (sent_terms[0], nearest) + tuple(sent_terms[2:])
    sent_terms, one_kept, two_got = fence(sent_terms, one_kept, two_got)
    two_terms = net.send_z(net.last_z(tuple(two_kept) + tuple(two_got)))
    own_part = net.add(sent_terms)
    grad_a_one = through(dq, w_q) + own_part[:count]
    grad_states = own_part[count:]
    part_one, grad_g_one = norm_one_back(grad_a_one)
    grad_rows = grad_second + part_one

    small_grad = jnp.pad(jnp.stack([grad_g_one, grad_g_two, grad_g_three]), ((0, 1), (0, 0)))
    small_grad = small_grad.reshape(4, nz, shard).swapaxes(0, 1).reshape(nz, -1)
    small_grad = jnp.concatenate([small_grad, table_grad.reshape(nz, table_size)], axis=1).astype(BF)
    small_size = small_grad.shape[1]
    small_cols = math.ceil(small_size / each)
    small_width = LANES * math.ceil(small_cols / LANES)
    small_grad = jnp.pad(small_grad, ((0, 0), (0, each * small_cols - small_size))).reshape(nz, each, small_cols)
    small_grad = jnp.pad(small_grad, ((0, 0), (0, 0), (0, small_width - small_cols)))
    one_got, small_grad = fence(one_got, small_grad)
    one_parts = net.sum_chips(one_give, one_kept, one_got)
    two = net.gather_ctx(net.add(two_terms).astype(BF))
    one_sum = net.last_half(one_parts)[0]
    one_terms = net.send_z(net.split_z(one_sum, small_grad))
    one = net.gather_ctx(net.add(one_terms).astype(BF))
    total_two = flat(two).astype(F32)
    total_one = flat(one[..., : 3 * width]).astype(F32)
    total_gate, total_up, total_down = place_ff(three, nz, half, wide, down_half, width)
    small_total = jnp.sum(one[..., 3 * width : 3 * width + small_cols].reshape(nc, -1).astype(F32), axis=0)
    gain_total = small_total[: 4 * shard].reshape(4, shard)
    table_total = small_total[4 * shard : 4 * shard + table_size].reshape(-1, heads)

    return (
        result.astype(BF)[None],
        grad_rows[None],
        grad_states[None],
        gain_total[0],
        total_one[:, :width],
        total_one[:, width : 2 * width],
        total_one[:, 2 * width : 3 * width],
        total_two[:, :width],
        table_total,
        gain_total[1],
        total_two[:, width : 2 * width],
        total_two[:, 2 * width : 3 * width],
        total_two[:, 3 * width : 4 * width],
        total_two[:, 4 * width :],
        gain_total[2],
        total_gate,
        total_up,
        total_down,
    )


def solution(mesh):
    rows = P("fsdp", "ctx", None)
    gain = P("fsdp")
    weight = P("fsdp", None)
    gradients = (
        gain, weight, weight, weight, weight, weight, gain, weight, weight, weight, weight, gain, weight, weight, weight
    )
    return jax.shard_map(
        per_device,
        mesh=mesh,
        in_specs=(rows, rows, rows, P(), P()) + gradients,
        out_specs=(rows, rows, rows) + gradients,
        check_vma=False,
    )
```
